32 devices in a mesh: dp: 8 (over z, x), row: 2 (over core), col: 2 (over y).
Axes of the slice: x: 2, y: 2, z: 4, core: 2. Of those that a mesh axis runs over, the one named last changes fastest.
Arguments:
- tokens: bfloat16 [3136, 512], P(('dp', 'row'), 'col'), may hold values from -6 to 6
- cotangent: bfloat16 [3136, 512], P(('dp', 'row'), 'col'), may hold values from -12 to 12
- qkv_weight: bfloat16 [2, 512, 3, 512], P(None, 'col', None, 'row'), may hold values from -0.25 to 0.25
- qv_bias: bfloat16 [2, 2, 512], P(None, None, 'row'), may hold values from -3 to 3
- out_weight: bfloat16 [2, 512, 512], P(None, 'row', 'col'), may hold values from -1 to 1
- out_bias: bfloat16 [2, 512], P(None, 'col'), may hold values from -3 to 3
- up_weight: bfloat16 [2, 512, 2048], P(None, 'col', 'row'), may hold values from -0.25 to 0.25
- up_bias: bfloat16 [2, 2048], P(None, 'row'), may hold values from -3 to 3
- down_weight: bfloat16 [2, 2048, 512], P(None, 'row', 'col'), may hold values from -0.125 to 0.125
- down_bias: bfloat16 [2, 512], P(None, 'col'), may hold values from -3 to 3
- norm_gain: bfloat16 [2, 2, 512], P(None, None, 'col'), may hold values from 0.5 to 1.5
- norm_shift: bfloat16 [2, 2, 512], P(None, None, 'col'), may hold values from -3 to 3
- bias_table: bfloat16 [2, 169, 16], P(None, None, 'row'), may hold values from -4 to 4
- index_map: int32 [49, 49], replicated, may hold values from 0 to 168
- region_ids: int32 [196], replicated, may hold values from 0 to 3
Outputs:
- output: bfloat16 [3136, 512], P(('dp', 'row'), 'col')
- input_grad: bfloat16 [3136, 512], P(('dp', 'row'), 'col')
- grad_qkv_weight: float32 [2, 512, 3, 512], P(None, 'col', None, 'row')
- grad_qv_bias: float32 [2, 2, 512], P(None, None, 'row')
- grad_out_weight: float32 [2, 512, 512], P(None, 'row', 'col')
- grad_out_bias: float32 [2, 512], P(None, 'col')
- grad_up_weight: float32 [2, 512, 2048], P(None, 'col', 'row')
- grad_up_bias: float32 [2, 2048], P(None, 'row')
- grad_down_weight: float32 [2, 2048, 512], P(None, 'row', 'col')
- grad_down_bias: float32 [2, 512], P(None, 'col')
- grad_norm_gain: float32 [2, 2, 512], P(None, None, 'col')
- grad_norm_shift: float32 [2, 2, 512], P(None, None, 'col')
- grad_bias_table: float32 [2, 169, 16], P(None, None, 'row')
The draws below stay inside these ranges and needn't reach their ends.
All inputs are finite; a program needn't handle non-finite values.
Results may differ from the reference program's by a relative error of at most 0.03.
Values may be sent and summed in bfloat16 or wider, within the bound.
No kernel may reach another device: no remote copies, remote signals or barrier semaphores. Data moves between devices by JAX's collectives and lax.ppermute only.
A program may use at most 128 MiB of HBM per device.

```python
import math
import jax
import jax.numpy as jnp
from jax import lax

D = 512
HEADS = 16
HEAD_DIM = 32
FF = 2048
GRID = 14
WINDOW = 7
SHIFT = 3
REGIONS = 4
TABLE = 169
LAYERS = 2
IMAGES = 16
TOKENS = 3136


def draw_cotangent(key, part):
    position = jnp.arange(TOKENS, dtype=jnp.float32) / max(TOKENS - 1, 1)
    ramp = 1.0 + 2.0 * position
    base = jnp.clip(jax.random.normal(key, (TOKENS, D), jnp.float32), -4.0, 4.0)
    return (base * ramp[:, None]).astype(jnp.bfloat16)


def draw_index_map(key, part):
    span = WINDOW * WINDOW
    values = jax.random.randint(key, (span, span), 0, TABLE, dtype=jnp.int32)
    return values.at[0, 0].set(TABLE - 1).at[0, 1].set(0)


def draw_region_ids(key, part):
    values = jax.random.randint(key, (GRID * GRID,), 0, REGIONS, dtype=jnp.int32)
    return values.at[0].set(REGIONS - 1).at[1].set(0)


def block_levels(stream_key, shape, cuts, least, top_value):
    def one(dim, parts):
        steps = jax.random.uniform(jax.random.fold_in(jax.random.fold_in(stream_key, 6), dim), (parts,), jnp.float32, least / len(cuts), top_value / len(cuts))
        return jnp.repeat(jnp.exp(steps), shape[dim] // parts).reshape((-1,) + (1,) * (len(shape) - dim - 1))

    factor_of = one(*cuts[0])
    for cut in cuts[1:]:
        factor_of = factor_of * one(*cut)
    return factor_of


def bell_draw(stream_key, dims, spread, bound, shards=(), kind=jnp.bfloat16):
    array = spread * jax.random.normal(stream_key, dims, jnp.float32)
    if shards:
        array = array * block_levels(stream_key, dims, shards, -0.22, 0.18)
    return jnp.clip(array, -bound, bound).astype(kind)


def setup_inputs(seed: int = 0) -> dict:
    streams_of = jax.random.split(jax.random.key(seed), 16)
    return {
        "tokens": bell_draw(streams_of[0], (TOKENS, D), 1.0, 6.0, ((0, 16), (1, 2))),
        "cotangent": draw_cotangent(jax.random.fold_in(streams_of[15], 71), 0),
        "qkv_weight": bell_draw(streams_of[2], (LAYERS, D, 3, D), D ** -0.5, 0.25, ((1, 2), (3, 2))),
        "qv_bias": bell_draw(streams_of[3], (LAYERS, 2, D), 0.5, 3.0, ((2, 2),)),
        "out_weight": bell_draw(streams_of[4], (LAYERS, D, D), (D // 16) ** -0.5, 1.0, ((1, 2), (2, 2))),
        "out_bias": bell_draw(streams_of[5], (LAYERS, D), 0.5, 3.0, ((1, 2),)),
        "up_weight": bell_draw(streams_of[6], (LAYERS, D, FF), D ** -0.5, 0.25, ((1, 2), (2, 2))),
        "up_bias": bell_draw(streams_of[7], (LAYERS, FF), 0.5, 3.0, ((1, 2),)),
        "down_weight": bell_draw(streams_of[8], (LAYERS, FF, D), FF ** -0.5, 0.125, ((1, 2), (2, 2))),
        "down_bias": bell_draw(streams_of[9], (LAYERS, D), 0.5, 3.0, ((1, 2),)),
        "norm_gain": jnp.clip(1.0 + 0.1 * jax.random.normal(streams_of[10], (LAYERS, 2, D), jnp.float32), 0.5, 1.5).astype(jnp.bfloat16),
        "norm_shift": bell_draw(streams_of[11], (LAYERS, 2, D), 0.5, 3.0, ((2, 2),)),
        "bias_table": bell_draw(streams_of[12], (LAYERS, TABLE, HEADS), 1.0, 4.0, ((2, 2),)),
        "index_map": draw_index_map(jax.random.fold_in(streams_of[15], 71), 0),
        "region_ids": draw_region_ids(jax.random.fold_in(streams_of[15], 71), 0),
    }


@jax.custom_vjp
def low(v):
    return lax.optimization_barrier(v.astype(jnp.bfloat16)).astype(jnp.float32)

@jax.custom_vjp
def low_back(v):
    return v

def low_keep(v):
    return (low(v), None)

def low_pass(kept, grad):
    return (grad,)

def back_keep(v):
    return (v, None)

def back_low(kept, grad):
    return (low(grad),)
low.defvjp(low_keep, low_pass)
low_back.defvjp(back_keep, back_low)
EPS = 1e-05
NEG = -1000000000.0
HIGH = lax.Precision.HIGHEST

def matmul(left, right):
    return jnp.dot(left, right, precision=HIGH, preferred_element_type=jnp.float32)

def layer_norm(values, norm_scale, norm_offset):
    average = lax.optimization_barrier(jnp.mean(values, -1, keepdims=True))
    variance = lax.optimization_barrier(jnp.mean(jnp.square(values - average), -1, keepdims=True))
    return (values - average) * lax.rsqrt(variance + EPS) * norm_scale + norm_offset

def to_windows(values, images, shifted):
    per_side = GRID // WINDOW
    channels = values.shape[-1]
    laid_out = values.reshape(images, GRID, GRID, channels)
    if shifted:
        laid_out = jnp.roll(laid_out, (-SHIFT, -SHIFT), (1, 2))
    laid_out = laid_out.reshape(images, per_side, WINDOW, per_side, WINDOW, channels).transpose(0, 1, 3, 2, 4, 5)
    return laid_out.reshape(images * per_side * per_side, WINDOW * WINDOW, channels)

def from_windows(values, images, shifted):
    per_side = GRID // WINDOW
    channels = values.shape[-1]
    laid_out = values.reshape(images, per_side, per_side, WINDOW, WINDOW, channels).transpose(0, 1, 3, 2, 4, 5)
    laid_out = laid_out.reshape(images, GRID, GRID, channels)
    if shifted:
        laid_out = jnp.roll(laid_out, (SHIFT, SHIFT), (1, 2))
    return laid_out.reshape(images * GRID * GRID, channels)

def region_windows(region_ids):
    per_side = GRID // WINDOW
    laid_out = region_ids.reshape(per_side, WINDOW, per_side, WINDOW).transpose(0, 2, 1, 3)
    return laid_out.reshape(per_side * per_side, WINDOW * WINDOW)

def attention(queries, keyset, valueset, table, index_map, region_ids, shifted, images):
    span = WINDOW * WINDOW
    query_win = to_windows(queries, images, shifted).reshape(-1, span, HEADS, HEAD_DIM)
    key_win = to_windows(keyset, images, shifted).reshape(-1, span, HEADS, HEAD_DIM)
    value_win = to_windows(valueset, images, shifted).reshape(-1, span, HEADS, HEAD_DIM)
    scores = jnp.einsum('bihd,bjhd->bhij', query_win, key_win, precision=HIGH) / math.sqrt(HEAD_DIM)
    scores = scores + jnp.transpose(table[index_map], (2, 0, 1))[None]
    if shifted:
        window_ids = region_windows(region_ids)
        allowed = window_ids[:, :, None] == window_ids[:, None, :]
        scores = scores.reshape(images, -1, HEADS, span, span)
        scores = jnp.where(allowed[None, :, None], scores, NEG)
        scores = scores.reshape(-1, HEADS, span, span)
    scores = low_back(scores)
    probs = jax.nn.softmax(scores, axis=-1)
    output_win = jnp.einsum('bhij,bjhd->bihd', low(probs), value_win, precision=HIGH)
    merged = from_windows(output_win.reshape(-1, span, D), images, shifted)
    return low(low_back(merged))

def block(params, hidden_in, index_map, region_ids, images):
    qkv_weight, qv_bias, out_weight, out_bias, up_weight, up_bias, down_weight, down_bias, norm_gain, norm_shift, bias_table = params
    residual = hidden_in
    for layer in range(LAYERS):
        shifted = layer % 2 == 1
        normed = low(layer_norm(residual, norm_gain[layer, 0], norm_shift[layer, 0]))
        projected = matmul(normed, qkv_weight[layer].reshape(D, 3 * D)).reshape(-1, 3, D)
        queries = low(low_back(projected[:, 0] + qv_bias[layer, 0]))
        keyset = low(low_back(projected[:, 1]))
        valueset = low(low_back(projected[:, 2] + qv_bias[layer, 1]))
        attended = attention(queries, keyset, valueset, bias_table[layer], index_map, region_ids, shifted, images)
        residual = residual + low_back(matmul(attended, out_weight[layer]) + out_bias[layer])
        normed = low(layer_norm(residual, norm_gain[layer, 1], norm_shift[layer, 1]))
        before = low_back(matmul(normed, up_weight[layer]) + up_bias[layer])
        hidden = low(jax.nn.gelu(before, approximate=False))
        residual = residual + low_back(matmul(hidden, down_weight[layer]) + down_bias[layer])
    return residual

def reference(tokens, cotangent, qkv_weight, qv_bias, out_weight, out_bias, up_weight, up_bias, down_weight, down_bias, norm_gain, norm_shift, bias_table, index_map, region_ids):
    params = tuple((item.astype(jnp.float32) for item in (qkv_weight, qv_bias, out_weight, out_bias, up_weight, up_bias, down_weight, down_bias, norm_gain, norm_shift, bias_table)))
    group = math.gcd(IMAGES, 16)
    steps_total = IMAGES // group
    group_rows = group * GRID * GRID
    inputs = tokens.astype(jnp.float32).reshape(steps_total, group_rows, D)
    grads_in = cotangent.astype(jnp.float32).reshape(steps_total, group_rows, D)

    def forward(weights, values):
        return block(weights, values, index_map, region_ids, group)

    def advance(accum, pair):
        values, upstream = pair
        result, pull = jax.vjp(forward, params, values)
        weight_grads, value_grad = pull(upstream)
        return (jax.tree.map(jnp.add, accum, weight_grads), (result, value_grad))
    start = jax.tree.map(jnp.zeros_like, params)
    accum, (results, value_grads) = lax.scan(advance, start, (inputs, grads_in))
    return (results.reshape(TOKENS, D).astype(jnp.bfloat16), value_grads.reshape(TOKENS, D).astype(jnp.bfloat16), accum[0], accum[1], accum[2], accum[3], accum[4], accum[5], accum[6], accum[7], accum[8], accum[9], accum[10])
```

```python
import math

import jax
import jax.numpy as jnp
import numpy as np
from jax import lax
from jax.experimental import pallas as pl
from jax.experimental.pallas import tpu as pltpu
from jax.sharding import PartitionSpec as P

D = 512
HEADS = 16
HEAD_DIM = 32
FF = 2048
GRID = 14
WINDOW = 7
SHIFT = 3
TABLE = 169
LAYERS = 2
SPAN = WINDOW * WINDOW
IMAGE = GRID * GRID

EPS = 1e-05
NEG = -1000000000.0
HIGH = lax.Precision.HIGHEST
SCALE = 1.0 / math.sqrt(HEAD_DIM)

HALF = IMAGE // 2
PAD = 128
ROWS = 2 * PAD
ROLL = SHIFT * GRID
GROUP = 128 // HEAD_DIM
GROUPS = HEADS // GROUP
STACK = GROUP * PAD
CHUNK = 512
BF = jnp.bfloat16
F32 = jnp.float32


def swap(values, axis):
    return lax.ppermute(values, axis, [(0, 1), (1, 0)])


def mm(left, right):
    return lax.dot_general(left, right, (((1,), (0,)), ((), ())), preferred_element_type=F32)


def mm_nt(left, right):
    return lax.dot_general(left, right, (((1,), (1,)), ((), ())), preferred_element_type=F32)


def mm_tn(left, right):
    return lax.dot_general(left, right, (((0,), (0,)), ((), ())), preferred_element_type=F32)


def token_positions(layer):
    token = np.arange(HALF)
    line, column = token // GRID, token % GRID
    if layer % 2 == 1:
        column = (column - SHIFT) % GRID
    return line * WINDOW + column % WINDOW, column // WINDOW, line * GRID + column


def position_one_hot(layer):
    position, _, _ = token_positions(layer)
    picks = np.zeros((PAD, PAD), np.float32)
    picks[np.arange(HALF), position] = 1.0
    return picks


def mask_of(layer, region_ids):
    _, window, place = token_positions(layer)
    same = np.zeros((PAD, PAD), bool)
    same[:HALF, :HALF] = window[:, None] == window[None, :]
    same[HALF:, :HALF] = True
    allowed = jnp.broadcast_to(jnp.asarray(same)[None], (2, PAD, PAD))
    if layer % 2 == 1:
        ids = jnp.roll(region_ids.reshape(2, WINDOW, GRID), SHIFT, 2).reshape(2, HALF)
        ids = jnp.pad(ids, ((0, 0), (0, PAD - HALF)), constant_values=-1)
        pad_row = jnp.asarray(np.arange(PAD) >= HALF)[None, :, None]
        allowed = allowed & ((ids[:, :, None] == ids[:, None, :]) | pad_row)
    return jnp.where(allowed, 0.0, NEG).astype(F32)


def head_mask():
    lane = lax.broadcasted_iota(jnp.int32, (STACK, PAD), 1) // HEAD_DIM
    row = lax.broadcasted_iota(jnp.int32, (STACK, PAD), 0) // PAD
    return lane == row


def stack_heads(values, mask):
    tiled = jnp.concatenate([values] * GROUP, axis=0)
    return jnp.where(mask, tiled, jnp.zeros_like(tiled))


def unstack_heads(values, mask):
    kept = jnp.where(mask, values, 0.0)
    total = kept[0:PAD]
    for head in range(1, GROUP):
        total = total + kept[head * PAD : (head + 1) * PAD]
    return total


def norm_parts(values):
    average = jnp.mean(values, -1, keepdims=True)
    centred = values - average
    variance = jnp.mean(centred * centred, -1, keepdims=True)
    inverse = lax.rsqrt(variance + EPS)
    return centred * inverse, inverse


def norm_back(grad_normed, values, gain):
    xhat, inverse = norm_parts(values)
    scaled = grad_normed * gain
    mean_one = jnp.mean(scaled, -1, keepdims=True)
    mean_two = jnp.mean(scaled * xhat, -1, keepdims=True)
    grad_input = inverse * (scaled - mean_one - xhat * mean_two)
    return grad_input, jnp.sum(grad_normed * xhat, 0, keepdims=True), jnp.sum(grad_normed, 0, keepdims=True)


def split_halves(values):
    return values[:, : D // 2], values[:, D // 2 :]


def gelu_slope(values):
    return 0.5 * (1.0 + lax.erf(values * (1.0 / math.sqrt(2.0)))) + values * jnp.exp(
        -0.5 * values * values
    ) * (1.0 / math.sqrt(2.0 * math.pi))


GAIN_ONE, GAIN_TWO, SHIFT_ONE, SHIFT_TWO, OUT_BIAS, DOWN_BIAS, Q_BIAS, V_BIAS, UP_BIAS = 0, 1, 2, 3, 4, 5, 6, 7, 8


def prep_kernel(table_ref, index_ref, picks_ref, bias_ref, pairs_ref):
    rows = table_ref.shape[1]
    for position in range(SPAN):
        wanted = index_ref[position : position + 1, :]
        hot = (lax.broadcasted_iota(jnp.int32, (rows, PAD), 0) == wanted).astype(F32).astype(BF)
        pairs_ref[position] = mm(table_ref[...], hot)
    for layer in range(LAYERS):
        picks = picks_ref[layer]
        for head in range(HEADS):
            bias = pairs_ref[:, layer * HEADS + head, :]
            spread = mm(picks[:, :64], bias.astype(BF)).astype(BF)
            bias_ref[layer, head] = mm_nt(spread, picks)


def attn_fwd_kernel(
    x_ref, small_ref, q00, q01, q10, q11, o00, o01, o10, o11, bias_ref, mask_ref,
    mid_ref, normed_ref, qkv_ref, probs_ref, att_ref,
):
    x = x_ref[...]
    xhat, _ = norm_parts(x)
    normed = (
        xhat * small_ref[GAIN_ONE : GAIN_ONE + 1] + small_ref[SHIFT_ONE : SHIFT_ONE + 1]
    ).astype(BF)
    normed_ref[...] = normed
    near, far = split_halves(normed)
    half = D // 2
    for part, (own, other) in enumerate(((q00, q01), (q10, q11))):
        projected = mm(near, own[...]) + mm(far, other[...])
        lanes = slice(part * half, (part + 1) * half)
        qkv_ref[part, :, 0:half] = (projected[:, 0:half] + small_ref[Q_BIAS : Q_BIAS + 1, lanes]).astype(BF)
        qkv_ref[part, :, half : 2 * half] = projected[:, half : 2 * half].astype(BF)
        qkv_ref[part, :, 2 * half :] = (
            projected[:, 2 * half :] + small_ref[V_BIAS : V_BIAS + 1, lanes]
        ).astype(BF)
    mask = head_mask()
    for group in range(GROUPS):
        part, lane = group // 2, (group % 2) * 128
        bias = bias_ref[group * GROUP : (group + 1) * GROUP]
        for side in range(2):
            rows = slice(side * PAD, (side + 1) * PAD)
            query = qkv_ref[part, rows, lane : lane + 128]
            key = qkv_ref[part, rows, half + lane : half + lane + 128]
            value = qkv_ref[part, rows, 2 * half + lane : 2 * half + lane + 128]
            scores = mm_nt(stack_heads(query, mask), key).reshape(GROUP, PAD, PAD) * SCALE
            scores = scores + (bias + mask_ref[side][None])
            peak = jnp.max(scores, -1, keepdims=True)
            expos = jnp.exp(scores - peak)
            totals = jnp.sum(expos, -1, keepdims=True)
            probs = (expos / totals).astype(BF).reshape(STACK, PAD)
            probs_ref[side, group] = probs
            attended = unstack_heads(mm(probs, value), mask)
            att_ref[rows, group * 128 : (group + 1) * 128] = attended.astype(BF)
    first, second = split_halves(att_ref[...])
    near = mm(first, o00[...]) + mm(second, o10[...])
    far = mm(first, o01[...]) + mm(second, o11[...])
    mid_ref[...] = x + jnp.concatenate([near, far], axis=1) + small_ref[OUT_BIAS : OUT_BIAS + 1]


def roll_rows(values_ref, result_ref):
    rest = HALF - ROLL
    result_ref[...] = jnp.zeros_like(result_ref)
    for side in range(2):
        here, there = side * PAD, (1 - side) * PAD
        result_ref[here : here + rest, :] = values_ref[here + ROLL : here + HALF, :]
        result_ref[here + rest : here + HALF, :] = values_ref[there : there + ROLL, :]


def unroll_rows(values_ref, result_ref):
    rest = HALF - ROLL
    result_ref[...] = jnp.zeros_like(result_ref)
    for side in range(2):
        here, there = side * PAD, (1 - side) * PAD
        result_ref[here + ROLL : here + HALF, :] = values_ref[here : here + rest, :]
        result_ref[here : here + ROLL, :] = values_ref[there + rest : there + HALF, :]


def clear_padding(values):
    row = lax.broadcasted_iota(jnp.int32, values.shape, 0) % PAD
    return jnp.where(row < HALF, values, 0.0)


def ffn_fwd_kernel(
    layer, mid_ref, small_ref, u00, u01, u10, u11, d00, d01, d10, d11,
    x_ref, normed_ref, pre_ref, hidden_ref, scratch,
):
    middle = mid_ref[...]
    xhat, _ = norm_parts(middle)
    normed = (
        xhat * small_ref[GAIN_TWO : GAIN_TWO + 1] + small_ref[SHIFT_TWO : SHIFT_TWO + 1]
    ).astype(BF)
    normed_ref[...] = normed
    near, far = split_halves(normed)
    sums = [jnp.zeros((ROWS, D // 2), F32), jnp.zeros((ROWS, D // 2), F32)]
    per_part = FF // 2 // CHUNK
    for chunk in range(FF // CHUNK):
        part, at = chunk // per_part, (chunk % per_part) * CHUNK
        up_own, up_other, down_own, down_other = ((u00, u01, d00, d01), (u10, u11, d10, d11))[part]
        pre = mm(near, up_own[:, at : at + CHUNK]) + mm(far, up_other[:, at : at + CHUNK])
        pre = pre + small_ref[UP_BIAS + chunk : UP_BIAS + chunk + 1]
        pre_ref[:, chunk * CHUNK : (chunk + 1) * CHUNK] = pre
        hidden = (pre * (0.5 * (1.0 + lax.erf(pre * (1.0 / math.sqrt(2.0)))))).astype(BF)
        hidden_ref[:, chunk * CHUNK : (chunk + 1) * CHUNK] = hidden
        sums[0] = sums[0] + mm(hidden, down_own[at : at + CHUNK, :])
        sums[1] = sums[1] + mm(hidden, down_other[at : at + CHUNK, :])
    result = middle + jnp.concatenate(sums, axis=1) + small_ref[DOWN_BIAS : DOWN_BIAS + 1]
    scratch[...] = result
    if layer % 2 == 0:
        roll_rows(scratch, x_ref)
    else:
        unroll_rows(scratch, x_ref)


def ffn_bwd_kernel(
    grad_ref, mid_ref, small_ref, normed_ref, pre_ref, hidden_ref, u00, u01, u10, u11, d00, d01, d10, d11,
    grad_mid_ref, keep_ref, send_ref, small_keep_ref, small_send_ref,
):
    half = D // 2
    grad = grad_ref[...]
    grad_down = grad.astype(BF)
    near, far = split_halves(grad_down)
    normed_near = normed_ref[:, :half]
    per_part = FF // 2 // CHUNK
    outs = (keep_ref, send_ref)
    small_outs = (small_keep_ref, small_send_ref)
    sums = [jnp.zeros((ROWS, half), F32), jnp.zeros((ROWS, half), F32)]
    for chunk in range(FF // CHUNK):
        part, at = chunk // per_part, (chunk % per_part) * CHUNK
        up_own, up_other, down_own, down_other = ((u00, u01, d00, d01), (u10, u11, d10, d11))[part]
        lanes = slice(chunk * CHUNK, (chunk + 1) * CHUNK)
        grad_hidden = mm_nt(near, down_own[at : at + CHUNK, :]) + mm_nt(far, down_other[at : at + CHUNK, :])
        grad_pre_wide = (grad_hidden * gelu_slope(pre_ref[:, lanes])).astype(BF)
        outs[part][at : at + CHUNK, :] = mm_tn(hidden_ref[:, lanes], near).astype(BF)
        grad_up = mm_tn(normed_near, grad_pre_wide).astype(BF)
        bias_sum = jnp.sum(grad_pre_wide.astype(F32), 0, keepdims=True)
        for piece in range(CHUNK // half):
            place = FF // 2 + (at // half + piece) * half
            outs[part][place : place + half, :] = grad_up[:, piece * half : (piece + 1) * half]
            line = 3 + at // half + piece
            small_outs[part][line : line + 1, :] = bias_sum[:, piece * half : (piece + 1) * half]
        sums[0] = sums[0] + mm_nt(grad_pre_wide, up_own[:, at : at + CHUNK])
        sums[1] = sums[1] + mm_nt(grad_pre_wide, up_other[:, at : at + CHUNK])
    grad_normed = jnp.concatenate(sums, axis=1)
    grad_input, grad_gain, grad_shift = norm_back(
        grad_normed, mid_ref[...], small_ref[GAIN_TWO : GAIN_TWO + 1]
    )
    grad_mid_ref[...] = clear_padding(grad + grad_input)
    down_bias = jnp.sum(near.astype(F32), 0, keepdims=True)
    for small in small_outs:
        small[0:1, :] = down_bias
        small[1:2, :] = grad_gain[:, :half]
        small[2:3, :] = grad_shift[:, :half]
        small[7:8, :] = jnp.zeros((1, half), F32)


def attn_bwd_kernel(
    layer, grad_mid_ref, x_ref, small_ref, normed_ref, qkv_ref, probs_ref, att_ref,
    q00, q01, q10, q11, o00, o01, o10, o11, picks_ref, picks_t_ref,
    grad_ref, keep_ref, send_ref, small_keep_ref, small_send_ref, table_ref, grad_qkv, scratch,
):
    half = D // 2
    grad_mid = grad_mid_ref[...]
    grad_att = grad_mid.astype(BF)
    near, far = split_halves(grad_att)
    outs = (keep_ref, send_ref)
    small_outs = (small_keep_ref, small_send_ref)
    mask = head_mask()
    picks = picks_ref[...]
    picks_t = picks_t_ref[...]
    normed_near = normed_ref[:, :half]
    sums = [jnp.zeros((ROWS, half), F32), jnp.zeros((ROWS, half), F32)]
    for part in range(2):
        out_own, out_other = ((o00, o01), (o10, o11))[part]
        qkv_own, qkv_other = ((q00, q01), (q10, q11))[part]
        grad_attended = (mm_nt(near, out_own[...]) + mm_nt(far, out_other[...])).astype(BF)
        outs[part][3 * half : 4 * half, :] = mm_tn(att_ref[:, part * half : (part + 1) * half], near).astype(BF)
        for inner in range(2):
            group, lane = part * 2 + inner, inner * 128
            tables = [jnp.zeros((64, PAD), F32) for _ in range(GROUP)]
            for side in range(2):
                rows = slice(side * PAD, (side + 1) * PAD)
                query = stack_heads(qkv_ref[part, rows, lane : lane + 128], mask)
                key = qkv_ref[part, rows, half + lane : half + lane + 128]
                value = qkv_ref[part, rows, 2 * half + lane : 2 * half + lane + 128]
                grad_out = stack_heads(grad_attended[rows, lane : lane + 128], mask)
                probs_low = probs_ref[side, group]
                probs = probs_low.astype(F32)
                grad_probs = mm_nt(grad_out, value)
                weighted = jnp.sum(probs * grad_probs, -1, keepdims=True)
                grad_scores = (probs * (grad_probs - weighted)).astype(BF)
                grad_value = mm_tn(probs_low, grad_out)
                grad_query = unstack_heads(mm(grad_scores, key), mask) * SCALE
                grad_key = mm_tn(grad_scores, query) * SCALE
                grad_qkv[part, rows, lane : lane + 128] = grad_query.astype(BF)
                grad_qkv[part, rows, half + lane : half + lane + 128] = grad_key.astype(BF)
                grad_qkv[part, rows, 2 * half + lane : 2 * half + lane + 128] = grad_value.astype(BF)
                picked = mm(grad_scores, picks).astype(BF)
                for head in range(GROUP):
                    tables[head] = tables[head] + mm(picks_t[:64], picked[head * PAD : (head + 1) * PAD])
            for head in range(GROUP):
                table_ref[group * GROUP + head] = tables[head][:56]
        grads = grad_qkv[part]
        wide = mm_tn(normed_near, grads).astype(BF)
        for piece in range(3):
            outs[part][piece * half : (piece + 1) * half, :] = wide[:, piece * half : (piece + 1) * half]
        small_outs[part][3:4, :] = jnp.sum(grads[:, :half].astype(F32), 0, keepdims=True)
        small_outs[part][4:5, :] = jnp.sum(grads[:, 2 * half :].astype(F32), 0, keepdims=True)
        sums[0] = sums[0] + mm_nt(grads, qkv_own[...])
        sums[1] = sums[1] + mm_nt(grads, qkv_other[...])
    grad_input, grad_gain, grad_shift = norm_back(
        jnp.concatenate(sums, axis=1), x_ref[...], small_ref[GAIN_ONE : GAIN_ONE + 1]
    )
    total = clear_padding(grad_mid + grad_input)
    if layer % 2 == 1:
        scratch[...] = total
        unroll_rows(scratch, grad_ref)
    else:
        grad_ref[...] = total
    out_bias = jnp.sum(near.astype(F32), 0, keepdims=True)
    for small in small_outs:
        small[0:1, :] = out_bias
        small[1:2, :] = grad_gain[:, :half]
        small[2:3, :] = grad_shift[:, :half]
        small[5:8, :] = jnp.zeros((3, half), F32)


def call(kernel, outs, scratch, args, flops):
    vmem = pl.BlockSpec(memory_space=pltpu.VMEM)
    moved = sum(a.size * a.dtype.itemsize for a in args) + sum(
        math.prod(shape) * jnp.dtype(kind).itemsize for shape, kind in outs
    )
    return pl.pallas_call(
        kernel,
        out_shape=[jax.ShapeDtypeStruct(shape, kind) for shape, kind in outs],
        in_specs=[vmem] * len(args),
        out_specs=[vmem] * len(outs),
        scratch_shapes=scratch,
        compiler_params=pltpu.CompilerParams(vmem_limit_bytes=40 * 1024 * 1024),
        cost_estimate=pl.CostEstimate(flops=flops, bytes_accessed=moved, transcendentals=0),
    )(*args)


def part_of(kernel, layer):
    def run(*refs):
        kernel(layer, *refs)

    return run


def dp_sum(values):
    return lax.psum(values, "dp")


def on_device(
    tokens, cotangent, qkv_weight, qv_bias, out_weight, out_bias, up_weight, up_bias,
    down_weight, down_bias, norm_gain, norm_shift, bias_table, index_map, region_ids,
):
    half = D // 2
    col_own = jnp.concatenate(
        [tokens, cotangent, norm_gain.reshape(4, half), norm_shift.reshape(4, half), out_bias, down_bias], 0
    )
    tables_own = jnp.pad(
        bias_table.transpose(0, 2, 1).reshape(LAYERS * HEADS // 2, TABLE), ((0, 0), (0, 256 - TABLE))
    )
    row_own = jnp.concatenate([qv_bias.reshape(4, half), up_bias.reshape(8, half), tables_own], 0)
    col_other = swap(col_own, "col")
    row_other = swap(row_own, "row")
    col_all = jnp.concatenate([col_own, col_other], 1)

    blocks = []
    for layer in range(LAYERS):
        own = [
            qkv_weight[layer].reshape(half, 3 * half), out_weight[layer], up_weight[layer], down_weight[layer],
        ]
        other_col = [swap(piece, "col") for piece in own]
        other_row = [swap(piece, "row") for piece in own]
        other_both = [swap(piece, "row") for piece in other_col]
        blocks.append(
            [(a, b, c, d) for a, b, c, d in zip(own, other_col, other_row, other_both)]
        )

    small_cols = col_all[2 * IMAGE :].astype(F32)
    row_both = jnp.concatenate([row_own, row_other], 1).astype(F32)
    ups = jnp.concatenate(
        [row_own[4:12].reshape(LAYERS, 2, D), row_other[4:12].reshape(LAYERS, 2, D)], 1
    ).astype(F32)
    smalls = []
    for layer in range(LAYERS):
        smalls.append(
            jnp.concatenate(
                [
                    small_cols[2 * layer : 2 * layer + 2],
                    small_cols[4 + 2 * layer : 6 + 2 * layer],
                    small_cols[8 + layer : 9 + layer],
                    small_cols[10 + layer : 11 + layer],
                    row_both[2 * layer : 2 * layer + 2],
                    ups[layer],
                    jnp.zeros((4, D), F32),
                ],
                0,
            )
        )
    heads = HEADS // 2
    tables = jnp.concatenate(
        [row_own[12 : 12 + heads], row_other[12 : 12 + heads], row_own[12 + heads :], row_other[12 + heads :]], 0
    )
    index_pad = jnp.pad(index_map, ((0, 64 - SPAN), (0, PAD - SPAN)), constant_values=-1)
    picks = np.stack([position_one_hot(layer) for layer in range(LAYERS)])
    picks_t = jnp.asarray(picks.transpose(0, 2, 1), BF)
    picks = jnp.asarray(picks, BF)
    masks = [mask_of(layer, region_ids) for layer in range(LAYERS)]

    (bias,) = call(
        prep_kernel,
        [((LAYERS, HEADS, PAD, PAD), F32)],
        [pltpu.VMEM((64, LAYERS * HEADS, PAD), F32)],
        [tables, index_pad, picks],
        10**7,
    )

    def to_rows(values):
        return jnp.pad(values.reshape(2, HALF, -1), ((0, 0), (0, PAD - HALF), (0, 0))).reshape(ROWS, -1)

    x = to_rows(col_all[:IMAGE].astype(F32))
    saved = []
    for layer in range(LAYERS):
        wq, wo, wu, wd = blocks[layer]
        middle, normed_one, qkv, probs, att = call(
            attn_fwd_kernel,
            [
                ((ROWS, D), F32), ((ROWS, D), BF), ((2, ROWS, 3 * half), BF),
                ((2, GROUPS, STACK, PAD), BF), ((ROWS, D), BF),
            ],
            [],
            [x, smalls[layer], *wq, *wo, bias[layer], masks[layer]],
            10**9,
        )
        result, normed_two, pre, hidden = call(
            part_of(ffn_fwd_kernel, layer),
            [((ROWS, D), F32), ((ROWS, D), BF), ((ROWS, FF), F32), ((ROWS, FF), BF)],
            [pltpu.VMEM((ROWS, D), F32)],
            [middle, smalls[layer], *wu, *wd],
            10**9,
        )
        saved.append((x, middle, normed_one, qkv, probs, att, normed_two, pre, hidden))
        x = result

    def from_rows(values):
        return values.reshape(2, PAD, -1)[:, :HALF, :half].reshape(IMAGE, half).astype(BF)

    output = from_rows(x)
    grad = to_rows(jnp.roll(col_all[IMAGE : 2 * IMAGE], -ROLL, 0).astype(F32))

    one_hot = (index_map[:, :, None] == jnp.arange(256, dtype=jnp.int32)).astype(F32).reshape(SPAN * SPAN, 256)
    sums = [None] * LAYERS
    for layer in reversed(range(LAYERS)):
        x_in, middle, normed_one, qkv, probs, att, normed_two, pre, hidden = saved[layer]
        wq, wo, wu, wd = blocks[layer]
        small_shape = ((8, half), F32)
        grad_mid, keep, send, small_keep, small_send = call(
            ffn_bwd_kernel,
            [((ROWS, D), F32), ((FF, half), BF), ((FF, half), BF), small_shape, small_shape],
            [],
            [grad, middle, smalls[layer], normed_two, pre, hidden, *wu, *wd],
            2 * 10**9,
        )
        ffn_total = dp_sum(keep + swap(send, "row"))
        grad, keep, send, att_keep, att_send, pairs = call(
            part_of(attn_bwd_kernel, layer),
            [
                ((ROWS, D), F32), ((2 * D, half), BF), ((2 * D, half), BF), small_shape, small_shape,
                ((HEADS, 56, PAD), F32),
            ],
            [pltpu.VMEM((2, ROWS, 3 * half), BF), pltpu.VMEM((ROWS, D), F32)],
            [grad_mid, x_in, smalls[layer], normed_one, qkv, probs, att, *wq, *wo, picks[layer], picks_t[layer]],
            2 * 10**9,
        )
        table = jnp.dot(pairs[:, :SPAN, :SPAN].reshape(HEADS, SPAN * SPAN), one_hot, precision=HIGH)
        tail_keep = jnp.concatenate([small_keep, att_keep, table[:heads], jnp.zeros((8, half), F32)], 0)
        tail_send = jnp.concatenate([small_send, att_send, table[heads:], jnp.zeros((8, half), F32)], 0)
        keep = jnp.concatenate([keep, tail_keep.astype(BF)], 0)
        send = jnp.concatenate([send, tail_send.astype(BF)], 0)
        sums[layer] = (ffn_total, dp_sum(keep + swap(send, "row")))
    input_grad = from_rows(grad)

    def both(pick):
        return jnp.stack([pick(*sums[layer]).astype(F32) for layer in range(LAYERS)])

    base = 2 * D
    grad_down_weight = both(lambda f, a: f[: FF // 2])
    grad_up_weight = both(lambda f, a: f[FF // 2 :].reshape(4, half, half).transpose(1, 0, 2).reshape(half, FF // 2))
    grad_qkv_weight = both(lambda f, a: a[: 3 * half].reshape(3, half, half).transpose(1, 0, 2))
    grad_out_weight = both(lambda f, a: a[3 * half : base])
    grad_qv_bias = both(lambda f, a: a[base + 11 : base + 13])
    grad_out_bias = both(lambda f, a: a[base + 8])
    grad_up_bias = both(lambda f, a: a[base + 3 : base + 7].reshape(FF // 2))
    grad_down_bias = both(lambda f, a: a[base])
    grad_norm_gain = both(lambda f, a: jnp.stack([a[base + 9], a[base + 1]]))
    grad_norm_shift = both(lambda f, a: jnp.stack([a[base + 10], a[base + 2]]))
    grad_bias_table = both(lambda f, a: a[base + 16 : base + 24, :TABLE].T)
    return (
        output, input_grad, grad_qkv_weight, grad_qv_bias, grad_out_weight, grad_out_bias, grad_up_weight,
        grad_up_bias, grad_down_weight, grad_down_bias, grad_norm_gain, grad_norm_shift, grad_bias_table,
    )


def solution(mesh):
    in_specs = (
        P(("dp", "row"), "col"),
        P(("dp", "row"), "col"),
        P(None, "col", None, "row"),
        P(None, None, "row"),
        P(None, "row", "col"),
        P(None, "col"),
        P(None, "col", "row"),
        P(None, "row"),
        P(None, "row", "col"),
        P(None, "col"),
        P(None, None, "col"),
        P(None, None, "col"),
        P(None, None, "row"),
        P(),
        P(),
    )
    out_specs = (
        P(("dp", "row"), "col"),
        P(("dp", "row"), "col"),
        P(None, "col", None, "row"),
        P(None, None, "row"),
        P(None, "row", "col"),
        P(None, "col"),
        P(None, "col", "row"),
        P(None, "row"),
        P(None, "row", "col"),
        P(None, "col"),
        P(None, None, "col"),
        P(None, None, "col"),
        P(None, None, "row"),
    )
    return jax.shard_map(
        on_device, mesh=mesh, in_specs=in_specs, out_specs=out_specs, check_vma=False
    )
```

```python
import math

import jax
import jax.numpy as jnp
import numpy as np
from jax import lax
from jax.experimental import pallas as pl
from jax.experimental.pallas import tpu as pltpu
from jax.sharding import PartitionSpec as P

D = 512
HEADS = 16
HEAD_DIM = 32
FF = 2048
GRID = 14
WINDOW = 7
SHIFT = 3
TABLE = 169
LAYERS = 2
SPAN = WINDOW * WINDOW
IMAGE = GRID * GRID

EPS = 1e-05
NEG = -1000000000.0
HIGH = lax.Precision.HIGHEST
SCALE = 1.0 / math.sqrt(HEAD_DIM)

HALF = IMAGE // 2
PAD = 128
ROWS = 2 * PAD
ROLL = SHIFT * GRID
GROUP = 128 // HEAD_DIM
GROUPS = HEADS // GROUP
STACK = GROUP * PAD
CHUNK = 512
BF = jnp.bfloat16
F32 = jnp.float32


def swap(values, axis):
    return lax.ppermute(values, axis, [(0, 1), (1, 0)])


def mm(left, right):
    return lax.dot_general(left, right, (((1,), (0,)), ((), ())), preferred_element_type=F32)


def mm_nt(left, right):
    return lax.dot_general(left, right, (((1,), (1,)), ((), ())), preferred_element_type=F32)


def mm_tn(left, right):
    return lax.dot_general(left, right, (((0,), (0,)), ((), ())), preferred_element_type=F32)


def token_positions(layer):
    token = np.arange(HALF)
    line, column = token // GRID, token % GRID
    if layer % 2 == 1:
        column = (column - SHIFT) % GRID
    return line * WINDOW + column % WINDOW, column // WINDOW, line * GRID + column


def position_one_hot(layer):
    position, _, _ = token_positions(layer)
    picks = np.zeros((PAD, PAD), np.float32)
    picks[np.arange(HALF), position] = 1.0
    return picks


def mask_of(layer, region_ids):
    _, window, place = token_positions(layer)
    same = np.zeros((PAD, PAD), bool)
    same[:HALF, :HALF] = window[:, None] == window[None, :]
    same[HALF:, :HALF] = True
    allowed = jnp.broadcast_to(jnp.asarray(same)[None], (2, PAD, PAD))
    if layer % 2 == 1:
        ids = jnp.roll(region_ids.reshape(2, WINDOW, GRID), SHIFT, 2).reshape(2, HALF)
        ids = jnp.pad(ids, ((0, 0), (0, PAD - HALF)), constant_values=-1)
        pad_row = jnp.asarray(np.arange(PAD) >= HALF)[None, :, None]
        allowed = allowed & ((ids[:, :, None] == ids[:, None, :]) | pad_row)
    return jnp.where(allowed, 0.0, NEG).astype(F32)


def head_mask():
    lane = lax.broadcasted_iota(jnp.int32, (STACK, PAD), 1) // HEAD_DIM
    row = lax.broadcasted_iota(jnp.int32, (STACK, PAD), 0) // PAD
    return lane == row


def stack_heads(values, mask):
    tiled = jnp.concatenate([values] * GROUP, axis=0)
    return jnp.where(mask, tiled, jnp.zeros_like(tiled))


def unstack_heads(values, mask):
    kept = jnp.where(mask, values, 0.0)
    total = kept[0:PAD]
    for head in range(1, GROUP):
        total = total + kept[head * PAD : (head + 1) * PAD]
    return total


def norm_parts(values):
    average = jnp.mean(values, -1, keepdims=True)
    centred = values - average
    variance = jnp.mean(centred * centred, -1, keepdims=True)
    inverse = lax.rsqrt(variance + EPS)
    return centred * inverse, inverse


def norm_back(grad_normed, values, gain):
    xhat, inverse = norm_parts(values)
    scaled = grad_normed * gain
    mean_one = jnp.mean(scaled, -1, keepdims=True)
    mean_two = jnp.mean(scaled * xhat, -1, keepdims=True)
    grad_input = inverse * (scaled - mean_one - xhat * mean_two)
    return grad_input, jnp.sum(grad_normed * xhat, 0, keepdims=True), jnp.sum(grad_normed, 0, keepdims=True)


def split_halves(values):
    return values[:, : D // 2], values[:, D // 2 :]


def gelu_and_slope(values):
    below = 0.5 * (1.0 + lax.erf(values * (1.0 / math.sqrt(2.0))))
    density = jnp.exp(-0.5 * values * values) * (1.0 / math.sqrt(2.0 * math.pi))
    return values * below, below + values * density


TABLE_ROWS = 176

GAIN_ONE, GAIN_TWO, SHIFT_ONE, SHIFT_TWO, OUT_BIAS, DOWN_BIAS, Q_BIAS, V_BIAS, UP_BIAS = 0, 1, 2, 3, 4, 5, 6, 7, 8


def prep_kernel(
    parity_ref, misc_ref, misc_far, row_ref, row_far, index_ref, picks_ref,
    x_ref, grad_ref, small_zero, small_one, bias_zero, bias_one, pairs_ref, index_pad, flat,
):
    half, quarter = D // 2, D // 4
    even = parity_ref[0] == 0

    def ordered(values):
        low, high = values[:, :quarter], values[:, quarter:]
        return jnp.where(even, low, high), jnp.where(even, high, low)

    def lay_out(at):
        first, second = ordered(misc_far[at : at + 208, :].astype(F32))
        flat[:, 0:half] = misc_ref[at : at + 208, :].astype(F32)
        flat[:, half : half + quarter] = first
        flat[:, half + quarter :] = second

    x_ref[...] = jnp.zeros_like(x_ref)
    grad_ref[...] = jnp.zeros_like(grad_ref)
    lay_out(TOKENS_AT)
    x_ref[0:HALF, :] = flat[0:HALF, :]
    x_ref[PAD : PAD + HALF, :] = flat[HALF:IMAGE, :]
    lay_out(COT_AT)
    rest = HALF - ROLL
    grad_ref[0:HALF, :] = flat[ROLL : ROLL + HALF, :]
    grad_ref[PAD : PAD + rest, :] = flat[ROLL + HALF : IMAGE, :]
    grad_ref[PAD + rest : PAD + HALF, :] = flat[0:ROLL, :]

    near = misc_ref[SMALL_AT:MISC_ROWS, :].astype(F32)
    far_first, far_second = ordered(misc_far[SMALL_AT:MISC_ROWS, :].astype(F32))
    rows_near, rows_far = row_ref[...].astype(F32), row_far[...].astype(F32)
    for layer, small in enumerate((small_zero, small_one)):
        small[...] = jnp.zeros_like(small)

        def features(row, source):
            small[row : row + 1, 0:half] = near[source : source + 1]
            small[row : row + 1, half : half + quarter] = far_first[source : source + 1]
            small[row : row + 1, half + quarter :] = far_second[source : source + 1]

        for which in range(2):
            features(GAIN_ONE + which, 2 * layer + which)
            features(SHIFT_ONE + which, 4 + 2 * layer + which)
            for part, source in enumerate((rows_near, rows_far)):
                lanes = slice(part * half, (part + 1) * half)
                at = 2 * layer + which
                small[Q_BIAS + which : Q_BIAS + which + 1, lanes] = source[at : at + 1]
                line = UP_BIAS + 2 * part + which
                for piece in range(2):
                    at = 4 + 2 * (2 * which + piece) + layer
                    small[line : line + 1, piece * half : (piece + 1) * half] = source[at : at + 1]
        features(OUT_BIAS, 8 + layer)
        features(DOWN_BIAS, 10 + layer)

    heads = HEADS // 2
    tables = []
    for layer in range(LAYERS):
        for source in (rows_near, rows_far):
            tables.append(source[16 + layer * heads : 16 + (layer + 1) * heads, :TABLE_ROWS])
    table = jnp.concatenate(tables, 0).astype(BF)
    index_pad[...] = jnp.full(index_pad.shape, -1, jnp.int32)
    index_pad[0:SPAN, 0:SPAN] = index_ref[...]
    pairs_ref[SPAN:64] = jnp.zeros((64 - SPAN, LAYERS * HEADS, PAD), F32)
    for position in range(SPAN):
        wanted = index_pad[position : position + 1, :]
        hot = (lax.broadcasted_iota(jnp.int32, (TABLE_ROWS, PAD), 0) == wanted).astype(F32).astype(BF)
        pairs_ref[position] = mm(table, hot)
    for layer, bias_ref in enumerate((bias_zero, bias_one)):
        picks = picks_ref[layer]
        for head in range(HEADS):
            bias = pairs_ref[:, layer * HEADS + head, :]
            spread = mm(picks[:, :64], bias.astype(BF)).astype(BF)
            bias_ref[head] = mm_nt(spread, picks)


class Fetch:
    def __init__(self, copies, ref):
        self.copies, self.ref, self.waiting = copies, ref, True

    def start(self):
        for copy in self.copies:
            copy.start()

    def ready(self):
        if self.waiting:
            self.waiting = False
            for copy in self.copies:
                copy.wait()
        return self.ref

    def __getitem__(self, index):
        return self.ready()[index]


def whole_fetch(source, room, sems, at):
    return Fetch([pltpu.make_async_copy(source, room, sems.at[at])], room)


def attn_weights(layer, sources, rooms, sems, at):
    half, quarter = D // 2, D // 4
    qkv, out, from_col, from_dp, whole_row, from_col_row, from_dp_row = sources
    qkvs, outs = [], []
    whole_at = layer * TAIL_AT
    for part, packs in enumerate(((from_col, from_dp), (from_col_row, from_dp_row))):
        room_qkv, room_out = rooms[2 * part], rooms[2 * part + 1]
        pairs, pairs_out = [], []
        for kind in range(3):
            lines = slice(whole_at + QKV_AT + kind * half, whole_at + QKV_AT + (kind + 1) * half)
            source = qkv.at[layer, kind] if part == 0 else whole_row.at[lines, :]
            pairs.append((source, room_qkv.at[kind, 0:half, :]))
        source = out.at[layer] if part == 0 else whole_row.at[whole_at + OUT_AT : whole_at + TAIL_AT, :]
        pairs_out.append((source, room_out.at[:, 0:half]))
        for slot, pack in enumerate(packs):
            first = half + slot * quarter
            for kind in range(3):
                pairs.append(
                    (
                        pack.at[kind * quarter : (kind + 1) * quarter, :],
                        room_qkv.at[kind, first : first + quarter, :],
                    )
                )
            for side in range(2):
                lanes = slice(side * quarter, (side + 1) * quarter)
                pairs_out.append((pack.at[3 * quarter : 4 * quarter, lanes], room_out.at[lanes, first : first + quarter]))
        for found, room, list_of in ((pairs, room_qkv, qkvs), (pairs_out, room_out, outs)):
            copies = []
            for source, target in found:
                copies.append(pltpu.make_async_copy(source, target, sems.at[at]))
                at += 1
            list_of.append(Fetch(copies, room))
    return qkvs, outs


ATTN_COPIES = 2 * (9 + 5)
ATTN_ROOMS = [((3, D, D // 2), BF), ((D // 2, D), BF)] * 2


def ffn_weights(layer, sources, rooms, sems, at):
    half, quarter, wide = D // 2, D // 4, FF // 4
    up, down, from_col, from_dp, whole_row, from_col_row, from_dp_row = sources
    ups, downs = [], []
    whole_at = layer * TAIL_AT
    for part, packs in enumerate(((from_col, from_dp), (from_col_row, from_dp_row))):
        room_up, room_down = rooms[2 * part], rooms[2 * part + 1]
        pairs, pairs_down = [], []
        for piece in range(4):
            lanes = slice(piece * half, (piece + 1) * half)
            lines = slice(whole_at + UP_AT + piece * half, whole_at + UP_AT + (piece + 1) * half)
            source = up.at[layer, :, lanes] if part == 0 else whole_row.at[lines, :]
            pairs.append((source, room_up.at[0:half, lanes]))
        source = down.at[layer] if part == 0 else whole_row.at[whole_at + DOWN_AT : whole_at + UP_AT, :]
        pairs_down.append((source, room_down.at[:, 0:half]))
        for slot, pack in enumerate(packs):
            first = half + slot * quarter
            for piece in range(4):
                lanes = slice(piece * half, (piece + 1) * half)
                pairs.append(
                    (
                        pack.at[D + piece * quarter : D + (piece + 1) * quarter, :],
                        room_up.at[first : first + quarter, lanes],
                    )
                )
            for side in range(2):
                lanes = slice(side * quarter, (side + 1) * quarter)
                pairs_down.append(
                    (
                        pack.at[2 * D :, lanes],
                        room_down.at[side * wide : (side + 1) * wide, first : first + quarter],
                    )
                )
        for found, room, list_of in ((pairs, room_up, ups), (pairs_down, room_down, downs)):
            copies = []
            for source, target in found:
                copies.append(pltpu.make_async_copy(source, target, sems.at[at]))
                at += 1
            list_of.append(Fetch(copies, room))
    return ups, downs


FFN_COPIES = 2 * (12 + 5)
FFN_ROOMS = [((D, FF // 2), BF), ((FF // 2, D), BF)] * 2


def misc_kernel(qv_bias, up_bias, table, misc_row):
    half = D // 2
    rows = [qv_bias[0], qv_bias[1]] + [up_bias[:, piece * half : (piece + 1) * half] for piece in range(4)]
    rows = [row.astype(F32) for row in rows] + [jnp.zeros((4, half), F32)]
    misc_row[0:16, :] = jnp.concatenate(rows, 0).astype(BF)
    tables = jnp.concatenate([table[layer].astype(F32) for layer in range(LAYERS)], 0)
    misc_row[16:32, :] = jnp.pad(tables, ((0, 0), (0, half - TABLE))).astype(BF)


def pack_kernel(
    parity_ref, qkv, out, up, down, tokens, cot, gain, shift, out_bias, down_bias, _,
    misc_out, pack_zero, pack_one, whole, *rest,
):
    rooms, results, (in_sems, out_sems) = rest[:8], rest[8:11], rest[11:]
    half, quarter = D // 2, D // 4
    even = parity_ref[0] == 0
    fetched = []
    for layer in range(LAYERS):
        for number, source in enumerate((qkv, out, up, down)):
            at = 4 * layer + number
            fetched.append(whole_fetch(source.at[layer], rooms[at], in_sems, at))
    for item in fetched:
        item.start()
    sent = []

    def send(source, target):
        copy = pltpu.make_async_copy(source, target, out_sems.at[len(sent)])
        copy.start()
        sent.append(copy)

    misc = results[0]
    misc[...] = jnp.zeros_like(misc)
    misc[TOKENS_AT : TOKENS_AT + IMAGE, :] = tokens[...]
    misc[COT_AT : COT_AT + IMAGE, :] = cot[...]
    rows = [gain[0], gain[1], shift[0], shift[1], out_bias[...], down_bias[...]]
    misc[SMALL_AT : SMALL_AT + 12, :] = jnp.concatenate([row.astype(F32) for row in rows], 0).astype(BF)
    send(misc, misc_out)
    for layer in range(LAYERS):
        pack = results[1 + layer]
        at = layer * TAIL_AT
        qkv_l, out_l, up_l, down_l = [item.ready() for item in fetched[4 * layer : 4 * layer + 4]]
        for kind in range(3):
            pack[kind * quarter : (kind + 1) * quarter, :] = jnp.where(
                even, qkv_l[kind, 0:quarter, :], qkv_l[kind, quarter:half, :]
            )
        chosen = jnp.where(even, out_l[:, 0:quarter], out_l[:, quarter:half])
        pack[3 * quarter : 4 * quarter, 0:quarter] = chosen[0:quarter]
        pack[3 * quarter : 4 * quarter, quarter:half] = chosen[quarter:half]
        chosen = jnp.where(even, up_l[0:quarter, :], up_l[quarter:half, :])
        for piece in range(4):
            lines = slice(D + piece * quarter, D + (piece + 1) * quarter)
            pack[lines, :] = chosen[:, piece * half : (piece + 1) * half]
        chosen = jnp.where(even, down_l[:, 0:quarter], down_l[:, quarter:half])
        pack[2 * D :, 0:quarter] = chosen[0 : FF // 4]
        pack[2 * D :, quarter:half] = chosen[FF // 4 :]
        send(pack, (pack_zero, pack_one)[layer])
        send(down_l, whole.at[at + DOWN_AT : at + UP_AT, :])
        for piece in range(4):
            lines = slice(at + UP_AT + piece * half, at + UP_AT + (piece + 1) * half)
            send(up_l.at[:, piece * half : (piece + 1) * half], whole.at[lines, :])
        for kind in range(3):
            send(qkv_l.at[kind], whole.at[at + QKV_AT + kind * half : at + QKV_AT + (kind + 1) * half, :])
        send(out_l, whole.at[at + OUT_AT : at + TAIL_AT, :])
    for copy in sent:
        copy.wait()


def after_kernel(*refs):
    pass


def after(value, token):
    (result,) = call(
        after_kernel, [(value.shape, value.dtype)], [], [value, token], 0, [ANY] * 2, [ANY], limit=1, aliases={0: 0}
    )
    return result


TOKENS_AT, COT_AT, SMALL_AT, MISC_ROWS = 0, 208, 416, 432


def combine_kernel(place_ref, ffn_keep, ffn_got, keep, got, tail_keep, tail_got, *rest):
    pieces_ref, one_ref, two_ref, flat = rest[-4:]
    flat[0:FF, :] = ffn_keep[...].astype(F32) + ffn_got[...].astype(F32)
    flat[FF : FF + 2 * D, :] = keep[...].astype(F32) + got[...].astype(F32)
    flat[TAIL_AT:, :] = jnp.zeros((BLOCK_ROWS - TAIL_AT, D // 2), F32)
    flat[TAIL_AT : TAIL_AT + 24, :] = tail_keep[...] + tail_got[...]
    for number in range(2 * RING):
        pieces_ref[number] = flat[number * PIECE : (number + 1) * PIECE, :].astype(BF)
    place = place_ref[0]
    one_ref[...] = pieces_ref[lax.rem(place + RING - 1, RING)]
    two_ref[...] = pieces_ref[RING + lax.rem(place + 1, RING)]


def attn_fwd_kernel(
    layer, weights, x_ref, small_ref, bias_ref, mask_ref, mid_ref, normed_ref, qkv_ref, probs_ref, att_ref,
):
    qkv_weights, out_weights = weights
    x = x_ref[...]
    xhat, _ = norm_parts(x)
    normed = (
        xhat * small_ref[GAIN_ONE : GAIN_ONE + 1] + small_ref[SHIFT_ONE : SHIFT_ONE + 1]
    ).astype(BF)
    normed_ref[...] = normed
    half = D // 2
    for part in range(2):
        lanes = slice(part * half, (part + 1) * half)
        for kind in range(3):
            projected = mm(normed, qkv_weights[part][kind])
            if kind != 1:
                row = Q_BIAS if kind == 0 else V_BIAS
                projected = projected + small_ref[row : row + 1, lanes]
            qkv_ref[part, :, kind * half : (kind + 1) * half] = projected.astype(BF)
    mask = head_mask()
    for group in range(GROUPS):
        part, lane = group // 2, (group % 2) * 128
        bias = bias_ref[group * GROUP : (group + 1) * GROUP]
        for side in range(2):
            rows = slice(side * PAD, (side + 1) * PAD)
            query = qkv_ref[part, rows, lane : lane + 128]
            key = qkv_ref[part, rows, half + lane : half + lane + 128]
            value = qkv_ref[part, rows, 2 * half + lane : 2 * half + lane + 128]
            scores = mm_nt(stack_heads(query, mask), key).reshape(GROUP, PAD, PAD) * SCALE
            scores = scores + (bias + mask_ref[side][None])
            peak = jnp.max(scores, -1, keepdims=True)
            expos = jnp.exp(scores - peak)
            totals = jnp.sum(expos, -1, keepdims=True)
            probs = (expos / totals).astype(BF).reshape(STACK, PAD)
            probs_ref[side, group] = probs
            attended = unstack_heads(mm(probs, value), mask)
            att_ref[rows, group * 128 : (group + 1) * 128] = attended.astype(BF)
    first, second = split_halves(att_ref[...])
    mixed = mm(first, out_weights[0][...]) + mm(second, out_weights[1][...])
    mid_ref[...] = x + mixed + small_ref[OUT_BIAS : OUT_BIAS + 1]


def roll_rows(values_ref, result_ref):
    rest = HALF - ROLL
    result_ref[...] = jnp.zeros_like(result_ref)
    for side in range(2):
        here, there = side * PAD, (1 - side) * PAD
        result_ref[here : here + rest, :] = values_ref[here + ROLL : here + HALF, :]
        result_ref[here + rest : here + HALF, :] = values_ref[there : there + ROLL, :]


def unroll_rows(values_ref, result_ref):
    rest = HALF - ROLL
    result_ref[...] = jnp.zeros_like(result_ref)
    for side in range(2):
        here, there = side * PAD, (1 - side) * PAD
        result_ref[here + ROLL : here + HALF, :] = values_ref[here : here + rest, :]
        result_ref[here : here + ROLL, :] = values_ref[there + rest : there + HALF, :]


def clear_padding(values):
    row = lax.broadcasted_iota(jnp.int32, values.shape, 0) % PAD
    return jnp.where(row < HALF, values, 0.0)


def ffn_fwd_kernel(
    layer, weights, mid_ref, small_ref, x_ref, normed_ref, slope_ref, hidden_ref, scratch, flat,
):
    up_weights, down_weights = weights
    half = D // 2
    middle = mid_ref[...]
    xhat, _ = norm_parts(middle)
    normed = (
        xhat * small_ref[GAIN_TWO : GAIN_TWO + 1] + small_ref[SHIFT_TWO : SHIFT_TWO + 1]
    ).astype(BF)
    normed_ref[...] = normed
    total = jnp.zeros((ROWS, D), F32)
    per_part = FF // 2 // CHUNK
    for chunk in range(FF // CHUNK):
        part, at = chunk // per_part, (chunk % per_part) * CHUNK
        pre = mm(normed, up_weights[part][:, at : at + CHUNK]) + small_ref[UP_BIAS + chunk : UP_BIAS + chunk + 1]
        hidden, slope = gelu_and_slope(pre)
        hidden = hidden.astype(BF)
        slope_ref[:, chunk * CHUNK : (chunk + 1) * CHUNK] = slope.astype(BF)
        hidden_ref[:, chunk * CHUNK : (chunk + 1) * CHUNK] = hidden
        total = total + mm(hidden, down_weights[part][at : at + CHUNK, :])
    result = middle + total + small_ref[DOWN_BIAS : DOWN_BIAS + 1]
    scratch[...] = result
    if layer % 2 == 0:
        roll_rows(scratch, x_ref)
    else:
        rest = HALF - ROLL
        flat[ROLL : ROLL + HALF, :] = scratch[0:HALF, 0:half]
        flat[ROLL + HALF : IMAGE, :] = scratch[PAD : PAD + rest, 0:half]
        flat[0:ROLL, :] = scratch[PAD + rest : PAD + HALF, 0:half]
        x_ref[...] = flat[0:IMAGE, :].astype(BF)


def ffn_bwd_kernel(
    layer, weights, grad_ref, slope_ref, hidden_ref, normed_ref, small_ref, mid_ref,
    grad_mid_ref, keep_ref, send_ref, small_keep_ref, small_send_ref,
):
    up_weights, down_weights = weights
    half = D // 2
    grad = grad_ref[...]
    grad_down = grad.astype(BF)
    near = grad_down[:, :half]
    per_part = FF // 2 // CHUNK
    outs = (keep_ref, send_ref)
    small_outs = (small_keep_ref, small_send_ref)
    grad_normed = jnp.zeros((ROWS, D), F32)
    for chunk in range(FF // CHUNK):
        part, at = chunk // per_part, (chunk % per_part) * CHUNK
        at_lanes = slice(at, at + CHUNK)
        lanes = slice(chunk * CHUNK, (chunk + 1) * CHUNK)
        grad_hidden = mm_nt(grad_down, down_weights[part][at_lanes, :])
        grad_pre_wide = (grad_hidden * slope_ref[:, lanes].astype(F32)).astype(BF)
        outs[part][at : at + CHUNK, :] = mm_tn(hidden_ref[:, lanes], near).astype(BF)
        grad_up = mm_tn(normed_ref[:, :half], grad_pre_wide).astype(BF)
        bias_sum = jnp.sum(grad_pre_wide.astype(F32), 0, keepdims=True)
        for piece in range(CHUNK // half):
            place = FF // 2 + (at // half + piece) * half
            outs[part][place : place + half, :] = grad_up[:, piece * half : (piece + 1) * half]
            line = 3 + at // half + piece
            small_outs[part][line : line + 1, :] = bias_sum[:, piece * half : (piece + 1) * half]
        grad_normed = grad_normed + mm_nt(grad_pre_wide, up_weights[part][:, at_lanes])
    grad_input, grad_gain, grad_shift = norm_back(
        grad_normed, mid_ref[...], small_ref[GAIN_TWO : GAIN_TWO + 1]
    )
    grad_mid_ref[...] = clear_padding(grad + grad_input)
    down_bias = jnp.sum(near.astype(F32), 0, keepdims=True)
    for small in small_outs:
        small[0:1, :] = down_bias
        small[1:2, :] = grad_gain[:, :half]
        small[2:3, :] = grad_shift[:, :half]
        small[7:8, :] = jnp.zeros((1, half), F32)


def attn_bwd_kernel(
    layer, weights, grad_mid_ref, att_ref, qkv_ref, probs_ref, picks_ref, picks_t_ref, normed_ref, small_ref, x_ref,
    grad_ref, keep_ref, send_ref, small_keep_ref, small_send_ref, table_ref, grad_qkv, scratch, flat,
):
    qkv_weights, out_weights = weights
    half = D // 2
    grad_mid = grad_mid_ref[...]
    grad_att = grad_mid.astype(BF)
    near = grad_att[:, :half]
    outs = (keep_ref, send_ref)
    small_outs = (small_keep_ref, small_send_ref)
    mask = head_mask()
    grad_normed = jnp.zeros((ROWS, D), F32)
    for part in range(2):
        grad_attended = mm_nt(grad_att, out_weights[part][...]).astype(BF)
        outs[part][3 * half : 4 * half, :] = mm_tn(att_ref[:, part * half : (part + 1) * half], near).astype(BF)
        for inner in range(2):
            group, lane = part * 2 + inner, inner * 128
            tables = [jnp.zeros((64, PAD), F32) for _ in range(GROUP)]
            for side in range(2):
                rows = slice(side * PAD, (side + 1) * PAD)
                query = stack_heads(qkv_ref[part, rows, lane : lane + 128], mask)
                key = qkv_ref[part, rows, half + lane : half + lane + 128]
                value = qkv_ref[part, rows, 2 * half + lane : 2 * half + lane + 128]
                grad_out = stack_heads(grad_attended[rows, lane : lane + 128], mask)
                probs_low = probs_ref[side, group]
                probs = probs_low.astype(F32)
                grad_probs = mm_nt(grad_out, value)
                weighted = jnp.sum(probs * grad_probs, -1, keepdims=True)
                grad_scores = (probs * (grad_probs - weighted)).astype(BF)
                grad_value = mm_tn(probs_low, grad_out)
                grad_query = unstack_heads(mm(grad_scores, key), mask) * SCALE
                grad_key = mm_tn(grad_scores, query) * SCALE
                grad_qkv[part, rows, lane : lane + 128] = grad_query.astype(BF)
                grad_qkv[part, rows, half + lane : half + lane + 128] = grad_key.astype(BF)
                grad_qkv[part, rows, 2 * half + lane : 2 * half + lane + 128] = grad_value.astype(BF)
                picked = mm(grad_scores, picks_ref[...]).astype(BF)
                for head in range(GROUP):
                    tables[head] = tables[head] + mm(picks_t_ref[0:64, :], picked[head * PAD : (head + 1) * PAD])
            for head in range(GROUP):
                table_ref[group * GROUP + head] = tables[head][:56]
        for kind in range(3):
            lanes = slice(kind * half, (kind + 1) * half)
            grads = grad_qkv[part, :, lanes]
            outs[part][kind * half : (kind + 1) * half, :] = mm_tn(normed_ref[:, :half], grads).astype(BF)
            grad_normed = grad_normed + mm_nt(grads, qkv_weights[part][kind])
            if kind != 1:
                line = 3 + kind // 2
                small_outs[part][line : line + 1, :] = jnp.sum(grads.astype(F32), 0, keepdims=True)
    grad_input, grad_gain, grad_shift = norm_back(
        grad_normed, x_ref[...], small_ref[GAIN_ONE : GAIN_ONE + 1]
    )
    total = clear_padding(grad_mid + grad_input)
    scratch[...] = total
    if layer % 2 == 1:
        unroll_rows(scratch, grad_ref)
    else:
        flat[0:HALF, :] = scratch[0:HALF, 0:half]
        flat[HALF:IMAGE, :] = scratch[PAD : PAD + HALF, 0:half]
        grad_ref[...] = flat[0:IMAGE, :].astype(BF)
    out_bias = jnp.sum(near.astype(F32), 0, keepdims=True)
    for small in small_outs:
        small[0:1, :] = out_bias
        small[1:2, :] = grad_gain[:, :half]
        small[2:3, :] = grad_shift[:, :half]
        small[5:8, :] = jnp.zeros((3, half), F32)


DOWN_AT, UP_AT, QKV_AT, OUT_AT, TAIL_AT = 0, 1024, 2048, 2816, 3072
BLOCK_ROWS = 3200
RING = 8
PIECE = BLOCK_ROWS // (2 * RING)


def unpack_kernel(count, *refs):
    starts = refs[0]
    pieces = refs[1 : 1 + 2 * count]
    (qkv_ref, qv_ref, out_ref, out_bias_ref, up_ref, up_bias_ref, down_ref, down_bias_ref,
     gain_ref, shift_ref, table_ref, block) = refs[1 + 2 * count :]
    half = D // 2
    for layer in range(LAYERS):
        for number in range(count):
            piece = pieces[layer * count + number]
            size = piece.shape[0]
            at = pl.multiple_of(starts[number], 8)
            block[pl.ds(at, size), :] = piece[...].astype(F32)
        down_ref[layer] = block[DOWN_AT : DOWN_AT + FF // 2, :]
        for piece in range(4):
            up_ref[layer, :, piece * half : (piece + 1) * half] = block[
                UP_AT + piece * half : UP_AT + (piece + 1) * half, :
            ]
        for kind in range(3):
            qkv_ref[layer, kind] = block[QKV_AT + kind * half : QKV_AT + (kind + 1) * half, :]
        out_ref[layer] = block[OUT_AT : OUT_AT + half, :]
        tail = block[TAIL_AT : TAIL_AT + 24, :]
        down_bias_ref[layer : layer + 1, :] = tail[0:1]
        gain_ref[layer, 1:2, :] = tail[1:2]
        shift_ref[layer, 1:2, :] = tail[2:3]
        for piece in range(4):
            up_bias_ref[layer : layer + 1, piece * half : (piece + 1) * half] = tail[3 + piece : 4 + piece]
        out_bias_ref[layer : layer + 1, :] = tail[8:9]
        gain_ref[layer, 0:1, :] = tail[9:10]
        shift_ref[layer, 0:1, :] = tail[10:11]
        qv_ref[layer] = tail[11:13]
        table_ref[layer] = tail[16:24, :TABLE]


ANY = pl.BlockSpec(memory_space=pl.ANY)
VMEM = pl.BlockSpec(memory_space=pltpu.VMEM)
SMEM = pl.BlockSpec(memory_space=pltpu.SMEM)


def call(kernel, outs, scratch, args, micros, specs=None, out_specs=None, limit=40, aliases=None):
    return pl.pallas_call(
        kernel,
        out_shape=[jax.ShapeDtypeStruct(shape, kind) for shape, kind in outs],
        in_specs=specs or [VMEM] * len(args),
        out_specs=out_specs or [VMEM] * len(outs),
        scratch_shapes=scratch,
        input_output_aliases=aliases or {},
        compiler_params=pltpu.CompilerParams(vmem_limit_bytes=limit * 1024 * 1024),
        cost_estimate=pl.CostEstimate(flops=int(micros * 1.15e6), bytes_accessed=0, transcendentals=0),
    )(*args)


def layer_call(kernel, layer, outs, scratch, weights, args, micros, attn, behind=()):
    rooms, weight_copies, load = (
        (ATTN_ROOMS, ATTN_COPIES, attn_weights) if attn else (FFN_ROOMS, FFN_COPIES, ffn_weights)
    )

    def run(*refs):
        refs = list(refs)

        def take(number):
            taken = refs[:number]
            del refs[:number]
            return taken

        weight_refs, arg_refs, _, out_refs = take(len(weights)), take(len(args)), take(len(behind)), take(len(outs))
        weight_rooms, arg_rooms, others, (sems,) = take(len(rooms)), take(len(args)), take(len(scratch)), take(1)
        fetched = [
            whole_fetch(ref, room, sems, weight_copies + at) for at, (ref, room) in enumerate(zip(arg_refs, arg_rooms))
        ]
        loaded = load(layer, weight_refs, weight_rooms, sems, 0)
        if kernel in FORWARD:
            pending = fetched[:2] + loaded[0] + fetched[2:] + loaded[1]
        else:
            pending = fetched[:1] + loaded[1] + fetched[1:] + loaded[0]
        for item in pending:
            item.start()
        kernel(layer, loaded, *fetched, *out_refs, *others)
        for item in pending:
            item.ready()

    spaces = (
        [pltpu.VMEM(shape, kind) for shape, kind in rooms]
        + [pltpu.VMEM(a.shape, a.dtype) for a in args]
        + scratch
        + [pltpu.SemaphoreType.DMA((weight_copies + len(args),))]
    )
    operands = [*weights, *args, *behind]
    return call(run, outs, spaces, operands, micros, [ANY] * len(operands))


FORWARD = (attn_fwd_kernel, ffn_fwd_kernel)


def part_of(kernel, layer):
    def run(*refs):
        return kernel(layer, *refs)

    return run


def ring_perms():
    order = [0, 2, 4, 6, 7, 5, 3, 1]
    onward = [(order[i], order[(i + 1) % RING]) for i in range(RING)]
    return onward, [(b, a) for a, b in onward]


def ring_sum(pieces, place, one, two):
    onward, back = ring_perms()
    for step in range(RING - 1):
        one, two = lax.ppermute(one, "dp", onward), lax.ppermute(two, "dp", back)
        one = one + pick(pieces, (place - 2 - step) % RING)
        two = two + pick(pieces, RING + (place + 2 + step) % RING)
    return ring_gather(one, two)


def pick(values, index):
    return lax.dynamic_index_in_dim(values, index, 0, keepdims=False)


def ring_gather(one, two):
    onward, back = ring_perms()
    pieces = [one, two]
    for _ in range(RING - 1):
        one, two = lax.ppermute(one, "dp", onward), lax.ppermute(two, "dp", back)
        pieces += [one, two]
    return pieces


def piece_starts(place):
    starts = []
    for step in range(RING):
        starts += [((place - step) % RING) * PIECE, (RING + (place + step) % RING) * PIECE]
    return jnp.stack(starts).astype(jnp.int32)


def on_device(
    ring, tokens, cotangent, qkv_weight, qv_bias, out_weight, out_bias, up_weight, up_bias,
    down_weight, down_bias, norm_gain, norm_shift, bias_table, index_map, region_ids,
):
    half, quarter = D // 2, D // 4
    device = lax.axis_index("dp")
    parity = device % 2
    neighbours = [(i, i ^ 1) for i in range(lax.axis_size("dp"))]

    wholes = [qkv_weight.transpose(0, 2, 1, 3), out_weight, up_weight, down_weight]
    parity_ref = parity.astype(jnp.int32).reshape(1)
    (misc_row,) = call(
        misc_kernel, [((32, half), BF)], [], [qv_bias, up_bias, bias_table.transpose(0, 2, 1)], 1
    )
    row_far = swap(misc_row, "row")
    sources = [*wholes, tokens, cotangent, norm_gain, norm_shift, out_bias, down_bias]
    pack_outs = [((MISC_ROWS, half), BF), ((3 * D, half), BF), ((3 * D, half), BF)]
    misc, *packs, whole = call(
        pack_kernel,
        [*pack_outs, ((LAYERS * TAIL_AT, half), BF)],
        [pltpu.VMEM(value.shape[1:], value.dtype) for value in wholes] * LAYERS
        + [pltpu.VMEM(shape, kind) for shape, kind in pack_outs]
        + [pltpu.SemaphoreType.DMA((8,)), pltpu.SemaphoreType.DMA((21,))],
        [parity_ref, *sources, misc_row],
        3,
        [SMEM] + [ANY] * 4 + [VMEM] * 6 + [ANY],
        [ANY] * 4,
        limit=60,
    )
    whole_row, misc_far = swap(whole, "row"), swap(misc, "col")
    from_col = [swap(pack, "col") for pack in packs]
    from_col[0] = after(from_col[0], misc_far)

    def block(pack, token):
        from_dp = lax.ppermute(pack, "dp", neighbours)
        if token is not None:
            from_dp = after(from_dp, token)
        return [pack, from_dp, whole_row, swap(pack, "row"), swap(from_dp, "row")]

    blocks = [block(from_col[0], None)]
    picks = np.stack([position_one_hot(layer) for layer in range(LAYERS)])
    picks_t = [jnp.asarray(pick.T, BF) for pick in picks]
    picks_all = jnp.asarray(picks, BF)
    picks = [jnp.asarray(pick, BF) for pick in picks]
    masks = [mask_of(layer, region_ids) for layer in range(LAYERS)]
    wide = ((ROWS, D), F32)
    x, grad, *rest = call(
        prep_kernel,
        [wide, wide, ((16, D), F32), ((16, D), F32), ((HEADS, PAD, PAD), F32), ((HEADS, PAD, PAD), F32)],
        [
            pltpu.VMEM((64, LAYERS * HEADS, PAD), F32), pltpu.VMEM((56, PAD), jnp.int32),
            pltpu.VMEM((208, D), F32),
        ],
        [parity_ref, misc, misc_far, misc_row, row_far, index_map, picks_all],
        4,
        [SMEM] + [VMEM] * 6,
    )
    smalls, bias = rest[:2], rest[2:4]
    from_col[1] = after(from_col[1], x)

    image = ((IMAGE, half), BF)
    saved = []
    for layer in range(LAYERS):
        middle, normed_one, qkv, probs, att = layer_call(
            attn_fwd_kernel,
            layer,
            [
                wide, ((ROWS, D), BF), ((2, ROWS, 3 * half), BF),
                ((2, GROUPS, STACK, PAD), BF), ((ROWS, D), BF),
            ],
            [],
            [*wholes[:2], *blocks[layer]],
            [x, smalls[layer], bias[layer], masks[layer]],
            4,
            True,
        )
        result, normed_two, pre, hidden = layer_call(
            ffn_fwd_kernel,
            layer,
            [wide if layer < LAYERS - 1 else image, ((ROWS, D), BF), ((ROWS, FF), BF), ((ROWS, FF), BF)],
            [pltpu.VMEM((ROWS, D), F32), pltpu.VMEM((200, half), F32)],
            [*wholes[2:], *blocks[layer]],
            [middle, smalls[layer]],
            4,
            False,
        )
        if layer == 0:
            blocks.append(block(from_col[1], result))
        saved.append((x, middle, normed_one, qkv, probs, att, normed_two, pre, hidden))
        x = result
    output = x

    heads = HEADS // 2
    one_hot = (index_map[:, :, None] == jnp.arange(256, dtype=jnp.int32)).astype(F32).reshape(SPAN * SPAN, 256)
    sums = [None] * LAYERS
    place = jnp.where(parity == 0, device // 2, RING - 1 - device // 2)
    place_ref = place.astype(jnp.int32).reshape(1)
    for layer in reversed(range(LAYERS)):
        x_in, middle, normed_one, qkv, probs, att, normed_two, pre, hidden = saved[layer]
        small_shape = ((8, half), F32)
        grad_mid, ffn_keep, ffn_send, small_keep, small_send = layer_call(
            ffn_bwd_kernel,
            layer,
            [wide, ((FF, half), BF), ((FF, half), BF), small_shape, small_shape],
            [],
            [*wholes[2:], *blocks[layer]],
            [grad, pre, hidden, normed_two, smalls[layer], middle],
            5,
            False,
        )
        ffn_got = swap(ffn_send, "row")
        grad, keep, send, att_keep, att_send, counts = layer_call(
            attn_bwd_kernel,
            layer,
            [
                wide if layer > 0 else image, ((2 * D, half), BF), ((2 * D, half), BF), small_shape, small_shape,
                ((HEADS, 56, PAD), F32),
            ],
            [pltpu.VMEM((2, ROWS, 3 * half), BF), pltpu.VMEM((ROWS, D), F32), pltpu.VMEM((200, half), F32)],
            [*wholes[:2], *blocks[layer]],
            [grad_mid, att, qkv, probs, picks[layer], picks_t[layer], normed_one, smalls[layer], x_in],
            6,
            True,
        )
        got = swap(send, "row")
        table = jnp.dot(counts[:, :SPAN, :SPAN].reshape(HEADS, SPAN * SPAN), one_hot, precision=HIGH)
        tail_keep = jnp.concatenate([small_keep, att_keep, table[:heads]], 0)
        tail_send = jnp.concatenate([small_send, att_send, table[heads:]], 0)
        pieces, one, two = call(
            combine_kernel,
            [((2 * RING, PIECE, half), BF), ((PIECE, half), BF), ((PIECE, half), BF)],
            [pltpu.VMEM((BLOCK_ROWS, half), F32)],
            [place_ref, ffn_keep, ffn_got, keep, got, tail_keep, swap(tail_send, "row")],
            2,
            [SMEM] + [VMEM] * 6,
            limit=24,
        )
        if ring:
            sums[layer] = ring_sum(pieces, place, one, two)
        else:
            sums[layer] = [lax.psum(pieces.reshape(BLOCK_ROWS, half), "dp")]
    input_grad = grad

    count = len(sums[0])
    starts = piece_starts(place) if ring else jnp.zeros((1,), jnp.int32)
    qkv, qv, outw, outb, up, upb, down, downb, gain, shift, table = call(
        part_of(unpack_kernel, count),
        [
            ((LAYERS, 3, half, half), F32), ((LAYERS, 2, half), F32), ((LAYERS, half, half), F32),
            ((LAYERS, half), F32), ((LAYERS, half, FF // 2), F32), ((LAYERS, FF // 2), F32),
            ((LAYERS, FF // 2, half), F32), ((LAYERS, half), F32), ((LAYERS, 2, half), F32),
            ((LAYERS, 2, half), F32), ((LAYERS, heads, TABLE), F32),
        ],
        [pltpu.VMEM((BLOCK_ROWS, half), F32)],
        [starts, *sums[0], *sums[1]],
        4,
        [SMEM] + [VMEM] * (2 * count),
    )
    return (
        output, input_grad, qkv.transpose(0, 2, 1, 3), qv, outw, outb, up, upb, down, downb, gain, shift,
        table.transpose(0, 2, 1),
    )


def solution(mesh):
    in_specs = (
        P(("dp", "row"), "col"),
        P(("dp", "row"), "col"),
        P(None, "col", None, "row"),
        P(None, None, "row"),
        P(None, "row", "col"),
        P(None, "col"),
        P(None, "col", "row"),
        P(None, "row"),
        P(None, "row", "col"),
        P(None, "col"),
        P(None, None, "col"),
        P(None, None, "col"),
        P(None, None, "row"),
        P(),
        P(),
    )
    out_specs = (
        P(("dp", "row"), "col"),
        P(("dp", "row"), "col"),
        P(None, "col", None, "row"),
        P(None, None, "row"),
        P(None, "row", "col"),
        P(None, "col"),
        P(None, "col", "row"),
        P(None, "row"),
        P(None, "row", "col"),
        P(None, "col"),
        P(None, None, "col"),
        P(None, None, "col"),
        P(None, None, "row"),
    )
    ring = mesh.shape["dp"] == RING
    return jax.shard_map(
        part_of(on_device, ring), mesh=mesh, in_specs=in_specs, out_specs=out_specs, check_vma=False
    )
```

```python
import math

import jax
import jax.numpy as jnp
import numpy as np
from jax import lax
from jax.experimental import pallas as pl
from jax.experimental.pallas import tpu as pltpu
from jax.sharding import PartitionSpec as P

D = 512
HEADS = 16
HEAD_DIM = 32
FF = 2048
GRID = 14
WINDOW = 7
SHIFT = 3
TABLE = 169
LAYERS = 2
SPAN = WINDOW * WINDOW
IMAGE = GRID * GRID

EPS = 1e-05
NEG = -1000000000.0
HIGH = lax.Precision.HIGHEST
SCALE = 1.0 / math.sqrt(HEAD_DIM)

HALF = IMAGE // 2
PAD = 128
ROWS = 2 * PAD
ROLL = SHIFT * GRID
GROUP = 128 // HEAD_DIM
GROUPS = HEADS // GROUP
STACK = GROUP * PAD
CHUNK = 512
BF = jnp.bfloat16
F32 = jnp.float32


def swap(values, axis):
    return lax.ppermute(values, axis, [(0, 1), (1, 0)])


def mm(left, right):
    return lax.dot_general(left, right, (((1,), (0,)), ((), ())), preferred_element_type=F32)


def mm_nt(left, right):
    return lax.dot_general(left, right, (((1,), (1,)), ((), ())), preferred_element_type=F32)


def mm_tn(left, right):
    return lax.dot_general(left, right, (((0,), (0,)), ((), ())), preferred_element_type=F32)


def token_positions(layer):
    token = np.arange(HALF)
    line, column = token // GRID, token % GRID
    if layer % 2 == 1:
        column = (column - SHIFT) % GRID
    return line * WINDOW + column % WINDOW, column // WINDOW, line * GRID + column


def position_one_hot(layer):
    position, _, _ = token_positions(layer)
    picks = np.zeros((PAD, PAD), np.float32)
    picks[np.arange(HALF), position] = 1.0
    return picks


def mask_of(layer, region_ids):
    _, window, place = token_positions(layer)
    same = np.zeros((PAD, PAD), bool)
    same[:HALF, :HALF] = window[:, None] == window[None, :]
    same[HALF:, :HALF] = True
    allowed = jnp.broadcast_to(jnp.asarray(same)[None], (2, PAD, PAD))
    if layer % 2 == 1:
        ids = jnp.roll(region_ids.reshape(2, WINDOW, GRID), SHIFT, 2).reshape(2, HALF)
        ids = jnp.pad(ids, ((0, 0), (0, PAD - HALF)), constant_values=-1)
        pad_row = jnp.asarray(np.arange(PAD) >= HALF)[None, :, None]
        allowed = allowed & ((ids[:, :, None] == ids[:, None, :]) | pad_row)
    return jnp.where(allowed, 0.0, NEG).astype(F32)


def head_mask():
    lane = lax.broadcasted_iota(jnp.int32, (STACK, PAD), 1) // HEAD_DIM
    row = lax.broadcasted_iota(jnp.int32, (STACK, PAD), 0) // PAD
    return lane == row


def stack_heads(values, mask):
    tiled = jnp.concatenate([values] * GROUP, axis=0)
    return jnp.where(mask, tiled, jnp.zeros_like(tiled))


def unstack_heads(values, mask):
    kept = jnp.where(mask, values, 0.0)
    total = kept[0:PAD]
    for head in range(1, GROUP):
        total = total + kept[head * PAD : (head + 1) * PAD]
    return total


def norm_parts(values):
    average = jnp.mean(values, -1, keepdims=True)
    centred = values - average
    variance = jnp.mean(centred * centred, -1, keepdims=True)
    inverse = lax.rsqrt(variance + EPS)
    return centred * inverse, inverse


def norm_back(grad_normed, values, gain):
    xhat, inverse = norm_parts(values)
    scaled = grad_normed * gain
    mean_one = jnp.mean(scaled, -1, keepdims=True)
    mean_two = jnp.mean(scaled * xhat, -1, keepdims=True)
    grad_input = inverse * (scaled - mean_one - xhat * mean_two)
    return grad_input, jnp.sum(grad_normed * xhat, 0, keepdims=True), jnp.sum(grad_normed, 0, keepdims=True)


def split_halves(values):
    return values[:, : D // 2], values[:, D // 2 :]


def gelu_and_slope(values):
    below = 0.5 * (1.0 + lax.erf(values * (1.0 / math.sqrt(2.0))))
    density = jnp.exp(-0.5 * values * values) * (1.0 / math.sqrt(2.0 * math.pi))
    return values * below, below + values * density


TABLE_ROWS = 176

GAIN_ONE, GAIN_TWO, SHIFT_ONE, SHIFT_TWO, OUT_BIAS, DOWN_BIAS, Q_BIAS, V_BIAS, UP_BIAS = 0, 1, 2, 3, 4, 5, 6, 7, 8


def prep_kernel(
    parity_ref, misc_ref, misc_far, row_ref, row_far, index_ref, picks_ref,
    x_ref, grad_ref, small_zero, small_one, bias_zero, bias_one, pairs_ref, index_pad, flat,
):
    half, quarter = D // 2, D // 4
    even = parity_ref[0] == 0

    def ordered(values):
        low, high = values[:, :quarter], values[:, quarter:]
        return jnp.where(even, low, high), jnp.where(even, high, low)

    def lay_out(at):
        first, second = ordered(misc_far[at : at + 208, :].astype(F32))
        flat[:, 0:half] = misc_ref[at : at + 208, :].astype(F32)
        flat[:, half : half + quarter] = first
        flat[:, half + quarter :] = second

    x_ref[...] = jnp.zeros_like(x_ref)
    grad_ref[...] = jnp.zeros_like(grad_ref)
    lay_out(TOKENS_AT)
    x_ref[0:HALF, :] = flat[0:HALF, :]
    x_ref[PAD : PAD + HALF, :] = flat[HALF:IMAGE, :]
    lay_out(COT_AT)
    rest = HALF - ROLL
    grad_ref[0:HALF, :] = flat[ROLL : ROLL + HALF, :]
    grad_ref[PAD : PAD + rest, :] = flat[ROLL + HALF : IMAGE, :]
    grad_ref[PAD + rest : PAD + HALF, :] = flat[0:ROLL, :]

    near = misc_ref[SMALL_AT:MISC_ROWS, :].astype(F32)
    far_first, far_second = ordered(misc_far[SMALL_AT:MISC_ROWS, :].astype(F32))
    rows_near, rows_far = row_ref[...].astype(F32), row_far[...].astype(F32)
    for layer, small in enumerate((small_zero, small_one)):
        small[...] = jnp.zeros_like(small)

        def features(row, source):
            small[row : row + 1, 0:half] = near[source : source + 1]
            small[row : row + 1, half : half + quarter] = far_first[source : source + 1]
            small[row : row + 1, half + quarter :] = far_second[source : source + 1]

        for which in range(2):
            features(GAIN_ONE + which, 2 * layer + which)
            features(SHIFT_ONE + which, 4 + 2 * layer + which)
            for part, source in enumerate((rows_near, rows_far)):
                lanes = slice(part * half, (part + 1) * half)
                at = 2 * layer + which
                small[Q_BIAS + which : Q_BIAS + which + 1, lanes] = source[at : at + 1]
                line = UP_BIAS + 2 * part + which
                for piece in range(2):
                    at = 4 + 2 * (2 * which + piece) + layer
                    small[line : line + 1, piece * half : (piece + 1) * half] = source[at : at + 1]
        features(OUT_BIAS, 8 + layer)
        features(DOWN_BIAS, 10 + layer)

    heads = HEADS // 2
    tables = []
    for layer in range(LAYERS):
        for source in (rows_near, rows_far):
            tables.append(source[16 + layer * heads : 16 + (layer + 1) * heads, :TABLE_ROWS])
    table = jnp.concatenate(tables, 0).astype(BF)
    index_pad[...] = jnp.full(index_pad.shape, -1, jnp.int32)
    index_pad[0:SPAN, 0:SPAN] = index_ref[...]
    pairs_ref[SPAN:64] = jnp.zeros((64 - SPAN, LAYERS * HEADS, PAD), F32)
    for position in range(SPAN):
        wanted = index_pad[position : position + 1, :]
        hot = (lax.broadcasted_iota(jnp.int32, (TABLE_ROWS, PAD), 0) == wanted).astype(F32).astype(BF)
        pairs_ref[position] = mm(table, hot)
    for layer, bias_ref in enumerate((bias_zero, bias_one)):
        picks = picks_ref[layer]
        for head in range(HEADS):
            bias = pairs_ref[:, layer * HEADS + head, :]
            spread = mm(picks[:, :64], bias.astype(BF)).astype(BF)
            bias_ref[head] = mm_nt(spread, picks)


class Fetch:
    def __init__(self, copies, ref):
        self.copies, self.ref, self.waiting = copies, ref, True

    def start(self):
        for copy in self.copies:
            copy.start()

    def ready(self):
        if self.waiting:
            self.waiting = False
            for copy in self.copies:
                copy.wait()
        return self.ref

    def __getitem__(self, index):
        return self.ready()[index]


def whole_fetch(source, room, sems, at):
    return Fetch([pltpu.make_async_copy(source, room, sems.at[at])], room)


def attn_weights(layer, sources, rooms, sems, at):
    half, quarter = D // 2, D // 4
    qkv, out, from_col, from_dp, whole_row, from_col_row, from_dp_row = sources
    qkvs, outs = [], []
    whole_at = layer * TAIL_AT
    for part, packs in enumerate(((from_col, from_dp), (from_col_row, from_dp_row))):
        room_qkv, room_out = rooms[2 * part], rooms[2 * part + 1]
        pairs, pairs_out = [], []
        for kind in range(3):
            lines = slice(whole_at + QKV_AT + kind * half, whole_at + QKV_AT + (kind + 1) * half)
            source = qkv.at[layer, kind] if part == 0 else whole_row.at[lines, :]
            pairs.append((source, room_qkv.at[kind, 0:half, :]))
        source = out.at[layer] if part == 0 else whole_row.at[whole_at + OUT_AT : whole_at + TAIL_AT, :]
        pairs_out.append((source, room_out.at[:, 0:half]))
        for slot, pack in enumerate(packs):
            first = half + slot * quarter
            for kind in range(3):
                pairs.append(
                    (
                        pack.at[kind * quarter : (kind + 1) * quarter, :],
                        room_qkv.at[kind, first : first + quarter, :],
                    )
                )
            for side in range(2):
                lanes = slice(side * quarter, (side + 1) * quarter)
                pairs_out.append((pack.at[3 * quarter : 4 * quarter, lanes], room_out.at[lanes, first : first + quarter]))
        for found, room, list_of in ((pairs, room_qkv, qkvs), (pairs_out, room_out, outs)):
            copies = []
            for source, target in found:
                copies.append(pltpu.make_async_copy(source, target, sems.at[at]))
                at += 1
            list_of.append(Fetch(copies, room))
    return qkvs, outs


ATTN_COPIES = 2 * (9 + 5)
ATTN_ROOMS = [((3, D, D // 2), BF), ((D // 2, D), BF)] * 2


def ffn_weights(layer, sources, rooms, sems, at):
    half, quarter, wide = D // 2, D // 4, FF // 4
    up, down, from_col, from_dp, whole_row, from_col_row, from_dp_row = sources
    ups, downs = [], []
    whole_at = layer * TAIL_AT
    for part, packs in enumerate(((from_col, from_dp), (from_col_row, from_dp_row))):
        room_up, room_down = rooms[2 * part], rooms[2 * part + 1]
        pairs, pairs_down = [], []
        for piece in range(4):
            lanes = slice(piece * half, (piece + 1) * half)
            lines = slice(whole_at + UP_AT + piece * half, whole_at + UP_AT + (piece + 1) * half)
            source = up.at[layer, :, lanes] if part == 0 else whole_row.at[lines, :]
            pairs.append((source, room_up.at[0:half, lanes]))
        source = down.at[layer] if part == 0 else whole_row.at[whole_at + DOWN_AT : whole_at + UP_AT, :]
        pairs_down.append((source, room_down.at[:, 0:half]))
        for slot, pack in enumerate(packs):
            first = half + slot * quarter
            for piece in range(4):
                lanes = slice(piece * half, (piece + 1) * half)
                pairs.append(
                    (
                        pack.at[D + piece * quarter : D + (piece + 1) * quarter, :],
                        room_up.at[first : first + quarter, lanes],
                    )
                )
            for side in range(2):
                lanes = slice(side * quarter, (side + 1) * quarter)
                pairs_down.append(
                    (
                        pack.at[2 * D :, lanes],
                        room_down.at[side * wide : (side + 1) * wide, first : first + quarter],
                    )
                )
        for found, room, list_of in ((pairs, room_up, ups), (pairs_down, room_down, downs)):
            copies = []
            for source, target in found:
                copies.append(pltpu.make_async_copy(source, target, sems.at[at]))
                at += 1
            list_of.append(Fetch(copies, room))
    return ups, downs


FFN_COPIES = 2 * (12 + 5)
FFN_ROOMS = [((D, FF // 2), BF), ((FF // 2, D), BF)] * 2


def misc_kernel(qv_bias, up_bias, table, misc_row):
    half = D // 2
    rows = [qv_bias[0], qv_bias[1]] + [up_bias[:, piece * half : (piece + 1) * half] for piece in range(4)]
    rows = [row.astype(F32) for row in rows] + [jnp.zeros((4, half), F32)]
    misc_row[0:16, :] = jnp.concatenate(rows, 0).astype(BF)
    tables = jnp.concatenate([table[layer].astype(F32) for layer in range(LAYERS)], 0)
    misc_row[16:32, :] = jnp.pad(tables, ((0, 0), (0, half - TABLE))).astype(BF)


def pack_kernel(
    parity_ref, qkv, out, up, down, tokens, cot, gain, shift, out_bias, down_bias, _,
    pack_zero, pack_one, whole, *rest,
):
    rooms, results, (in_sems, out_sems) = rest[:8], rest[8:11], rest[11:]
    half, quarter = D // 2, D // 4
    even = parity_ref[0] == 0
    fetched = []
    for layer in range(LAYERS):
        for number, source in enumerate((qkv, out, up, down)):
            at = 4 * layer + number
            fetched.append(whole_fetch(source.at[layer], rooms[at], in_sems, at))
    for item in fetched:
        item.start()
    sent = []

    def send(source, target):
        copy = pltpu.make_async_copy(source, target, out_sems.at[len(sent)])
        copy.start()
        sent.append(copy)

    misc = results[0]
    misc[...] = jnp.zeros_like(misc)
    misc[TOKENS_AT : TOKENS_AT + IMAGE, :] = tokens[...]
    misc[COT_AT : COT_AT + IMAGE, :] = cot[...]
    rows = [gain[0], gain[1], shift[0], shift[1], out_bias[...], down_bias[...]]
    misc[SMALL_AT : SMALL_AT + 12, :] = jnp.concatenate([row.astype(F32) for row in rows], 0).astype(BF)
    send(misc, pack_zero.at[0:MISC_ROWS, :])
    for layer in range(LAYERS):
        pack = results[1 + layer]
        at = layer * TAIL_AT
        qkv_l, out_l, up_l, down_l = [item.ready() for item in fetched[4 * layer : 4 * layer + 4]]
        for kind in range(3):
            pack[kind * quarter : (kind + 1) * quarter, :] = jnp.where(
                even, qkv_l[kind, 0:quarter, :], qkv_l[kind, quarter:half, :]
            )
        chosen = jnp.where(even, out_l[:, 0:quarter], out_l[:, quarter:half])
        pack[3 * quarter : 4 * quarter, 0:quarter] = chosen[0:quarter]
        pack[3 * quarter : 4 * quarter, quarter:half] = chosen[quarter:half]
        chosen = jnp.where(even, up_l[0:quarter, :], up_l[quarter:half, :])
        for piece in range(4):
            lines = slice(D + piece * quarter, D + (piece + 1) * quarter)
            pack[lines, :] = chosen[:, piece * half : (piece + 1) * half]
        chosen = jnp.where(even, down_l[:, 0:quarter], down_l[:, quarter:half])
        pack[2 * D :, 0:quarter] = chosen[0 : FF // 4]
        pack[2 * D :, quarter:half] = chosen[FF // 4 :]
        send(pack, pack_zero.at[MISC_ROWS:, :] if layer == 0 else pack_one)
        send(down_l, whole.at[at + DOWN_AT : at + UP_AT, :])
        for piece in range(4):
            lines = slice(at + UP_AT + piece * half, at + UP_AT + (piece + 1) * half)
            send(up_l.at[:, piece * half : (piece + 1) * half], whole.at[lines, :])
        for kind in range(3):
            send(qkv_l.at[kind], whole.at[at + QKV_AT + kind * half : at + QKV_AT + (kind + 1) * half, :])
        send(out_l, whole.at[at + OUT_AT : at + TAIL_AT, :])
    for copy in sent:
        copy.wait()


def after_kernel(*refs):
    pass


def after(value, token):
    (result,) = call(
        after_kernel, [(value.shape, value.dtype)], [], [value, token], 0, [ANY] * 2, [ANY], limit=1, aliases={0: 0}
    )
    return result


TOKENS_AT, COT_AT, SMALL_AT, MISC_ROWS = 0, 208, 416, 432


def combine_kernel(place_ref, ffn_keep, ffn_got, keep, got, tail_keep, tail_got, *rest):
    pieces_ref, one_ref, two_ref, flat = rest[-4:]
    flat[0:FF, :] = ffn_keep[...].astype(F32) + ffn_got[...].astype(F32)
    flat[FF : FF + 2 * D, :] = keep[...].astype(F32) + got[...].astype(F32)
    flat[TAIL_AT:, :] = jnp.zeros((BLOCK_ROWS - TAIL_AT, D // 2), F32)
    flat[TAIL_AT : TAIL_AT + 24, :] = tail_keep[...] + tail_got[...]
    for number in range(2 * RING):
        pieces_ref[number] = flat[number * PIECE : (number + 1) * PIECE, :].astype(BF)
    place = place_ref[0]
    one_ref[...] = pieces_ref[lax.rem(place + RING - 1, RING)]
    two_ref[...] = pieces_ref[RING + lax.rem(place + 1, RING)]


def attn_fwd_kernel(
    layer, weights, x_ref, small_ref, bias_ref, mask_ref, mid_ref, normed_ref, qkv_ref, probs_ref, att_ref,
):
    qkv_weights, out_weights = weights
    x = x_ref[...]
    xhat, _ = norm_parts(x)
    normed = (
        xhat * small_ref[GAIN_ONE : GAIN_ONE + 1] + small_ref[SHIFT_ONE : SHIFT_ONE + 1]
    ).astype(BF)
    normed_ref[...] = normed
    half = D // 2
    for part in range(2):
        lanes = slice(part * half, (part + 1) * half)
        for kind in range(3):
            projected = mm(normed, qkv_weights[part][kind])
            if kind != 1:
                row = Q_BIAS if kind == 0 else V_BIAS
                projected = projected + small_ref[row : row + 1, lanes]
            qkv_ref[part, :, kind * half : (kind + 1) * half] = projected.astype(BF)
    mask = head_mask()
    for group in range(GROUPS):
        part, lane = group // 2, (group % 2) * 128
        bias = bias_ref[group * GROUP : (group + 1) * GROUP]
        for side in range(2):
            rows = slice(side * PAD, (side + 1) * PAD)
            query = qkv_ref[part, rows, lane : lane + 128]
            key = qkv_ref[part, rows, half + lane : half + lane + 128]
            value = qkv_ref[part, rows, 2 * half + lane : 2 * half + lane + 128]
            scores = mm_nt(stack_heads(query, mask), key).reshape(GROUP, PAD, PAD) * SCALE
            scores = scores + (bias + mask_ref[side][None])
            peak = jnp.max(scores, -1, keepdims=True)
            expos = jnp.exp(scores - peak)
            totals = jnp.sum(expos, -1, keepdims=True)
            probs = (expos / totals).astype(BF).reshape(STACK, PAD)
            probs_ref[side, group] = probs
            attended = unstack_heads(mm(probs, value), mask)
            att_ref[rows, group * 128 : (group + 1) * 128] = attended.astype(BF)
    first, second = split_halves(att_ref[...])
    mixed = mm(first, out_weights[0][...]) + mm(second, out_weights[1][...])
    mid_ref[...] = x + mixed + small_ref[OUT_BIAS : OUT_BIAS + 1]


def roll_rows(values_ref, result_ref):
    rest = HALF - ROLL
    result_ref[...] = jnp.zeros_like(result_ref)
    for side in range(2):
        here, there = side * PAD, (1 - side) * PAD
        result_ref[here : here + rest, :] = values_ref[here + ROLL : here + HALF, :]
        result_ref[here + rest : here + HALF, :] = values_ref[there : there + ROLL, :]


def unroll_rows(values_ref, result_ref):
    rest = HALF - ROLL
    result_ref[...] = jnp.zeros_like(result_ref)
    for side in range(2):
        here, there = side * PAD, (1 - side) * PAD
        result_ref[here + ROLL : here + HALF, :] = values_ref[here : here + rest, :]
        result_ref[here : here + ROLL, :] = values_ref[there + rest : there + HALF, :]


def clear_padding(values):
    row = lax.broadcasted_iota(jnp.int32, values.shape, 0) % PAD
    return jnp.where(row < HALF, values, 0.0)


def ffn_fwd_kernel(
    layer, weights, mid_ref, small_ref, x_ref, normed_ref, slope_ref, hidden_ref, scratch, flat,
):
    up_weights, down_weights = weights
    half = D // 2
    middle = mid_ref[...]
    xhat, _ = norm_parts(middle)
    normed = (
        xhat * small_ref[GAIN_TWO : GAIN_TWO + 1] + small_ref[SHIFT_TWO : SHIFT_TWO + 1]
    ).astype(BF)
    normed_ref[...] = normed
    total = jnp.zeros((ROWS, D), F32)
    per_part = FF // 2 // CHUNK
    for chunk in range(FF // CHUNK):
        part, at = chunk // per_part, (chunk % per_part) * CHUNK
        pre = mm(normed, up_weights[part][:, at : at + CHUNK]) + small_ref[UP_BIAS + chunk : UP_BIAS + chunk + 1]
        hidden, slope = gelu_and_slope(pre)
        hidden = hidden.astype(BF)
        slope_ref[:, chunk * CHUNK : (chunk + 1) * CHUNK] = slope.astype(BF)
        hidden_ref[:, chunk * CHUNK : (chunk + 1) * CHUNK] = hidden
        total = total + mm(hidden, down_weights[part][at : at + CHUNK, :])
    result = middle + total + small_ref[DOWN_BIAS : DOWN_BIAS + 1]
    scratch[...] = result
    if layer % 2 == 0:
        roll_rows(scratch, x_ref)
    else:
        rest = HALF - ROLL
        flat[ROLL : ROLL + HALF, :] = scratch[0:HALF, 0:half]
        flat[ROLL + HALF : IMAGE, :] = scratch[PAD : PAD + rest, 0:half]
        flat[0:ROLL, :] = scratch[PAD + rest : PAD + HALF, 0:half]
        x_ref[...] = flat[0:IMAGE, :].astype(BF)


def ffn_bwd_kernel(
    layer, weights, grad_ref, slope_ref, hidden_ref, normed_ref, small_ref, mid_ref,
    grad_mid_ref, keep_ref, send_ref, small_keep_ref, small_send_ref,
):
    up_weights, down_weights = weights
    half = D // 2
    grad = grad_ref[...]
    grad_down = grad.astype(BF)
    near = grad_down[:, :half]
    per_part = FF // 2 // CHUNK
    outs = (keep_ref, send_ref)
    small_outs = (small_keep_ref, small_send_ref)
    grad_normed = jnp.zeros((ROWS, D), F32)
    for chunk in range(FF // CHUNK):
        part, at = chunk // per_part, (chunk % per_part) * CHUNK
        at_lanes = slice(at, at + CHUNK)
        lanes = slice(chunk * CHUNK, (chunk + 1) * CHUNK)
        grad_hidden = mm_nt(grad_down, down_weights[part][at_lanes, :])
        grad_pre_wide = (grad_hidden * slope_ref[:, lanes].astype(F32)).astype(BF)
        outs[part][at : at + CHUNK, :] = mm_tn(hidden_ref[:, lanes], near).astype(BF)
        grad_up = mm_tn(normed_ref[:, :half], grad_pre_wide).astype(BF)
        bias_sum = jnp.sum(grad_pre_wide.astype(F32), 0, keepdims=True)
        for piece in range(CHUNK // half):
            place = FF // 2 + (at // half + piece) * half
            outs[part][place : place + half, :] = grad_up[:, piece * half : (piece + 1) * half]
            line = 3 + at // half + piece
            small_outs[part][line : line + 1, :] = bias_sum[:, piece * half : (piece + 1) * half]
        grad_normed = grad_normed + mm_nt(grad_pre_wide, up_weights[part][:, at_lanes])
    grad_input, grad_gain, grad_shift = norm_back(
        grad_normed, mid_ref[...], small_ref[GAIN_TWO : GAIN_TWO + 1]
    )
    grad_mid_ref[...] = clear_padding(grad + grad_input)
    down_bias = jnp.sum(near.astype(F32), 0, keepdims=True)
    for small in small_outs:
        small[0:1, :] = down_bias
        small[1:2, :] = grad_gain[:, :half]
        small[2:3, :] = grad_shift[:, :half]
        small[7:8, :] = jnp.zeros((1, half), F32)


def attn_bwd_kernel(
    layer, weights, grad_mid_ref, att_ref, qkv_ref, probs_ref, picks_ref, picks_t_ref, normed_ref, small_ref, x_ref,
    grad_ref, keep_ref, send_ref, small_keep_ref, small_send_ref, table_ref, grad_qkv, scratch, flat,
):
    qkv_weights, out_weights = weights
    half = D // 2
    grad_mid = grad_mid_ref[...]
    grad_att = grad_mid.astype(BF)
    near = grad_att[:, :half]
    outs = (keep_ref, send_ref)
    small_outs = (small_keep_ref, small_send_ref)
    mask = head_mask()
    grad_normed = jnp.zeros((ROWS, D), F32)
    for part in range(2):
        grad_attended = mm_nt(grad_att, out_weights[part][...]).astype(BF)
        outs[part][3 * half : 4 * half, :] = mm_tn(att_ref[:, part * half : (part + 1) * half], near).astype(BF)
        for inner in range(2):
            group, lane = part * 2 + inner, inner * 128
            tables = [jnp.zeros((64, PAD), F32) for _ in range(GROUP)]
            for side in range(2):
                rows = slice(side * PAD, (side + 1) * PAD)
                query = stack_heads(qkv_ref[part, rows, lane : lane + 128], mask)
                key = qkv_ref[part, rows, half + lane : half + lane + 128]
                value = qkv_ref[part, rows, 2 * half + lane : 2 * half + lane + 128]
                grad_out = stack_heads(grad_attended[rows, lane : lane + 128], mask)
                probs_low = probs_ref[side, group]
                probs = probs_low.astype(F32)
                grad_probs = mm_nt(grad_out, value)
                weighted = jnp.sum(probs * grad_probs, -1, keepdims=True)
                grad_scores = (probs * (grad_probs - weighted)).astype(BF)
                grad_value = mm_tn(probs_low, grad_out)
                grad_query = unstack_heads(mm(grad_scores, key), mask) * SCALE
                grad_key = mm_tn(grad_scores, query) * SCALE
                grad_qkv[part, rows, lane : lane + 128] = grad_query.astype(BF)
                grad_qkv[part, rows, half + lane : half + lane + 128] = grad_key.astype(BF)
                grad_qkv[part, rows, 2 * half + lane : 2 * half + lane + 128] = grad_value.astype(BF)
                picked = mm(grad_scores, picks_ref[...]).astype(BF)
                for head in range(GROUP):
                    tables[head] = tables[head] + mm(picks_t_ref[0:64, :], picked[head * PAD : (head + 1) * PAD])
            for head in range(GROUP):
                table_ref[group * GROUP + head] = tables[head][:56]
        for kind in range(3):
            lanes = slice(kind * half, (kind + 1) * half)
            grads = grad_qkv[part, :, lanes]
            outs[part][kind * half : (kind + 1) * half, :] = mm_tn(normed_ref[:, :half], grads).astype(BF)
            grad_normed = grad_normed + mm_nt(grads, qkv_weights[part][kind])
            if kind != 1:
                line = 3 + kind // 2
                small_outs[part][line : line + 1, :] = jnp.sum(grads.astype(F32), 0, keepdims=True)
    grad_input, grad_gain, grad_shift = norm_back(
        grad_normed, x_ref[...], small_ref[GAIN_ONE : GAIN_ONE + 1]
    )
    total = clear_padding(grad_mid + grad_input)
    scratch[...] = total
    if layer % 2 == 1:
        unroll_rows(scratch, grad_ref)
    else:
        flat[0:HALF, :] = scratch[0:HALF, 0:half]
        flat[HALF:IMAGE, :] = scratch[PAD : PAD + HALF, 0:half]
        grad_ref[...] = flat[0:IMAGE, :].astype(BF)
    out_bias = jnp.sum(near.astype(F32), 0, keepdims=True)
    for small in small_outs:
        small[0:1, :] = out_bias
        small[1:2, :] = grad_gain[:, :half]
        small[2:3, :] = grad_shift[:, :half]
        small[5:8, :] = jnp.zeros((3, half), F32)


DOWN_AT, UP_AT, QKV_AT, OUT_AT, TAIL_AT = 0, 1024, 2048, 2816, 3072
BLOCK_ROWS = 3200
RING = 8
PIECE = BLOCK_ROWS // (2 * RING)


def unpack_kernel(count, *refs):
    starts = refs[0]
    pieces = refs[1 : 1 + 2 * count]
    (qkv_ref, qv_ref, out_ref, out_bias_ref, up_ref, up_bias_ref, down_ref, down_bias_ref,
     gain_ref, shift_ref, table_ref, block) = refs[1 + 2 * count :]
    half = D // 2
    for layer in range(LAYERS):
        for number in range(count):
            piece = pieces[layer * count + number]
            size = piece.shape[0]
            at = pl.multiple_of(starts[number], 8)
            block[pl.ds(at, size), :] = piece[...].astype(F32)
        down_ref[layer] = block[DOWN_AT : DOWN_AT + FF // 2, :]
        for piece in range(4):
            up_ref[layer, :, piece * half : (piece + 1) * half] = block[
                UP_AT + piece * half : UP_AT + (piece + 1) * half, :
            ]
        for kind in range(3):
            qkv_ref[layer, kind] = block[QKV_AT + kind * half : QKV_AT + (kind + 1) * half, :]
        out_ref[layer] = block[OUT_AT : OUT_AT + half, :]
        tail = block[TAIL_AT : TAIL_AT + 24, :]
        down_bias_ref[layer : layer + 1, :] = tail[0:1]
        gain_ref[layer, 1:2, :] = tail[1:2]
        shift_ref[layer, 1:2, :] = tail[2:3]
        for piece in range(4):
            up_bias_ref[layer : layer + 1, piece * half : (piece + 1) * half] = tail[3 + piece : 4 + piece]
        out_bias_ref[layer : layer + 1, :] = tail[8:9]
        gain_ref[layer, 0:1, :] = tail[9:10]
        shift_ref[layer, 0:1, :] = tail[10:11]
        qv_ref[layer] = tail[11:13]
        table_ref[layer] = tail[16:24, :TABLE]


ANY = pl.BlockSpec(memory_space=pl.ANY)
VMEM = pl.BlockSpec(memory_space=pltpu.VMEM)
SMEM = pl.BlockSpec(memory_space=pltpu.SMEM)


def call(kernel, outs, scratch, args, micros, specs=None, out_specs=None, limit=40, aliases=None):
    return pl.pallas_call(
        kernel,
        out_shape=[jax.ShapeDtypeStruct(shape, kind) for shape, kind in outs],
        in_specs=specs or [VMEM] * len(args),
        out_specs=out_specs or [VMEM] * len(outs),
        scratch_shapes=scratch,
        input_output_aliases=aliases or {},
        compiler_params=pltpu.CompilerParams(vmem_limit_bytes=limit * 1024 * 1024),
        cost_estimate=pl.CostEstimate(flops=int(micros * 1.15e6), bytes_accessed=0, transcendentals=0),
    )(*args)


def layer_call(kernel, layer, outs, scratch, weights, args, micros, attn, behind=()):
    rooms, weight_copies, load = (
        (ATTN_ROOMS, ATTN_COPIES, attn_weights) if attn else (FFN_ROOMS, FFN_COPIES, ffn_weights)
    )

    def run(*refs):
        refs = list(refs)

        def take(number):
            taken = refs[:number]
            del refs[:number]
            return taken

        weight_refs, arg_refs, _, out_refs = take(len(weights)), take(len(args)), take(len(behind)), take(len(outs))
        weight_rooms, arg_rooms, others, (sems,) = take(len(rooms)), take(len(args)), take(len(scratch)), take(1)
        fetched = [
            whole_fetch(ref, room, sems, weight_copies + at) for at, (ref, room) in enumerate(zip(arg_refs, arg_rooms))
        ]
        loaded = load(layer, weight_refs, weight_rooms, sems, 0)
        if kernel in FORWARD:
            pending = fetched[:2] + loaded[0] + fetched[2:] + loaded[1]
        else:
            pending = fetched[:1] + loaded[1] + fetched[1:] + loaded[0]
        for item in pending:
            item.start()
        kernel(layer, loaded, *fetched, *out_refs, *others)
        for item in pending:
            item.ready()

    spaces = (
        [pltpu.VMEM(shape, kind) for shape, kind in rooms]
        + [pltpu.VMEM(a.shape, a.dtype) for a in args]
        + scratch
        + [pltpu.SemaphoreType.DMA((weight_copies + len(args),))]
    )
    operands = [*weights, *args, *behind]
    return call(run, outs, spaces, operands, micros, [ANY] * len(operands))


def turn_call(layer, forward, blocks, wholes, named, outs):
    half = D // 2
    weights = [*wholes[2:], *blocks, *wholes[:2], *blocks]
    names, args = list(named), list(named.values())
    inner = {"normed_two": ((ROWS, D), BF), "slope": ((ROWS, FF), BF), "hidden": ((ROWS, FF), BF)}
    inner = inner if forward else {}
    spaces = [
        ((ROWS, D), F32), ((200, half), F32), ((ROWS, D), F32), ((2, ROWS, 3 * half), BF), *inner.values(),
    ]

    def run(*refs):
        refs = list(refs)

        def take(number):
            taken = refs[:number]
            del refs[:number]
            return taken

        weight_refs, arg_refs, out_refs = take(14), take(len(args)), take(len(outs))
        ffn_rooms, attn_rooms, arg_rooms = take(4), take(4), take(len(args))
        scratch, flat, grad_mid, grad_qkv = take(4)
        made = dict(zip(inner, take(len(inner))))
        (sems,) = take(1)
        ups, downs = ffn_weights(layer, weight_refs[:7], ffn_rooms, sems, 0)
        qkvs, mixes = attn_weights(layer, weight_refs[7:], attn_rooms, sems, FFN_COPIES)
        got = {
            name: whole_fetch(ref, room, sems, FFN_COPIES + ATTN_COPIES + at)
            for at, (name, ref, room) in enumerate(zip(names, arg_refs, arg_rooms))
        }
        early = ("middle", "small") if forward else ("grad", "slope", "hidden")
        late = [got[name] for name in names if name not in early]
        early = [got[name] for name in early]
        if forward:
            pending = [*early, *ups, *downs, *late, *mixes, *qkvs]
        else:
            pending = [early[0], downs[0], *early[1:], got["normed_two"], ups[0], downs[1], ups[1]]
            pending += [item for item in late if item is not got["normed_two"]] + [*mixes, *qkvs]
        for item in pending:
            item.start()
        got.update(made)
        outputs = list(out_refs)
        if forward:
            ffn_fwd_kernel(
                layer, (ups, downs), got["middle"], got["small"], outputs.pop(0), got["normed_two"], got["slope"],
                got["hidden"], scratch, flat,
            )
        ffn_bwd_kernel(
            layer, (ups, downs), got["grad"], got["slope"], got["hidden"], got["normed_two"], got["small"],
            got["middle"], grad_mid, *outputs[:4],
        )
        attn_bwd_kernel(
            layer, (qkvs, mixes), grad_mid, got["att"], got["qkv"], got["probs"], got["picks"], got["picks_t"],
            got["normed_one"], got["small"], got["x"], *outputs[4:], grad_qkv, scratch, flat,
        )
        for item in pending:
            item.ready()

    scratch = (
        [pltpu.VMEM(shape, kind) for shape, kind in FFN_ROOMS + ATTN_ROOMS]
        + [pltpu.VMEM(a.shape, a.dtype) for a in args]
        + [pltpu.VMEM(shape, kind) for shape, kind in spaces]
        + [pltpu.SemaphoreType.DMA((FFN_COPIES + ATTN_COPIES + len(args),))]
    )
    operands = [*weights, *args]
    return call(run, outs, scratch, operands, 12, [ANY] * len(operands))


FORWARD = (attn_fwd_kernel, ffn_fwd_kernel)


def part_of(kernel, layer):
    def run(*refs):
        return kernel(layer, *refs)

    return run


def ring_perms():
    order = [0, 2, 4, 6, 7, 5, 3, 1]
    onward = [(order[i], order[(i + 1) % RING]) for i in range(RING)]
    return onward, [(b, a) for a, b in onward]


def ring_sum(pieces, place, one, two):
    onward, back = ring_perms()
    for step in range(RING - 1):
        one, two = lax.ppermute(one, "dp", onward), lax.ppermute(two, "dp", back)
        one = one + pick(pieces, (place - 2 - step) % RING)
        two = two + pick(pieces, RING + (place + 2 + step) % RING)
    return ring_gather(one, two)


def pick(values, index):
    return lax.dynamic_index_in_dim(values, index, 0, keepdims=False)


def ring_gather(one, two):
    onward, back = ring_perms()
    pieces = [one, two]
    for _ in range(RING - 1):
        one, two = lax.ppermute(one, "dp", onward), lax.ppermute(two, "dp", back)
        pieces += [one, two]
    return pieces


def piece_starts(place):
    starts = []
    for step in range(RING):
        starts += [((place - step) % RING) * PIECE, (RING + (place + step) % RING) * PIECE]
    return jnp.stack(starts).astype(jnp.int32)


def on_device(
    ring, tokens, cotangent, qkv_weight, qv_bias, out_weight, out_bias, up_weight, up_bias,
    down_weight, down_bias, norm_gain, norm_shift, bias_table, index_map, region_ids,
):
    half, quarter = D // 2, D // 4
    device = lax.axis_index("dp")
    parity = device % 2
    neighbours = [(i, i ^ 1) for i in range(lax.axis_size("dp"))]

    wholes = [qkv_weight.transpose(0, 2, 1, 3), out_weight, up_weight, down_weight]
    parity_ref = parity.astype(jnp.int32).reshape(1)
    (misc_row,) = call(
        misc_kernel, [((32, half), BF)], [], [qv_bias, up_bias, bias_table.transpose(0, 2, 1)], 1
    )
    row_far = swap(misc_row, "row")
    sources = [*wholes, tokens, cotangent, norm_gain, norm_shift, out_bias, down_bias]
    pack_outs = [((MISC_ROWS, half), BF), ((3 * D, half), BF), ((3 * D, half), BF)]
    packs = [None, None]
    packs[0], packs[1], whole = call(
        pack_kernel,
        [((MISC_ROWS + 3 * D, half), BF), ((3 * D, half), BF), ((LAYERS * TAIL_AT, half), BF)],
        [pltpu.VMEM(value.shape[1:], value.dtype) for value in wholes] * LAYERS
        + [pltpu.VMEM(shape, kind) for shape, kind in pack_outs]
        + [pltpu.SemaphoreType.DMA((8,)), pltpu.SemaphoreType.DMA((21,))],
        [parity_ref, *sources, misc_row],
        3,
        [SMEM] + [ANY] * 4 + [VMEM] * 6 + [ANY],
        [ANY] * 3,
        limit=60,
    )
    whole_row = swap(whole, "row")
    from_col = [swap(pack, "col") for pack in packs]
    misc, misc_far = packs[0][:MISC_ROWS], from_col[0][:MISC_ROWS]
    from_col[0] = from_col[0][MISC_ROWS:]

    def block(pack, token):
        from_dp = lax.ppermute(pack, "dp", neighbours)
        from_dp = after(from_dp, token)
        return [pack, from_dp, whole_row, swap(pack, "row"), swap(from_dp, "row")]

    picks = np.stack([position_one_hot(layer) for layer in range(LAYERS)])
    picks_t = [jnp.asarray(pick.T, BF) for pick in picks]
    picks_all = jnp.asarray(picks, BF)
    picks = [jnp.asarray(pick, BF) for pick in picks]
    masks = [mask_of(layer, region_ids) for layer in range(LAYERS)]
    wide = ((ROWS, D), F32)
    x, grad, *rest = call(
        prep_kernel,
        [wide, wide, ((16, D), F32), ((16, D), F32), ((HEADS, PAD, PAD), F32), ((HEADS, PAD, PAD), F32)],
        [
            pltpu.VMEM((64, LAYERS * HEADS, PAD), F32), pltpu.VMEM((56, PAD), jnp.int32),
            pltpu.VMEM((208, D), F32),
        ],
        [parity_ref, misc, misc_far, misc_row, row_far, index_map, picks_all],
        4,
        [SMEM] + [VMEM] * 6,
    )
    smalls, bias = rest[:2], rest[2:4]
    blocks = [block(from_col[0], x)]

    image = ((IMAGE, half), BF)
    saved = []
    for layer in range(LAYERS):
        middle, normed_one, qkv, probs, att = layer_call(
            attn_fwd_kernel,
            layer,
            [
                wide, ((ROWS, D), BF), ((2, ROWS, 3 * half), BF),
                ((2, GROUPS, STACK, PAD), BF), ((ROWS, D), BF),
            ],
            [],
            [*wholes[:2], *blocks[layer]],
            [x, smalls[layer], bias[layer], masks[layer]],
            4,
            True,
            [from_col[1]] if layer == 0 else [],
        )
        if layer == LAYERS - 1:
            saved.append((x, middle, normed_one, qkv, probs, att, None, None, None))
            break
        result, normed_two, pre, hidden = layer_call(
            ffn_fwd_kernel,
            layer,
            [wide, ((ROWS, D), BF), ((ROWS, FF), BF), ((ROWS, FF), BF)],
            [pltpu.VMEM((ROWS, D), F32), pltpu.VMEM((200, half), F32)],
            [*wholes[2:], *blocks[layer]],
            [middle, smalls[layer]],
            4,
            False,
        )
        if layer == 0:
            blocks.append(block(from_col[1], result))
        saved.append((x, middle, normed_one, qkv, probs, att, normed_two, pre, hidden))
        x = result

    heads = HEADS // 2
    one_hot = (index_map[:, :, None] == jnp.arange(256, dtype=jnp.int32)).astype(F32).reshape(SPAN * SPAN, 256)
    sums = [None] * LAYERS
    place = jnp.where(parity == 0, device // 2, RING - 1 - device // 2)
    place_ref = place.astype(jnp.int32).reshape(1)
    for layer in reversed(range(LAYERS)):
        x_in, middle, normed_one, qkv, probs, att, normed_two, pre, hidden = saved[layer]
        small_shape = ((8, half), F32)
        named = {
            "middle": middle, "small": smalls[layer], "grad": grad, "slope": pre, "hidden": hidden,
            "normed_two": normed_two, "att": att, "qkv": qkv, "probs": probs, "picks": picks[layer],
            "picks_t": picks_t[layer], "normed_one": normed_one, "x": x_in,
        }
        named = {name: value for name, value in named.items() if value is not None}
        last = layer == LAYERS - 1
        results = turn_call(
            layer,
            last,
            blocks[layer],
            wholes,
            named,
            [image] * last
            + [
                ((FF, half), BF), ((FF, half), BF), small_shape, small_shape,
                wide if layer > 0 else image, ((2 * D, half), BF), ((2 * D, half), BF), small_shape, small_shape,
                ((HEADS, 56, PAD), F32),
            ],
        )
        if last:
            output, *results = results
        ffn_keep, ffn_send, small_keep, small_send, grad, keep, send, att_keep, att_send, counts = results
        ffn_got = swap(ffn_send, "row")
        got = swap(send, "row")
        table = jnp.dot(counts[:, :SPAN, :SPAN].reshape(HEADS, SPAN * SPAN), one_hot, precision=HIGH)
        tail_keep = jnp.concatenate([small_keep, att_keep, table[:heads]], 0)
        tail_send = jnp.concatenate([small_send, att_send, table[heads:]], 0)
        pieces, one, two = call(
            combine_kernel,
            [((2 * RING, PIECE, half), BF), ((PIECE, half), BF), ((PIECE, half), BF)],
            [pltpu.VMEM((BLOCK_ROWS, half), F32)],
            [place_ref, ffn_keep, ffn_got, keep, got, tail_keep, swap(tail_send, "row")],
            2,
            [SMEM] + [VMEM] * 6,
            limit=24,
        )
        if ring:
            sums[layer] = ring_sum(pieces, place, one, two)
        else:
            sums[layer] = [lax.psum(pieces.reshape(BLOCK_ROWS, half), "dp")]
    input_grad = grad

    count = len(sums[0])
    starts = piece_starts(place) if ring else jnp.zeros((1,), jnp.int32)
    qkv, qv, outw, outb, up, upb, down, downb, gain, shift, table = call(
        part_of(unpack_kernel, count),
        [
            ((LAYERS, 3, half, half), F32), ((LAYERS, 2, half), F32), ((LAYERS, half, half), F32),
            ((LAYERS, half), F32), ((LAYERS, half, FF // 2), F32), ((LAYERS, FF // 2), F32),
            ((LAYERS, FF // 2, half), F32), ((LAYERS, half), F32), ((LAYERS, 2, half), F32),
            ((LAYERS, 2, half), F32), ((LAYERS, heads, TABLE), F32),
        ],
        [pltpu.VMEM((BLOCK_ROWS, half), F32)],
        [starts, *sums[0], *sums[1]],
        4,
        [SMEM] + [VMEM] * (2 * count),
    )
    return (
        output, input_grad, qkv.transpose(0, 2, 1, 3), qv, outw, outb, up, upb, down, downb, gain, shift,
        table.transpose(0, 2, 1),
    )


def solution(mesh):
    in_specs = (
        P(("dp", "row"), "col"),
        P(("dp", "row"), "col"),
        P(None, "col", None, "row"),
        P(None, None, "row"),
        P(None, "row", "col"),
        P(None, "col"),
        P(None, "col", "row"),
        P(None, "row"),
        P(None, "row", "col"),
        P(None, "col"),
        P(None, None, "col"),
        P(None, None, "col"),
        P(None, None, "row"),
        P(),
        P(),
    )
    out_specs = (
        P(("dp", "row"), "col"),
        P(("dp", "row"), "col"),
        P(None, "col", None, "row"),
        P(None, None, "row"),
        P(None, "row", "col"),
        P(None, "col"),
        P(None, "col", "row"),
        P(None, "row"),
        P(None, "row", "col"),
        P(None, "col"),
        P(None, None, "col"),
        P(None, None, "col"),
        P(None, None, "row"),
    )
    ring = mesh.shape["dp"] == RING
    return jax.shard_map(
        part_of(on_device, ring), mesh=mesh, in_specs=in_specs, out_specs=out_specs, check_vma=False
    )
```

```python
import math

import jax
import jax.numpy as jnp
import numpy as np
from jax import lax
from jax.experimental import pallas as pl
from jax.experimental.pallas import tpu as pltpu
from jax.sharding import PartitionSpec as P

D = 512
HEADS = 16
HEAD_DIM = 32
FF = 2048
GRID = 14
WINDOW = 7
SHIFT = 3
TABLE = 169
LAYERS = 2
SPAN = WINDOW * WINDOW
IMAGE = GRID * GRID

EPS = 1e-05
NEG = -1000000000.0
HIGH = lax.Precision.HIGHEST
SCALE = 1.0 / math.sqrt(HEAD_DIM)

HALF = IMAGE // 2
PAD = 128
ROWS = 2 * PAD
ROLL = SHIFT * GRID
GROUP = 128 // HEAD_DIM
GROUPS = HEADS // GROUP
STACK = GROUP * PAD
CHUNK = 512
BF = jnp.bfloat16
F32 = jnp.float32


def swap(values, axis):
    return lax.ppermute(values, axis, [(0, 1), (1, 0)])


def mm(left, right):
    return lax.dot_general(left, right, (((1,), (0,)), ((), ())), preferred_element_type=F32)


def mm_nt(left, right):
    return lax.dot_general(left, right, (((1,), (1,)), ((), ())), preferred_element_type=F32)


def mm_tn(left, right):
    return lax.dot_general(left, right, (((0,), (0,)), ((), ())), preferred_element_type=F32)


def token_positions(layer):
    token = np.arange(HALF)
    line, column = token // GRID, token % GRID
    if layer % 2 == 1:
        column = (column - SHIFT) % GRID
    return line * WINDOW + column % WINDOW, column // WINDOW, line * GRID + column


def position_one_hot(layer):
    position, _, _ = token_positions(layer)
    picks = np.zeros((PAD, PAD), np.float32)
    picks[np.arange(HALF), position] = 1.0
    return picks


def mask_of(layer, region_ids):
    _, window, place = token_positions(layer)
    same = np.zeros((PAD, PAD), bool)
    same[:HALF, :HALF] = window[:, None] == window[None, :]
    same[HALF:, :HALF] = True
    allowed = jnp.broadcast_to(jnp.asarray(same)[None], (2, PAD, PAD))
    if layer % 2 == 1:
        ids = jnp.roll(region_ids.reshape(2, WINDOW, GRID), SHIFT, 2).reshape(2, HALF)
        ids = jnp.pad(ids, ((0, 0), (0, PAD - HALF)), constant_values=-1)
        pad_row = jnp.asarray(np.arange(PAD) >= HALF)[None, :, None]
        allowed = allowed & ((ids[:, :, None] == ids[:, None, :]) | pad_row)
    return jnp.where(allowed, 0.0, NEG).astype(F32)


def head_mask():
    lane = lax.broadcasted_iota(jnp.int32, (STACK, PAD), 1) // HEAD_DIM
    row = lax.broadcasted_iota(jnp.int32, (STACK, PAD), 0) // PAD
    return lane == row


def stack_heads(values, mask):
    tiled = jnp.concatenate([values] * GROUP, axis=0)
    return jnp.where(mask, tiled, jnp.zeros_like(tiled))


def unstack_heads(values, mask):
    kept = jnp.where(mask, values, 0.0)
    total = kept[0:PAD]
    for head in range(1, GROUP):
        total = total + kept[head * PAD : (head + 1) * PAD]
    return total


def norm_parts(values):
    average = jnp.mean(values, -1, keepdims=True)
    centred = values - average
    variance = jnp.mean(centred * centred, -1, keepdims=True)
    inverse = lax.rsqrt(variance + EPS)
    return centred * inverse, inverse


def norm_back(grad_normed, values, gain):
    xhat, inverse = norm_parts(values)
    scaled = grad_normed * gain
    mean_one = jnp.mean(scaled, -1, keepdims=True)
    mean_two = jnp.mean(scaled * xhat, -1, keepdims=True)
    grad_input = inverse * (scaled - mean_one - xhat * mean_two)
    return grad_input, jnp.sum(grad_normed * xhat, 0, keepdims=True), jnp.sum(grad_normed, 0, keepdims=True)


def split_halves(values):
    return values[:, : D // 2], values[:, D // 2 :]


def gelu_and_slope(values):
    below = 0.5 * (1.0 + lax.erf(values * (1.0 / math.sqrt(2.0))))
    density = jnp.exp(-0.5 * values * values) * (1.0 / math.sqrt(2.0 * math.pi))
    return values * below, below + values * density


TABLE_ROWS = 176

GAIN_ONE, GAIN_TWO, SHIFT_ONE, SHIFT_TWO, OUT_BIAS, DOWN_BIAS, Q_BIAS, V_BIAS, UP_BIAS = 0, 1, 2, 3, 4, 5, 6, 7, 8


def prep_kernel(
    parity_ref, misc_ref, misc_far, row_ref, row_far, index_ref, picks_ref,
    x_ref, grad_ref, small_zero, small_one, bias_zero, bias_one, pairs_ref, index_pad, flat,
):
    half, quarter = D // 2, D // 4
    even = parity_ref[0] == 0

    def ordered(values):
        low, high = values[:, :quarter], values[:, quarter:]
        return jnp.where(even, low, high), jnp.where(even, high, low)

    def lay_out(at):
        first, second = ordered(misc_far[at : at + 208, :].astype(F32))
        flat[:, 0:half] = misc_ref[at : at + 208, :].astype(F32)
        flat[:, half : half + quarter] = first
        flat[:, half + quarter :] = second

    x_ref[...] = jnp.zeros_like(x_ref)
    grad_ref[...] = jnp.zeros_like(grad_ref)
    lay_out(TOKENS_AT)
    x_ref[0:HALF, :] = flat[0:HALF, :]
    x_ref[PAD : PAD + HALF, :] = flat[HALF:IMAGE, :]
    lay_out(COT_AT)
    rest = HALF - ROLL
    grad_ref[0:HALF, :] = flat[ROLL : ROLL + HALF, :]
    grad_ref[PAD : PAD + rest, :] = flat[ROLL + HALF : IMAGE, :]
    grad_ref[PAD + rest : PAD + HALF, :] = flat[0:ROLL, :]

    near = misc_ref[SMALL_AT:MISC_ROWS, :].astype(F32)
    far_first, far_second = ordered(misc_far[SMALL_AT:MISC_ROWS, :].astype(F32))
    rows_near, rows_far = row_ref[...].astype(F32), row_far[...].astype(F32)
    for layer, small in enumerate((small_zero, small_one)):
        small[...] = jnp.zeros_like(small)

        def features(row, source):
            small[row : row + 1, 0:half] = near[source : source + 1]
            small[row : row + 1, half : half + quarter] = far_first[source : source + 1]
            small[row : row + 1, half + quarter :] = far_second[source : source + 1]

        for which in range(2):
            features(GAIN_ONE + which, 2 * layer + which)
            features(SHIFT_ONE + which, 4 + 2 * layer + which)
            for part, source in enumerate((rows_near, rows_far)):
                lanes = slice(part * half, (part + 1) * half)
                at = 2 * layer + which
                small[Q_BIAS + which : Q_BIAS + which + 1, lanes] = source[at : at + 1]
                line = UP_BIAS + 2 * part + which
                for piece in range(2):
                    at = 4 + 2 * (2 * which + piece) + layer
                    small[line : line + 1, piece * half : (piece + 1) * half] = source[at : at + 1]
        features(OUT_BIAS, 8 + layer)
        features(DOWN_BIAS, 10 + layer)

    heads = HEADS // 2
    tables = []
    for layer in range(LAYERS):
        for source in (rows_near, rows_far):
            tables.append(source[16 + layer * heads : 16 + (layer + 1) * heads, :TABLE_ROWS])
    table = jnp.concatenate(tables, 0).astype(BF)
    index_pad[...] = jnp.full(index_pad.shape, -1, jnp.int32)
    index_pad[0:SPAN, 0:SPAN] = index_ref[...]
    pairs_ref[SPAN:64] = jnp.zeros((64 - SPAN, LAYERS * HEADS, PAD), F32)
    for position in range(SPAN):
        wanted = index_pad[position : position + 1, :]
        hot = (lax.broadcasted_iota(jnp.int32, (TABLE_ROWS, PAD), 0) == wanted).astype(F32).astype(BF)
        pairs_ref[position] = mm(table, hot)
    for layer, bias_ref in enumerate((bias_zero, bias_one)):
        picks = picks_ref[layer]
        for head in range(HEADS):
            bias = pairs_ref[:, layer * HEADS + head, :]
            spread = mm(picks[:, :64], bias.astype(BF)).astype(BF)
            bias_ref[head] = mm_nt(spread, picks)


class Fetch:
    def __init__(self, copies, ref):
        self.copies, self.ref, self.waiting = copies, ref, True

    def start(self):
        for copy in self.copies:
            copy.start()

    def ready(self):
        if self.waiting:
            self.waiting = False
            for copy in self.copies:
                copy.wait()
        return self.ref

    def __getitem__(self, index):
        return self.ready()[index]


def whole_fetch(source, room, sems, at):
    return Fetch([pltpu.make_async_copy(source, room, sems.at[at])], room)


def attn_weights(layer, sources, rooms, sems, at):
    half, quarter = D // 2, D // 4
    qkv, out, from_col, from_dp, whole_row, from_col_row, from_dp_row = sources
    qkvs, outs = [], []
    whole_at = layer * TAIL_AT
    for part, packs in enumerate(((from_col, from_dp), (from_col_row, from_dp_row))):
        room_qkv, room_out = rooms[2 * part], rooms[2 * part + 1]
        pairs, pairs_out = [], []
        for kind in range(3):
            lines = slice(whole_at + QKV_AT + kind * half, whole_at + QKV_AT + (kind + 1) * half)
            source = qkv.at[layer, kind] if part == 0 else whole_row.at[lines, :]
            pairs.append((source, room_qkv.at[kind, 0:half, :]))
        source = out.at[layer] if part == 0 else whole_row.at[whole_at + OUT_AT : whole_at + TAIL_AT, :]
        pairs_out.append((source, room_out.at[:, 0:half]))
        for slot, pack in enumerate(packs):
            first = half + slot * quarter
            for kind in range(3):
                pairs.append(
                    (
                        pack.at[kind * quarter : (kind + 1) * quarter, :],
                        room_qkv.at[kind, first : first + quarter, :],
                    )
                )
            for side in range(2):
                lanes = slice(side * quarter, (side + 1) * quarter)
                pairs_out.append((pack.at[3 * quarter : 4 * quarter, lanes], room_out.at[lanes, first : first + quarter]))
        for found, room, list_of in ((pairs, room_qkv, qkvs), (pairs_out, room_out, outs)):
            copies = []
            for source, target in found:
                copies.append(pltpu.make_async_copy(source, target, sems.at[at]))
                at += 1
            list_of.append(Fetch(copies, room))
    return qkvs, outs


ATTN_COPIES = 2 * (9 + 5)
ATTN_ROOMS = [((3, D, D // 2), BF), ((D // 2, D), BF)] * 2


def ffn_weights(layer, sources, rooms, sems, at):
    half, quarter, wide = D // 2, D // 4, FF // 4
    up, down, from_col, from_dp, whole_row, from_col_row, from_dp_row = sources
    ups, downs = [], []
    whole_at = layer * TAIL_AT
    for part, packs in enumerate(((from_col, from_dp), (from_col_row, from_dp_row))):
        room_up, room_down = rooms[2 * part], rooms[2 * part + 1]
        pairs, pairs_down = [], []
        for piece in range(4):
            lanes = slice(piece * half, (piece + 1) * half)
            lines = slice(whole_at + UP_AT + piece * half, whole_at + UP_AT + (piece + 1) * half)
            source = up.at[layer, :, lanes] if part == 0 else whole_row.at[lines, :]
            pairs.append((source, room_up.at[0:half, lanes]))
        source = down.at[layer] if part == 0 else whole_row.at[whole_at + DOWN_AT : whole_at + UP_AT, :]
        pairs_down.append((source, room_down.at[:, 0:half]))
        for slot, pack in enumerate(packs):
            first = half + slot * quarter
            for piece in range(4):
                lanes = slice(piece * half, (piece + 1) * half)
                pairs.append(
                    (
                        pack.at[D + piece * quarter : D + (piece + 1) * quarter, :],
                        room_up.at[first : first + quarter, lanes],
                    )
                )
            for side in range(2):
                lanes = slice(side * quarter, (side + 1) * quarter)
                pairs_down.append(
                    (
                        pack.at[2 * D :, lanes],
                        room_down.at[side * wide : (side + 1) * wide, first : first + quarter],
                    )
                )
        for found, room, list_of in ((pairs, room_up, ups), (pairs_down, room_down, downs)):
            copies = []
            for source, target in found:
                copies.append(pltpu.make_async_copy(source, target, sems.at[at]))
                at += 1
            list_of.append(Fetch(copies, room))
    return ups, downs


FFN_COPIES = 2 * (12 + 5)
FFN_ROOMS = [((D, FF // 2), BF), ((FF // 2, D), BF)] * 2


def misc_kernel(qv_bias, up_bias, table, _, misc_row):
    half = D // 2
    rows = [qv_bias[0], qv_bias[1]] + [up_bias[:, piece * half : (piece + 1) * half] for piece in range(4)]
    rows = [row.astype(F32) for row in rows] + [jnp.zeros((4, half), F32)]
    misc_row[0:16, :] = jnp.concatenate(rows, 0).astype(BF)
    tables = jnp.concatenate([table[layer].astype(F32) for layer in range(LAYERS)], 0)
    misc_row[16:32, :] = jnp.pad(tables, ((0, 0), (0, half - TABLE))).astype(BF)


def pack_kernel(
    parity_ref, qkv, out, up, down, tokens, cot, gain, shift, out_bias, down_bias,
    pack_zero, pack_one, whole, *rest,
):
    rooms, results, (in_sems, out_sems) = rest[:8], rest[8:11], rest[11:]
    half, quarter = D // 2, D // 4
    even = parity_ref[0] == 0
    fetched = []
    for layer in range(LAYERS):
        for number, source in enumerate((qkv, out, up, down)):
            at = 4 * layer + number
            fetched.append(whole_fetch(source.at[layer], rooms[at], in_sems, at))
    for item in fetched:
        item.start()
    sent = []

    def send(source, target):
        copy = pltpu.make_async_copy(source, target, out_sems.at[len(sent)])
        copy.start()
        sent.append(copy)

    misc = results[0]
    misc[...] = jnp.zeros_like(misc)
    misc[TOKENS_AT : TOKENS_AT + IMAGE, :] = tokens[...]
    misc[COT_AT : COT_AT + IMAGE, :] = cot[...]
    rows = [gain[0], gain[1], shift[0], shift[1], out_bias[...], down_bias[...]]
    misc[SMALL_AT : SMALL_AT + 12, :] = jnp.concatenate([row.astype(F32) for row in rows], 0).astype(BF)
    send(misc, pack_zero.at[0:MISC_ROWS, :])
    for layer in range(LAYERS):
        pack = results[1 + layer]
        at = layer * TAIL_AT
        qkv_l, out_l, up_l, down_l = [item.ready() for item in fetched[4 * layer : 4 * layer + 4]]
        for kind in range(3):
            pack[kind * quarter : (kind + 1) * quarter, :] = jnp.where(
                even, qkv_l[kind, 0:quarter, :], qkv_l[kind, quarter:half, :]
            )
        chosen = jnp.where(even, out_l[:, 0:quarter], out_l[:, quarter:half])
        pack[3 * quarter : 4 * quarter, 0:quarter] = chosen[0:quarter]
        pack[3 * quarter : 4 * quarter, quarter:half] = chosen[quarter:half]
        chosen = jnp.where(even, up_l[0:quarter, :], up_l[quarter:half, :])
        for piece in range(4):
            lines = slice(D + piece * quarter, D + (piece + 1) * quarter)
            pack[lines, :] = chosen[:, piece * half : (piece + 1) * half]
        chosen = jnp.where(even, down_l[:, 0:quarter], down_l[:, quarter:half])
        pack[2 * D :, 0:quarter] = chosen[0 : FF // 4]
        pack[2 * D :, quarter:half] = chosen[FF // 4 :]
        send(pack, pack_zero.at[MISC_ROWS:, :] if layer == 0 else pack_one)
        send(down_l, whole.at[at + DOWN_AT : at + UP_AT, :])
        for piece in range(4):
            lines = slice(at + UP_AT + piece * half, at + UP_AT + (piece + 1) * half)
            send(up_l.at[:, piece * half : (piece + 1) * half], whole.at[lines, :])
        for kind in range(3):
            send(qkv_l.at[kind], whole.at[at + QKV_AT + kind * half : at + QKV_AT + (kind + 1) * half, :])
        send(out_l, whole.at[at + OUT_AT : at + TAIL_AT, :])
    for copy in sent:
        copy.wait()


def after_kernel(*refs):
    pass


def after(value, token):
    (result,) = call(
        after_kernel, [(value.shape, value.dtype)], [], [value, token], 0, [ANY] * 2, [ANY], limit=1, aliases={0: 0}
    )
    return result


TOKENS_AT, COT_AT, SMALL_AT, MISC_ROWS = 0, 208, 416, 432


def combine_kernel(place_ref, ffn_keep, ffn_got, keep, got, tail_keep, tail_got, *rest):
    pieces_ref, one_ref, two_ref, flat = rest[-4:]
    flat[0:FF, :] = ffn_keep[...].astype(F32) + ffn_got[...].astype(F32)
    flat[FF : FF + 2 * D, :] = keep[...].astype(F32) + got[...].astype(F32)
    flat[TAIL_AT:, :] = jnp.zeros((BLOCK_ROWS - TAIL_AT, D // 2), F32)
    flat[TAIL_AT : TAIL_AT + 24, :] = tail_keep[...] + tail_got[...]
    for number in range(2 * RING):
        pieces_ref[number] = flat[number * PIECE : (number + 1) * PIECE, :].astype(BF)
    place = place_ref[0]
    one_ref[...] = pieces_ref[lax.rem(place + RING - 1, RING)]
    two_ref[...] = pieces_ref[RING + lax.rem(place + 1, RING)]


def attn_fwd_kernel(
    layer, weights, x_ref, small_ref, bias_ref, mask_ref, mid_ref, normed_ref, qkv_ref, probs_ref, att_ref,
):
    qkv_weights, out_weights = weights
    x = x_ref[...]
    xhat, _ = norm_parts(x)
    normed = (
        xhat * small_ref[GAIN_ONE : GAIN_ONE + 1] + small_ref[SHIFT_ONE : SHIFT_ONE + 1]
    ).astype(BF)
    normed_ref[...] = normed
    half = D // 2
    for part in range(2):
        lanes = slice(part * half, (part + 1) * half)
        for kind in range(3):
            projected = mm(normed, qkv_weights[part][kind])
            if kind != 1:
                row = Q_BIAS if kind == 0 else V_BIAS
                projected = projected + small_ref[row : row + 1, lanes]
            qkv_ref[part, :, kind * half : (kind + 1) * half] = projected.astype(BF)
    mask = head_mask()
    for group in range(GROUPS):
        part, lane = group // 2, (group % 2) * 128
        bias = bias_ref[group * GROUP : (group + 1) * GROUP]
        for side in range(2):
            rows = slice(side * PAD, (side + 1) * PAD)
            query = qkv_ref[part, rows, lane : lane + 128]
            key = qkv_ref[part, rows, half + lane : half + lane + 128]
            value = qkv_ref[part, rows, 2 * half + lane : 2 * half + lane + 128]
            scores = mm_nt(stack_heads(query, mask), key).reshape(GROUP, PAD, PAD) * SCALE
            scores = scores + (bias + mask_ref[side][None])
            peak = jnp.max(scores, -1, keepdims=True)
            expos = jnp.exp(scores - peak)
            totals = jnp.sum(expos, -1, keepdims=True)
            probs = (expos / totals).astype(BF).reshape(STACK, PAD)
            probs_ref[side, group] = probs
            attended = unstack_heads(mm(probs, value), mask)
            att_ref[rows, group * 128 : (group + 1) * 128] = attended.astype(BF)
    first, second = split_halves(att_ref[...])
    mixed = mm(first, out_weights[0][...]) + mm(second, out_weights[1][...])
    mid_ref[...] = x + mixed + small_ref[OUT_BIAS : OUT_BIAS + 1]


def roll_rows(values_ref, result_ref):
    rest = HALF - ROLL
    result_ref[...] = jnp.zeros_like(result_ref)
    for side in range(2):
        here, there = side * PAD, (1 - side) * PAD
        result_ref[here : here + rest, :] = values_ref[here + ROLL : here + HALF, :]
        result_ref[here + rest : here + HALF, :] = values_ref[there : there + ROLL, :]


def unroll_rows(values_ref, result_ref):
    rest = HALF - ROLL
    result_ref[...] = jnp.zeros_like(result_ref)
    for side in range(2):
        here, there = side * PAD, (1 - side) * PAD
        result_ref[here + ROLL : here + HALF, :] = values_ref[here : here + rest, :]
        result_ref[here : here + ROLL, :] = values_ref[there + rest : there + HALF, :]


def clear_padding(values):
    row = lax.broadcasted_iota(jnp.int32, values.shape, 0) % PAD
    return jnp.where(row < HALF, values, 0.0)


def ffn_fwd_kernel(
    layer, weights, mid_ref, small_ref, x_ref, normed_ref, slope_ref, hidden_ref, scratch, flat,
):
    up_weights, down_weights = weights
    half = D // 2
    middle = mid_ref[...]
    xhat, _ = norm_parts(middle)
    normed = (
        xhat * small_ref[GAIN_TWO : GAIN_TWO + 1] + small_ref[SHIFT_TWO : SHIFT_TWO + 1]
    ).astype(BF)
    normed_ref[...] = normed
    total = jnp.zeros((ROWS, D), F32)
    per_part = FF // 2 // CHUNK
    for chunk in range(FF // CHUNK):
        part, at = chunk // per_part, (chunk % per_part) * CHUNK
        pre = mm(normed, up_weights[part][:, at : at + CHUNK]) + small_ref[UP_BIAS + chunk : UP_BIAS + chunk + 1]
        hidden, slope = gelu_and_slope(pre)
        hidden = hidden.astype(BF)
        slope_ref[:, chunk * CHUNK : (chunk + 1) * CHUNK] = slope.astype(BF)
        hidden_ref[:, chunk * CHUNK : (chunk + 1) * CHUNK] = hidden
        total = total + mm(hidden, down_weights[part][at : at + CHUNK, :])
    result = middle + total + small_ref[DOWN_BIAS : DOWN_BIAS + 1]
    scratch[...] = result
    if layer % 2 == 0:
        roll_rows(scratch, x_ref)
    else:
        rest = HALF - ROLL
        flat[ROLL : ROLL + HALF, :] = scratch[0:HALF, 0:half]
        flat[ROLL + HALF : IMAGE, :] = scratch[PAD : PAD + rest, 0:half]
        flat[0:ROLL, :] = scratch[PAD + rest : PAD + HALF, 0:half]
        x_ref[...] = flat[0:IMAGE, :].astype(BF)


def ffn_bwd_kernel(
    layer, weights, grad_ref, slope_ref, hidden_ref, normed_ref, small_ref, mid_ref,
    grad_mid_ref, keep_ref, send_ref, small_keep_ref, small_send_ref,
):
    up_weights, down_weights = weights
    half = D // 2
    grad = grad_ref[...]
    grad_down = grad.astype(BF)
    near = grad_down[:, :half]
    per_part = FF // 2 // CHUNK
    outs = (keep_ref, send_ref)
    small_outs = (small_keep_ref, small_send_ref)
    grad_normed = jnp.zeros((ROWS, D), F32)
    for chunk in range(FF // CHUNK):
        part, at = chunk // per_part, (chunk % per_part) * CHUNK
        at_lanes = slice(at, at + CHUNK)
        lanes = slice(chunk * CHUNK, (chunk + 1) * CHUNK)
        grad_hidden = mm_nt(grad_down, down_weights[part][at_lanes, :])
        grad_pre_wide = (grad_hidden * slope_ref[:, lanes].astype(F32)).astype(BF)
        outs[part][at : at + CHUNK, :] = mm_tn(hidden_ref[:, lanes], near).astype(BF)
        grad_up = mm_tn(normed_ref[:, :half], grad_pre_wide).astype(BF)
        bias_sum = jnp.sum(grad_pre_wide.astype(F32), 0, keepdims=True)
        for piece in range(CHUNK // half):
            place = FF // 2 + (at // half + piece) * half
            outs[part][place : place + half, :] = grad_up[:, piece * half : (piece + 1) * half]
            line = 3 + at // half + piece
            small_outs[part][line : line + 1, :] = bias_sum[:, piece * half : (piece + 1) * half]
        grad_normed = grad_normed + mm_nt(grad_pre_wide, up_weights[part][:, at_lanes])
    grad_input, grad_gain, grad_shift = norm_back(
        grad_normed, mid_ref[...], small_ref[GAIN_TWO : GAIN_TWO + 1]
    )
    grad_mid_ref[...] = clear_padding(grad + grad_input)
    down_bias = jnp.sum(near.astype(F32), 0, keepdims=True)
    for small in small_outs:
        small[0:1, :] = down_bias
        small[1:2, :] = grad_gain[:, :half]
        small[2:3, :] = grad_shift[:, :half]
        small[7:8, :] = jnp.zeros((1, half), F32)


def attn_bwd_kernel(
    layer, weights, grad_mid_ref, att_ref, qkv_ref, probs_ref, picks_ref, picks_t_ref, normed_ref, small_ref, x_ref,
    grad_ref, keep_ref, send_ref, small_keep_ref, small_send_ref, table_ref, grad_qkv, scratch, flat,
):
    qkv_weights, out_weights = weights
    half = D // 2
    grad_mid = grad_mid_ref[...]
    grad_att = grad_mid.astype(BF)
    near = grad_att[:, :half]
    outs = (keep_ref, send_ref)
    small_outs = (small_keep_ref, small_send_ref)
    mask = head_mask()
    grad_normed = jnp.zeros((ROWS, D), F32)
    for part in range(2):
        grad_attended = mm_nt(grad_att, out_weights[part][...]).astype(BF)
        outs[part][3 * half : 4 * half, :] = mm_tn(att_ref[:, part * half : (part + 1) * half], near).astype(BF)
        for inner in range(2):
            group, lane = part * 2 + inner, inner * 128
            tables = [jnp.zeros((64, PAD), F32) for _ in range(GROUP)]
            for side in range(2):
                rows = slice(side * PAD, (side + 1) * PAD)
                query = stack_heads(qkv_ref[part, rows, lane : lane + 128], mask)
                key = qkv_ref[part, rows, half + lane : half + lane + 128]
                value = qkv_ref[part, rows, 2 * half + lane : 2 * half + lane + 128]
                grad_out = stack_heads(grad_attended[rows, lane : lane + 128], mask)
                probs_low = probs_ref[side, group]
                probs = probs_low.astype(F32)
                grad_probs = mm_nt(grad_out, value)
                weighted = jnp.sum(probs * grad_probs, -1, keepdims=True)
                grad_scores = (probs * (grad_probs - weighted)).astype(BF)
                grad_value = mm_tn(probs_low, grad_out)
                grad_query = unstack_heads(mm(grad_scores, key), mask) * SCALE
                grad_key = mm_tn(grad_scores, query) * SCALE
                grad_qkv[part, rows, lane : lane + 128] = grad_query.astype(BF)
                grad_qkv[part, rows, half + lane : half + lane + 128] = grad_key.astype(BF)
                grad_qkv[part, rows, 2 * half + lane : 2 * half + lane + 128] = grad_value.astype(BF)
                picked = mm(grad_scores, picks_ref[...]).astype(BF)
                for head in range(GROUP):
                    tables[head] = tables[head] + mm(picks_t_ref[0:64, :], picked[head * PAD : (head + 1) * PAD])
            for head in range(GROUP):
                table_ref[group * GROUP + head] = tables[head][:56]
        for kind in range(3):
            lanes = slice(kind * half, (kind + 1) * half)
            grads = grad_qkv[part, :, lanes]
            outs[part][kind * half : (kind + 1) * half, :] = mm_tn(normed_ref[:, :half], grads).astype(BF)
            grad_normed = grad_normed + mm_nt(grads, qkv_weights[part][kind])
            if kind != 1:
                line = 3 + kind // 2
                small_outs[part][line : line + 1, :] = jnp.sum(grads.astype(F32), 0, keepdims=True)
    grad_input, grad_gain, grad_shift = norm_back(
        grad_normed, x_ref[...], small_ref[GAIN_ONE : GAIN_ONE + 1]
    )
    total = clear_padding(grad_mid + grad_input)
    scratch[...] = total
    if layer % 2 == 1:
        unroll_rows(scratch, grad_ref)
    else:
        flat[0:HALF, :] = scratch[0:HALF, 0:half]
        flat[HALF:IMAGE, :] = scratch[PAD : PAD + HALF, 0:half]
        grad_ref[...] = flat[0:IMAGE, :].astype(BF)
    out_bias = jnp.sum(near.astype(F32), 0, keepdims=True)
    for small in small_outs:
        small[0:1, :] = out_bias
        small[1:2, :] = grad_gain[:, :half]
        small[2:3, :] = grad_shift[:, :half]
        small[5:8, :] = jnp.zeros((3, half), F32)


DOWN_AT, UP_AT, QKV_AT, OUT_AT, TAIL_AT = 0, 1024, 2048, 2816, 3072
BLOCK_ROWS = 3200
RING = 8
PIECE = BLOCK_ROWS // (2 * RING)


def unpack_kernel(count, *refs):
    starts = refs[0]
    pieces = refs[1 : 1 + 2 * count]
    (qkv_ref, qv_ref, out_ref, out_bias_ref, up_ref, up_bias_ref, down_ref, down_bias_ref,
     gain_ref, shift_ref, table_ref, block) = refs[1 + 2 * count :]
    half = D // 2
    for layer in range(LAYERS):
        for number in range(count):
            piece = pieces[layer * count + number]
            size = piece.shape[0]
            at = pl.multiple_of(starts[number], 8)
            block[pl.ds(at, size), :] = piece[...].astype(F32)
        down_ref[layer] = block[DOWN_AT : DOWN_AT + FF // 2, :]
        for piece in range(4):
            up_ref[layer, :, piece * half : (piece + 1) * half] = block[
                UP_AT + piece * half : UP_AT + (piece + 1) * half, :
            ]
        for kind in range(3):
            qkv_ref[layer, kind] = block[QKV_AT + kind * half : QKV_AT + (kind + 1) * half, :]
        out_ref[layer] = block[OUT_AT : OUT_AT + half, :]
        tail = block[TAIL_AT : TAIL_AT + 24, :]
        down_bias_ref[layer : layer + 1, :] = tail[0:1]
        gain_ref[layer, 1:2, :] = tail[1:2]
        shift_ref[layer, 1:2, :] = tail[2:3]
        for piece in range(4):
            up_bias_ref[layer : layer + 1, piece * half : (piece + 1) * half] = tail[3 + piece : 4 + piece]
        out_bias_ref[layer : layer + 1, :] = tail[8:9]
        gain_ref[layer, 0:1, :] = tail[9:10]
        shift_ref[layer, 0:1, :] = tail[10:11]
        qv_ref[layer] = tail[11:13]
        table_ref[layer] = tail[16:24, :TABLE]


ANY = pl.BlockSpec(memory_space=pl.ANY)
VMEM = pl.BlockSpec(memory_space=pltpu.VMEM)
SMEM = pl.BlockSpec(memory_space=pltpu.SMEM)


def call(kernel, outs, scratch, args, micros, specs=None, out_specs=None, limit=40, aliases=None):
    return pl.pallas_call(
        kernel,
        out_shape=[jax.ShapeDtypeStruct(shape, kind) for shape, kind in outs],
        in_specs=specs or [VMEM] * len(args),
        out_specs=out_specs or [VMEM] * len(outs),
        scratch_shapes=scratch,
        input_output_aliases=aliases or {},
        compiler_params=pltpu.CompilerParams(vmem_limit_bytes=limit * 1024 * 1024),
        cost_estimate=pl.CostEstimate(flops=int(micros * 1.15e6), bytes_accessed=0, transcendentals=0),
    )(*args)


def layer_call(kernel, layer, outs, scratch, weights, args, micros, attn, behind=()):
    rooms, weight_copies, load = (
        (ATTN_ROOMS, ATTN_COPIES, attn_weights) if attn else (FFN_ROOMS, FFN_COPIES, ffn_weights)
    )

    def run(*refs):
        refs = list(refs)

        def take(number):
            taken = refs[:number]
            del refs[:number]
            return taken

        weight_refs, arg_refs, _, out_refs = take(len(weights)), take(len(args)), take(len(behind)), take(len(outs))
        weight_rooms, arg_rooms, others, (sems,) = take(len(rooms)), take(len(args)), take(len(scratch)), take(1)
        fetched = [
            whole_fetch(ref, room, sems, weight_copies + at) for at, (ref, room) in enumerate(zip(arg_refs, arg_rooms))
        ]
        loaded = load(layer, weight_refs, weight_rooms, sems, 0)
        if kernel in FORWARD:
            pending = fetched[:2] + loaded[0] + fetched[2:] + loaded[1]
        else:
            pending = fetched[:1] + loaded[1] + fetched[1:] + loaded[0]
        for item in pending:
            item.start()
        kernel(layer, loaded, *fetched, *out_refs, *others)
        for item in pending:
            item.ready()

    spaces = (
        [pltpu.VMEM(shape, kind) for shape, kind in rooms]
        + [pltpu.VMEM(a.shape, a.dtype) for a in args]
        + scratch
        + [pltpu.SemaphoreType.DMA((weight_copies + len(args),))]
    )
    operands = [*weights, *args, *behind]
    return call(run, outs, spaces, operands, micros, [ANY] * len(operands))


def turn_call(layer, forward, blocks, wholes, named, outs):
    half = D // 2
    weights = [*wholes[2:], *blocks, *wholes[:2], *blocks]
    names, args = list(named), list(named.values())
    inner = {"normed_two": ((ROWS, D), BF), "slope": ((ROWS, FF), BF), "hidden": ((ROWS, FF), BF)}
    inner = inner if forward else {}
    spaces = [
        ((ROWS, D), F32), ((200, half), F32), ((ROWS, D), F32), ((2, ROWS, 3 * half), BF), *inner.values(),
    ]

    def run(*refs):
        refs = list(refs)

        def take(number):
            taken = refs[:number]
            del refs[:number]
            return taken

        weight_refs, arg_refs, out_refs = take(14), take(len(args)), take(len(outs))
        ffn_rooms, attn_rooms, arg_rooms = take(4), take(4), take(len(args))
        scratch, flat, grad_mid, grad_qkv = take(4)
        made = dict(zip(inner, take(len(inner))))
        (sems,) = take(1)
        ups, downs = ffn_weights(layer, weight_refs[:7], ffn_rooms, sems, 0)
        qkvs, mixes = attn_weights(layer, weight_refs[7:], attn_rooms, sems, FFN_COPIES)
        got = {
            name: whole_fetch(ref, room, sems, FFN_COPIES + ATTN_COPIES + at)
            for at, (name, ref, room) in enumerate(zip(names, arg_refs, arg_rooms))
        }
        early = ("middle", "small") if forward else ("grad", "slope", "hidden")
        late = [got[name] for name in names if name not in early]
        early = [got[name] for name in early]
        if forward:
            pending = [*early, *ups, *downs, *late, *mixes, *qkvs]
        else:
            pending = [early[0], downs[0], *early[1:], got["normed_two"], ups[0], downs[1], ups[1]]
            pending += [item for item in late if item is not got["normed_two"]] + [*mixes, *qkvs]
        for item in pending:
            item.start()
        got.update(made)
        outputs = list(out_refs)
        if forward:
            ffn_fwd_kernel(
                layer, (ups, downs), got["middle"], got["small"], outputs.pop(0), got["normed_two"], got["slope"],
                got["hidden"], scratch, flat,
            )
        ffn_bwd_kernel(
            layer, (ups, downs), got["grad"], got["slope"], got["hidden"], got["normed_two"], got["small"],
            got["middle"], grad_mid, *outputs[:4],
        )
        attn_bwd_kernel(
            layer, (qkvs, mixes), grad_mid, got["att"], got["qkv"], got["probs"], got["picks"], got["picks_t"],
            got["normed_one"], got["small"], got["x"], *outputs[4:], grad_qkv, scratch, flat,
        )
        for item in pending:
            item.ready()

    scratch = (
        [pltpu.VMEM(shape, kind) for shape, kind in FFN_ROOMS + ATTN_ROOMS]
        + [pltpu.VMEM(a.shape, a.dtype) for a in args]
        + [pltpu.VMEM(shape, kind) for shape, kind in spaces]
        + [pltpu.SemaphoreType.DMA((FFN_COPIES + ATTN_COPIES + len(args),))]
    )
    operands = [*weights, *args]
    return call(run, outs, scratch, operands, 12, [ANY] * len(operands))


FORWARD = (attn_fwd_kernel, ffn_fwd_kernel)


def part_of(kernel, layer):
    def run(*refs):
        return kernel(layer, *refs)

    return run


def ring_perms():
    order = [0, 2, 4, 6, 7, 5, 3, 1]
    onward = [(order[i], order[(i + 1) % RING]) for i in range(RING)]
    return onward, [(b, a) for a, b in onward]


def ring_sum(pieces, place, one, two):
    onward, back = ring_perms()
    for step in range(RING - 1):
        one, two = lax.ppermute(one, "dp", onward), lax.ppermute(two, "dp", back)
        one = one + pick(pieces, (place - 2 - step) % RING)
        two = two + pick(pieces, RING + (place + 2 + step) % RING)
    return ring_gather(one, two)


def pick(values, index):
    return lax.dynamic_index_in_dim(values, index, 0, keepdims=False)


def ring_gather(one, two):
    onward, back = ring_perms()
    pieces = [one, two]
    for _ in range(RING - 1):
        one, two = lax.ppermute(one, "dp", onward), lax.ppermute(two, "dp", back)
        pieces += [one, two]
    return pieces


def piece_starts(place):
    starts = []
    for step in range(RING):
        starts += [((place - step) % RING) * PIECE, (RING + (place + step) % RING) * PIECE]
    return jnp.stack(starts).astype(jnp.int32)


def on_device(
    ring, tokens, cotangent, qkv_weight, qv_bias, out_weight, out_bias, up_weight, up_bias,
    down_weight, down_bias, norm_gain, norm_shift, bias_table, index_map, region_ids,
):
    half, quarter = D // 2, D // 4
    device = lax.axis_index("dp")
    parity = device % 2
    neighbours = [(i, i ^ 1) for i in range(lax.axis_size("dp"))]

    wholes = [qkv_weight.transpose(0, 2, 1, 3), out_weight, up_weight, down_weight]
    parity_ref = parity.astype(jnp.int32).reshape(1)
    sources = [*wholes, tokens, cotangent, norm_gain, norm_shift, out_bias, down_bias]
    pack_outs = [((MISC_ROWS, half), BF), ((3 * D, half), BF), ((3 * D, half), BF)]
    packs = [None, None]
    packs[0], packs[1], whole = call(
        pack_kernel,
        [((MISC_ROWS + 3 * D, half), BF), ((3 * D, half), BF), ((LAYERS * TAIL_AT, half), BF)],
        [pltpu.VMEM(value.shape[1:], value.dtype) for value in wholes] * LAYERS
        + [pltpu.VMEM(shape, kind) for shape, kind in pack_outs]
        + [pltpu.SemaphoreType.DMA((8,)), pltpu.SemaphoreType.DMA((21,))],
        [parity_ref, *sources],
        3,
        [SMEM] + [ANY] * 4 + [VMEM] * 6,
        [ANY] * 3,
        limit=60,
    )
    (misc_row,) = call(
        misc_kernel,
        [((32, half), BF)],
        [],
        [qv_bias, up_bias, bias_table.transpose(0, 2, 1), packs[1]],
        1,
        [VMEM] * 3 + [ANY],
    )
    row_far = swap(misc_row, "row")
    whole_row = swap(whole, "row")
    from_col = [swap(pack, "col") for pack in packs]
    misc, misc_far = packs[0][:MISC_ROWS], from_col[0][:MISC_ROWS]
    from_col[0] = from_col[0][MISC_ROWS:]

    def block(pack, token):
        from_dp = lax.ppermute(pack, "dp", neighbours)
        from_dp = after(from_dp, token)
        return [pack, from_dp, whole_row, swap(pack, "row"), swap(from_dp, "row")]

    picks = np.stack([position_one_hot(layer) for layer in range(LAYERS)])
    picks_t = [jnp.asarray(pick.T, BF) for pick in picks]
    picks_all = jnp.asarray(picks, BF)
    picks = [jnp.asarray(pick, BF) for pick in picks]
    masks = [mask_of(layer, region_ids) for layer in range(LAYERS)]
    wide = ((ROWS, D), F32)
    x, grad, *rest = call(
        prep_kernel,
        [wide, wide, ((16, D), F32), ((16, D), F32), ((HEADS, PAD, PAD), F32), ((HEADS, PAD, PAD), F32)],
        [
            pltpu.VMEM((64, LAYERS * HEADS, PAD), F32), pltpu.VMEM((56, PAD), jnp.int32),
            pltpu.VMEM((208, D), F32),
        ],
        [parity_ref, misc, misc_far, misc_row, row_far, index_map, picks_all],
        4,
        [SMEM] + [VMEM] * 6,
    )
    smalls, bias = rest[:2], rest[2:4]
    blocks = [block(from_col[0], x)]

    image = ((IMAGE, half), BF)
    saved = []
    for layer in range(LAYERS):
        middle, normed_one, qkv, probs, att = layer_call(
            attn_fwd_kernel,
            layer,
            [
                wide, ((ROWS, D), BF), ((2, ROWS, 3 * half), BF),
                ((2, GROUPS, STACK, PAD), BF), ((ROWS, D), BF),
            ],
            [],
            [*wholes[:2], *blocks[layer]],
            [x, smalls[layer], bias[layer], masks[layer]],
            4,
            True,
            [from_col[1]] if layer == 0 else [],
        )
        if layer == LAYERS - 1:
            saved.append((x, middle, normed_one, qkv, probs, att, None, None, None))
            break
        result, normed_two, pre, hidden = layer_call(
            ffn_fwd_kernel,
            layer,
            [wide, ((ROWS, D), BF), ((ROWS, FF), BF), ((ROWS, FF), BF)],
            [pltpu.VMEM((ROWS, D), F32), pltpu.VMEM((200, half), F32)],
            [*wholes[2:], *blocks[layer]],
            [middle, smalls[layer]],
            4,
            False,
        )
        if layer == 0:
            blocks.append(block(from_col[1], result))
        saved.append((x, middle, normed_one, qkv, probs, att, normed_two, pre, hidden))
        x = result

    heads = HEADS // 2
    one_hot = (index_map[:, :, None] == jnp.arange(256, dtype=jnp.int32)).astype(F32).reshape(SPAN * SPAN, 256)
    sums = [None] * LAYERS
    place = jnp.where(parity == 0, device // 2, RING - 1 - device // 2)
    place_ref = place.astype(jnp.int32).reshape(1)
    for layer in reversed(range(LAYERS)):
        x_in, middle, normed_one, qkv, probs, att, normed_two, pre, hidden = saved[layer]
        small_shape = ((8, half), F32)
        named = {
            "middle": middle, "small": smalls[layer], "grad": grad, "slope": pre, "hidden": hidden,
            "normed_two": normed_two, "att": att, "qkv": qkv, "probs": probs, "picks": picks[layer],
            "picks_t": picks_t[layer], "normed_one": normed_one, "x": x_in,
        }
        named = {name: value for name, value in named.items() if value is not None}
        last = layer == LAYERS - 1
        results = turn_call(
            layer,
            last,
            blocks[layer],
            wholes,
            named,
            [image] * last
            + [
                ((FF, half), BF), ((FF, half), BF), small_shape, small_shape,
                wide if layer > 0 else image, ((2 * D, half), BF), ((2 * D, half), BF), small_shape, small_shape,
                ((HEADS, 56, PAD), F32),
            ],
        )
        if last:
            output, *results = results
        ffn_keep, ffn_send, small_keep, small_send, grad, keep, send, att_keep, att_send, counts = results
        ffn_got = swap(ffn_send, "row")
        got = swap(send, "row")
        table = jnp.dot(counts[:, :SPAN, :SPAN].reshape(HEADS, SPAN * SPAN), one_hot, precision=HIGH)
        tail_keep = jnp.concatenate([small_keep, att_keep, table[:heads]], 0)
        tail_send = jnp.concatenate([small_send, att_send, table[heads:]], 0)
        pieces, one, two = call(
            combine_kernel,
            [((2 * RING, PIECE, half), BF), ((PIECE, half), BF), ((PIECE, half), BF)],
            [pltpu.VMEM((BLOCK_ROWS, half), F32)],
            [place_ref, ffn_keep, ffn_got, keep, got, tail_keep, swap(tail_send, "row")],
            2,
            [SMEM] + [VMEM] * 6,
            limit=24,
        )
        if ring:
            sums[layer] = ring_sum(pieces, place, one, two)
        else:
            sums[layer] = [lax.psum(pieces.reshape(BLOCK_ROWS, half), "dp")]
    input_grad = grad

    count = len(sums[0])
    starts = piece_starts(place) if ring else jnp.zeros((1,), jnp.int32)
    qkv, qv, outw, outb, up, upb, down, downb, gain, shift, table = call(
        part_of(unpack_kernel, count),
        [
            ((LAYERS, 3, half, half), F32), ((LAYERS, 2, half), F32), ((LAYERS, half, half), F32),
            ((LAYERS, half), F32), ((LAYERS, half, FF // 2), F32), ((LAYERS, FF // 2), F32),
            ((LAYERS, FF // 2, half), F32), ((LAYERS, half), F32), ((LAYERS, 2, half), F32),
            ((LAYERS, 2, half), F32), ((LAYERS, heads, TABLE), F32),
        ],
        [pltpu.VMEM((BLOCK_ROWS, half), F32)],
        [starts, *sums[0], *sums[1]],
        4,
        [SMEM] + [VMEM] * (2 * count),
    )
    return (
        output, input_grad, qkv.transpose(0, 2, 1, 3), qv, outw, outb, up, upb, down, downb, gain, shift,
        table.transpose(0, 2, 1),
    )


def solution(mesh):
    in_specs = (
        P(("dp", "row"), "col"),
        P(("dp", "row"), "col"),
        P(None, "col", None, "row"),
        P(None, None, "row"),
        P(None, "row", "col"),
        P(None, "col"),
        P(None, "col", "row"),
        P(None, "row"),
        P(None, "row", "col"),
        P(None, "col"),
        P(None, None, "col"),
        P(None, None, "col"),
        P(None, None, "row"),
        P(),
        P(),
    )
    out_specs = (
        P(("dp", "row"), "col"),
        P(("dp", "row"), "col"),
        P(None, "col", None, "row"),
        P(None, None, "row"),
        P(None, "row", "col"),
        P(None, "col"),
        P(None, "col", "row"),
        P(None, "row"),
        P(None, "row", "col"),
        P(None, "col"),
        P(None, None, "col"),
        P(None, None, "col"),
        P(None, None, "row"),
    )
    ring = mesh.shape["dp"] == RING
    return jax.shard_map(
        part_of(on_device, ring), mesh=mesh, in_specs=in_specs, out_specs=out_specs, check_vma=False
    )
```

```python
import math

import jax
import jax.numpy as jnp
import numpy as np
from jax import lax
from jax.experimental import pallas as pl
from jax.experimental.pallas import tpu as pltpu
from jax.sharding import PartitionSpec as P

D = 512
HEADS = 16
HEAD_DIM = 32
FF = 2048
GRID = 14
WINDOW = 7
SHIFT = 3
TABLE = 169
LAYERS = 2
SPAN = WINDOW * WINDOW
IMAGE = GRID * GRID

EPS = 1e-05
NEG = -1000000000.0
HIGH = lax.Precision.HIGHEST
SCALE = 1.0 / math.sqrt(HEAD_DIM)

HALF = IMAGE // 2
PAD = 128
ROWS = 2 * PAD
ROLL = SHIFT * GRID
GROUP = 128 // HEAD_DIM
GROUPS = HEADS // GROUP
STACK = GROUP * PAD
CHUNK = 512
BF = jnp.bfloat16
F32 = jnp.float32


def swap(values, axis):
    return lax.ppermute(values, axis, [(0, 1), (1, 0)])


def mm(left, right):
    return lax.dot_general(left, right, (((1,), (0,)), ((), ())), preferred_element_type=F32)


def mm_nt(left, right):
    return lax.dot_general(left, right, (((1,), (1,)), ((), ())), preferred_element_type=F32)


def mm_tn(left, right):
    return lax.dot_general(left, right, (((0,), (0,)), ((), ())), preferred_element_type=F32)


def token_positions(layer):
    token = np.arange(HALF)
    line, column = token // GRID, token % GRID
    if layer % 2 == 1:
        column = (column - SHIFT) % GRID
    return line * WINDOW + column % WINDOW, column // WINDOW, line * GRID + column


def position_one_hot(layer):
    position, _, _ = token_positions(layer)
    picks = np.zeros((PAD, PAD), np.float32)
    picks[np.arange(HALF), position] = 1.0
    return picks


def mask_of(layer, region_ids):
    _, window, place = token_positions(layer)
    same = np.zeros((PAD, PAD), bool)
    same[:HALF, :HALF] = window[:, None] == window[None, :]
    same[HALF:, :HALF] = True
    allowed = jnp.broadcast_to(jnp.asarray(same)[None], (2, PAD, PAD))
    if layer % 2 == 1:
        ids = jnp.roll(region_ids.reshape(2, WINDOW, GRID), SHIFT, 2).reshape(2, HALF)
        ids = jnp.pad(ids, ((0, 0), (0, PAD - HALF)), constant_values=-1)
        pad_row = jnp.asarray(np.arange(PAD) >= HALF)[None, :, None]
        allowed = allowed & ((ids[:, :, None] == ids[:, None, :]) | pad_row)
    return jnp.where(allowed, 0.0, NEG).astype(F32)


def head_mask():
    lane = lax.broadcasted_iota(jnp.int32, (STACK, PAD), 1) // HEAD_DIM
    row = lax.broadcasted_iota(jnp.int32, (STACK, PAD), 0) // PAD
    return lane == row


def stack_heads(values, mask):
    tiled = jnp.concatenate([values] * GROUP, axis=0)
    return jnp.where(mask, tiled, jnp.zeros_like(tiled))


def unstack_heads(values, mask):
    kept = jnp.where(mask, values, 0.0)
    total = kept[0:PAD]
    for head in range(1, GROUP):
        total = total + kept[head * PAD : (head + 1) * PAD]
    return total


def norm_parts(values):
    average = jnp.mean(values, -1, keepdims=True)
    centred = values - average
    variance = jnp.mean(centred * centred, -1, keepdims=True)
    inverse = lax.rsqrt(variance + EPS)
    return centred * inverse, inverse


def norm_back(grad_normed, values, gain):
    xhat, inverse = norm_parts(values)
    scaled = grad_normed * gain
    mean_one = jnp.mean(scaled, -1, keepdims=True)
    mean_two = jnp.mean(scaled * xhat, -1, keepdims=True)
    grad_input = inverse * (scaled - mean_one - xhat * mean_two)
    return grad_input, jnp.sum(grad_normed * xhat, 0, keepdims=True), jnp.sum(grad_normed, 0, keepdims=True)


def split_halves(values):
    return values[:, : D // 2], values[:, D // 2 :]


def gelu_and_slope(values):
    below = 0.5 * (1.0 + lax.erf(values * (1.0 / math.sqrt(2.0))))
    density = jnp.exp(-0.5 * values * values) * (1.0 / math.sqrt(2.0 * math.pi))
    return values * below, below + values * density


TABLE_ROWS = 176

GAIN_ONE, GAIN_TWO, SHIFT_ONE, SHIFT_TWO, OUT_BIAS, DOWN_BIAS, Q_BIAS, V_BIAS, UP_BIAS = 0, 1, 2, 3, 4, 5, 6, 7, 8


def prep_kernel(
    parity_ref, misc_ref, misc_far, row_ref, row_far, index_ref, picks_ref,
    x_ref, grad_ref, small_zero, small_one, bias_zero, bias_one, pairs_ref, index_pad, flat,
):
    half, quarter = D // 2, D // 4
    even = parity_ref[0] == 0

    def ordered(values):
        low, high = values[:, :quarter], values[:, quarter:]
        return jnp.where(even, low, high), jnp.where(even, high, low)

    def lay_out(at):
        first, second = ordered(misc_far[at : at + 208, :].astype(F32))
        flat[:, 0:half] = misc_ref[at : at + 208, :].astype(F32)
        flat[:, half : half + quarter] = first
        flat[:, half + quarter :] = second

    x_ref[...] = jnp.zeros_like(x_ref)
    grad_ref[...] = jnp.zeros_like(grad_ref)
    lay_out(TOKENS_AT)
    x_ref[0:HALF, :] = flat[0:HALF, :]
    x_ref[PAD : PAD + HALF, :] = flat[HALF:IMAGE, :]
    lay_out(COT_AT)
    rest = HALF - ROLL
    grad_ref[0:HALF, :] = flat[ROLL : ROLL + HALF, :]
    grad_ref[PAD : PAD + rest, :] = flat[ROLL + HALF : IMAGE, :]
    grad_ref[PAD + rest : PAD + HALF, :] = flat[0:ROLL, :]

    near = misc_ref[SMALL_AT:MISC_ROWS, :].astype(F32)
    far_first, far_second = ordered(misc_far[SMALL_AT:MISC_ROWS, :].astype(F32))
    rows_near, rows_far = row_ref[...].astype(F32), row_far[...].astype(F32)
    for layer, small in enumerate((small_zero, small_one)):
        small[...] = jnp.zeros_like(small)

        def features(row, source):
            small[row : row + 1, 0:half] = near[source : source + 1]
            small[row : row + 1, half : half + quarter] = far_first[source : source + 1]
            small[row : row + 1, half + quarter :] = far_second[source : source + 1]

        for which in range(2):
            features(GAIN_ONE + which, 2 * layer + which)
            features(SHIFT_ONE + which, 4 + 2 * layer + which)
            for part, source in enumerate((rows_near, rows_far)):
                lanes = slice(part * half, (part + 1) * half)
                at = 2 * layer + which
                small[Q_BIAS + which : Q_BIAS + which + 1, lanes] = source[at : at + 1]
                line = UP_BIAS + 2 * part + which
                for piece in range(2):
                    at = 4 + 2 * (2 * which + piece) + layer
                    small[line : line + 1, piece * half : (piece + 1) * half] = source[at : at + 1]
        features(OUT_BIAS, 8 + layer)
        features(DOWN_BIAS, 10 + layer)

    heads = HEADS // 2
    tables = []
    for layer in range(LAYERS):
        for source in (rows_near, rows_far):
            tables.append(source[16 + layer * heads : 16 + (layer + 1) * heads, :TABLE_ROWS])
    table = jnp.concatenate(tables, 0).astype(BF)
    index_pad[...] = jnp.full(index_pad.shape, -1, jnp.int32)
    index_pad[0:SPAN, 0:SPAN] = index_ref[...]
    pairs_ref[SPAN:64] = jnp.zeros((64 - SPAN, LAYERS * HEADS, PAD), F32)
    for position in range(SPAN):
        wanted = index_pad[position : position + 1, :]
        hot = (lax.broadcasted_iota(jnp.int32, (TABLE_ROWS, PAD), 0) == wanted).astype(F32).astype(BF)
        pairs_ref[position] = mm(table, hot)
    for layer, bias_ref in enumerate((bias_zero, bias_one)):
        picks = picks_ref[layer]
        for head in range(HEADS):
            bias = pairs_ref[:, layer * HEADS + head, :]
            spread = mm(picks[:, :64], bias.astype(BF)).astype(BF)
            bias_ref[head] = mm_nt(spread, picks)


class Fetch:
    def __init__(self, copies, ref):
        self.copies, self.ref, self.waiting = copies, ref, True

    def start(self):
        for copy in self.copies:
            copy.start()

    def ready(self):
        if self.waiting:
            self.waiting = False
            for copy in self.copies:
                copy.wait()
        return self.ref

    def __getitem__(self, index):
        return self.ready()[index]


def whole_fetch(source, room, sems, at):
    return Fetch([pltpu.make_async_copy(source, room, sems.at[at])], room)


def attn_weights(layer, sources, rooms, sems, at):
    half, quarter = D // 2, D // 4
    qkv, out, from_col, from_dp, whole_row, from_col_row, from_dp_row = sources
    qkvs, outs = [], []
    whole_at = layer * TAIL_AT
    for part, packs in enumerate(((from_col, from_dp), (from_col_row, from_dp_row))):
        room_qkv, room_out = rooms[2 * part], rooms[2 * part + 1]
        pairs, pairs_out = [], []
        for kind in range(3):
            lines = slice(whole_at + QKV_AT + kind * half, whole_at + QKV_AT + (kind + 1) * half)
            source = qkv.at[layer, kind] if part == 0 else whole_row.at[lines, :]
            pairs.append((source, room_qkv.at[kind, 0:half, :]))
        source = out.at[layer] if part == 0 else whole_row.at[whole_at + OUT_AT : whole_at + TAIL_AT, :]
        pairs_out.append((source, room_out.at[:, 0:half]))
        for slot, pack in enumerate(packs):
            first = half + slot * quarter
            for kind in range(3):
                pairs.append(
                    (
                        pack.at[kind * quarter : (kind + 1) * quarter, :],
                        room_qkv.at[kind, first : first + quarter, :],
                    )
                )
            for side in range(2):
                lanes = slice(side * quarter, (side + 1) * quarter)
                pairs_out.append((pack.at[3 * quarter : 4 * quarter, lanes], room_out.at[lanes, first : first + quarter]))
        for found, room, list_of in ((pairs, room_qkv, qkvs), (pairs_out, room_out, outs)):
            copies = []
            for source, target in found:
                copies.append(pltpu.make_async_copy(source, target, sems.at[at]))
                at += 1
            list_of.append(Fetch(copies, room))
    return qkvs, outs


ATTN_COPIES = 2 * (9 + 5)
ATTN_ROOMS = [((3, D, D // 2), BF), ((D // 2, D), BF)] * 2


def ffn_weights(layer, sources, rooms, sems, at):
    half, quarter, wide = D // 2, D // 4, FF // 4
    up, down, from_col, from_dp, whole_row, from_col_row, from_dp_row = sources
    ups, downs = [], []
    whole_at = layer * TAIL_AT
    for part, packs in enumerate(((from_col, from_dp), (from_col_row, from_dp_row))):
        room_up, room_down = rooms[2 * part], rooms[2 * part + 1]
        pairs, pairs_down = [], []
        for piece in range(4):
            lanes = slice(piece * half, (piece + 1) * half)
            lines = slice(whole_at + UP_AT + piece * half, whole_at + UP_AT + (piece + 1) * half)
            source = up.at[layer, :, lanes] if part == 0 else whole_row.at[lines, :]
            pairs.append((source, room_up.at[0:half, lanes]))
        source = down.at[layer] if part == 0 else whole_row.at[whole_at + DOWN_AT : whole_at + UP_AT, :]
        pairs_down.append((source, room_down.at[:, 0:half]))
        for slot, pack in enumerate(packs):
            first = half + slot * quarter
            for piece in range(4):
                lanes = slice(piece * half, (piece + 1) * half)
                pairs.append(
                    (
                        pack.at[D + piece * quarter : D + (piece + 1) * quarter, :],
                        room_up.at[first : first + quarter, lanes],
                    )
                )
            for side in range(2):
                lanes = slice(side * quarter, (side + 1) * quarter)
                pairs_down.append(
                    (
                        pack.at[2 * D :, lanes],
                        room_down.at[side * wide : (side + 1) * wide, first : first + quarter],
                    )
                )
        for found, room, list_of in ((pairs, room_up, ups), (pairs_down, room_down, downs)):
            copies = []
            for source, target in found:
                copies.append(pltpu.make_async_copy(source, target, sems.at[at]))
                at += 1
            list_of.append(Fetch(copies, room))
    return ups, downs


FFN_COPIES = 2 * (12 + 5)
FFN_ROOMS = [((D, FF // 2), BF), ((FF // 2, D), BF)] * 2


def misc_kernel(qv_bias, up_bias, table, _, misc_row):
    half = D // 2
    rows = [qv_bias[0], qv_bias[1]] + [up_bias[:, piece * half : (piece + 1) * half] for piece in range(4)]
    rows = [row.astype(F32) for row in rows] + [jnp.zeros((4, half), F32)]
    misc_row[0:16, :] = jnp.concatenate(rows, 0).astype(BF)
    tables = jnp.concatenate([table[layer].astype(F32) for layer in range(LAYERS)], 0)
    misc_row[16:32, :] = jnp.pad(tables, ((0, 0), (0, half - TABLE))).astype(BF)


def pack_kernel(
    parity_ref, qkv, out, up, down, tokens, cot, gain, shift, out_bias, down_bias,
    pack_zero, pack_one, whole, *rest,
):
    rooms, results, (in_sems, out_sems) = rest[:8], rest[8:11], rest[11:]
    half, quarter = D // 2, D // 4
    even = parity_ref[0] == 0
    fetched = []
    for layer in range(LAYERS):
        for number, source in enumerate((qkv, out, up, down)):
            at = 4 * layer + number
            fetched.append(whole_fetch(source.at[layer], rooms[at], in_sems, at))
    for item in fetched:
        item.start()
    sent = []

    def send(source, target):
        copy = pltpu.make_async_copy(source, target, out_sems.at[len(sent)])
        copy.start()
        sent.append(copy)

    misc = results[0]
    misc[...] = jnp.zeros_like(misc)
    misc[TOKENS_AT : TOKENS_AT + IMAGE, :] = tokens[...]
    misc[COT_AT : COT_AT + IMAGE, :] = cot[...]
    rows = [gain[0], gain[1], shift[0], shift[1], out_bias[...], down_bias[...]]
    misc[SMALL_AT : SMALL_AT + 12, :] = jnp.concatenate([row.astype(F32) for row in rows], 0).astype(BF)
    send(misc, pack_zero.at[0:MISC_ROWS, :])
    for layer in range(LAYERS):
        pack = results[1 + layer]
        at = layer * TAIL_AT
        qkv_l, out_l, up_l, down_l = [item.ready() for item in fetched[4 * layer : 4 * layer + 4]]
        for kind in range(3):
            pack[kind * quarter : (kind + 1) * quarter, :] = jnp.where(
                even, qkv_l[kind, 0:quarter, :], qkv_l[kind, quarter:half, :]
            )
        chosen = jnp.where(even, out_l[:, 0:quarter], out_l[:, quarter:half])
        pack[3 * quarter : 4 * quarter, 0:quarter] = chosen[0:quarter]
        pack[3 * quarter : 4 * quarter, quarter:half] = chosen[quarter:half]
        chosen = jnp.where(even, up_l[0:quarter, :], up_l[quarter:half, :])
        for piece in range(4):
            lines = slice(D + piece * quarter, D + (piece + 1) * quarter)
            pack[lines, :] = chosen[:, piece * half : (piece + 1) * half]
        chosen = jnp.where(even, down_l[:, 0:quarter], down_l[:, quarter:half])
        pack[2 * D :, 0:quarter] = chosen[0 : FF // 4]
        pack[2 * D :, quarter:half] = chosen[FF // 4 :]
        send(pack, pack_zero.at[MISC_ROWS:, :] if layer == 0 else pack_one)
        send(down_l, whole.at[at + DOWN_AT : at + UP_AT, :])
        for piece in range(4):
            lines = slice(at + UP_AT + piece * half, at + UP_AT + (piece + 1) * half)
            send(up_l.at[:, piece * half : (piece + 1) * half], whole.at[lines, :])
        for kind in range(3):
            send(qkv_l.at[kind], whole.at[at + QKV_AT + kind * half : at + QKV_AT + (kind + 1) * half, :])
        send(out_l, whole.at[at + OUT_AT : at + TAIL_AT, :])
    for copy in sent:
        copy.wait()


def after_kernel(*refs):
    pass


def after(value, token):
    (result,) = call(
        after_kernel, [(value.shape, value.dtype)], [], [value, token], 0, [ANY] * 2, [ANY], limit=1, aliases={0: 0}
    )
    return result


TOKENS_AT, COT_AT, SMALL_AT, MISC_ROWS = 0, 208, 416, 432


def combine_kernel(place_ref, ffn_keep, ffn_got, keep, got, tail_keep, tail_got, *rest):
    pieces_ref, one_ref, two_ref, flat = rest[-4:]
    flat[0:FF, :] = ffn_keep[...].astype(F32) + ffn_got[...].astype(F32)
    flat[FF : FF + 2 * D, :] = keep[...].astype(F32) + got[...].astype(F32)
    flat[TAIL_AT:, :] = jnp.zeros((BLOCK_ROWS - TAIL_AT, D // 2), F32)
    flat[TAIL_AT : TAIL_AT + 24, :] = tail_keep[...] + tail_got[...]
    for number in range(2 * RING):
        pieces_ref[number] = flat[number * PIECE : (number + 1) * PIECE, :].astype(BF)
    place = place_ref[0]
    one_ref[...] = pieces_ref[lax.rem(place + RING - 1, RING)]
    two_ref[...] = pieces_ref[RING + lax.rem(place + 1, RING)]


def attn_fwd_kernel(
    layer, weights, x_ref, small_ref, bias_ref, mask_ref, mid_ref, normed_ref, qkv_ref, probs_ref, att_ref,
):
    qkv_weights, out_weights = weights
    x = x_ref[...]
    xhat, _ = norm_parts(x)
    normed = (
        xhat * small_ref[GAIN_ONE : GAIN_ONE + 1] + small_ref[SHIFT_ONE : SHIFT_ONE + 1]
    ).astype(BF)
    normed_ref[...] = normed
    half = D // 2
    for part in range(2):
        lanes = slice(part * half, (part + 1) * half)
        for kind in range(3):
            projected = mm(normed, qkv_weights[part][kind])
            if kind != 1:
                row = Q_BIAS if kind == 0 else V_BIAS
                projected = projected + small_ref[row : row + 1, lanes]
            qkv_ref[part, :, kind * half : (kind + 1) * half] = projected.astype(BF)
    mask = head_mask()
    for group in range(GROUPS):
        part, lane = group // 2, (group % 2) * 128
        bias = bias_ref[group * GROUP : (group + 1) * GROUP]
        for side in range(2):
            rows = slice(side * PAD, (side + 1) * PAD)
            query = qkv_ref[part, rows, lane : lane + 128]
            key = qkv_ref[part, rows, half + lane : half + lane + 128]
            value = qkv_ref[part, rows, 2 * half + lane : 2 * half + lane + 128]
            scores = mm_nt(stack_heads(query, mask), key).reshape(GROUP, PAD, PAD) * SCALE
            scores = scores + (bias + mask_ref[side][None])
            peak = jnp.max(scores, -1, keepdims=True)
            expos = jnp.exp(scores - peak)
            totals = jnp.sum(expos, -1, keepdims=True)
            probs = (expos / totals).astype(BF).reshape(STACK, PAD)
            probs_ref[side, group] = probs
            attended = unstack_heads(mm(probs, value), mask)
            att_ref[rows, group * 128 : (group + 1) * 128] = attended.astype(BF)
    first, second = split_halves(att_ref[...])
    mixed = mm(first, out_weights[0][...]) + mm(second, out_weights[1][...])
    mid_ref[...] = x + mixed + small_ref[OUT_BIAS : OUT_BIAS + 1]


def roll_rows(values_ref, result_ref):
    rest = HALF - ROLL
    result_ref[...] = jnp.zeros_like(result_ref)
    for side in range(2):
        here, there = side * PAD, (1 - side) * PAD
        result_ref[here : here + rest, :] = values_ref[here + ROLL : here + HALF, :]
        result_ref[here + rest : here + HALF, :] = values_ref[there : there + ROLL, :]


def unroll_rows(values_ref, result_ref):
    rest = HALF - ROLL
    result_ref[...] = jnp.zeros_like(result_ref)
    for side in range(2):
        here, there = side * PAD, (1 - side) * PAD
        result_ref[here + ROLL : here + HALF, :] = values_ref[here : here + rest, :]
        result_ref[here : here + ROLL, :] = values_ref[there + rest : there + HALF, :]


def clear_padding(values):
    row = lax.broadcasted_iota(jnp.int32, values.shape, 0) % PAD
    return jnp.where(row < HALF, values, 0.0)


def ffn_fwd_kernel(
    layer, weights, mid_ref, small_ref, x_ref, normed_ref, slope_ref, hidden_ref, scratch, flat,
):
    up_weights, down_weights = weights
    half = D // 2
    middle = mid_ref[...]
    xhat, _ = norm_parts(middle)
    normed = (
        xhat * small_ref[GAIN_TWO : GAIN_TWO + 1] + small_ref[SHIFT_TWO : SHIFT_TWO + 1]
    ).astype(BF)
    normed_ref[...] = normed
    total = jnp.zeros((ROWS, D), F32)
    per_part = FF // 2 // CHUNK
    for chunk in range(FF // CHUNK):
        part, at = chunk // per_part, (chunk % per_part) * CHUNK
        pre = mm(normed, up_weights[part][:, at : at + CHUNK]) + small_ref[UP_BIAS + chunk : UP_BIAS + chunk + 1]
        hidden, slope = gelu_and_slope(pre)
        hidden = hidden.astype(BF)
        slope_ref[:, chunk * CHUNK : (chunk + 1) * CHUNK] = slope.astype(BF)
        hidden_ref[:, chunk * CHUNK : (chunk + 1) * CHUNK] = hidden
        total = total + mm(hidden, down_weights[part][at : at + CHUNK, :])
    result = middle + total + small_ref[DOWN_BIAS : DOWN_BIAS + 1]
    scratch[...] = result
    if layer % 2 == 0:
        roll_rows(scratch, x_ref)
    else:
        rest = HALF - ROLL
        flat[ROLL : ROLL + HALF, :] = scratch[0:HALF, 0:half]
        flat[ROLL + HALF : IMAGE, :] = scratch[PAD : PAD + rest, 0:half]
        flat[0:ROLL, :] = scratch[PAD + rest : PAD + HALF, 0:half]
        x_ref[...] = flat[0:IMAGE, :].astype(BF)


def ffn_bwd_kernel(
    layer, weights, grad_ref, slope_ref, hidden_ref, normed_ref, small_ref, mid_ref,
    grad_mid_ref, keep_ref, send_ref, small_keep_ref, small_send_ref,
):
    up_weights, down_weights = weights
    half = D // 2
    grad = grad_ref[...]
    grad_down = grad.astype(BF)
    near = grad_down[:, :half]
    per_part = FF // 2 // CHUNK
    outs = (keep_ref, send_ref)
    small_outs = (small_keep_ref, small_send_ref)
    grad_normed = jnp.zeros((ROWS, D), F32)
    for chunk in range(FF // CHUNK):
        part, at = chunk // per_part, (chunk % per_part) * CHUNK
        at_lanes = slice(at, at + CHUNK)
        lanes = slice(chunk * CHUNK, (chunk + 1) * CHUNK)
        grad_hidden = mm_nt(grad_down, down_weights[part][at_lanes, :])
        grad_pre_wide = (grad_hidden * slope_ref[:, lanes].astype(F32)).astype(BF)
        outs[part][at : at + CHUNK, :] = mm_tn(hidden_ref[:, lanes], near).astype(BF)
        grad_up = mm_tn(normed_ref[:, :half], grad_pre_wide).astype(BF)
        bias_sum = jnp.sum(grad_pre_wide.astype(F32), 0, keepdims=True)
        for piece in range(CHUNK // half):
            place = FF // 2 + (at // half + piece) * half
            outs[part][place : place + half, :] = grad_up[:, piece * half : (piece + 1) * half]
            line = 3 + at // half + piece
            small_outs[part][line : line + 1, :] = bias_sum[:, piece * half : (piece + 1) * half]
        grad_normed = grad_normed + mm_nt(grad_pre_wide, up_weights[part][:, at_lanes])
    grad_input, grad_gain, grad_shift = norm_back(
        grad_normed, mid_ref[...], small_ref[GAIN_TWO : GAIN_TWO + 1]
    )
    grad_mid_ref[...] = grad + grad_input
    down_bias = jnp.sum(near.astype(F32), 0, keepdims=True)
    for small in small_outs:
        small[0:1, :] = down_bias
        small[1:2, :] = grad_gain[:, :half]
        small[2:3, :] = grad_shift[:, :half]
        small[7:8, :] = jnp.zeros((1, half), F32)


def attn_bwd_kernel(
    layer, weights, grad_mid_ref, att_ref, qkv_ref, probs_ref, picks_ref, picks_t_ref, normed_ref, small_ref, x_ref,
    grad_ref, keep_ref, send_ref, small_keep_ref, small_send_ref, table_ref, grad_qkv, scratch, flat,
):
    qkv_weights, out_weights = weights
    half = D // 2
    grad_mid = grad_mid_ref[...]
    grad_att = grad_mid.astype(BF)
    near = grad_att[:, :half]
    outs = (keep_ref, send_ref)
    small_outs = (small_keep_ref, small_send_ref)
    mask = head_mask()
    grad_normed = jnp.zeros((ROWS, D), F32)
    for part in range(2):
        grad_attended = mm_nt(grad_att, out_weights[part][...]).astype(BF)
        outs[part][3 * half : 4 * half, :] = mm_tn(att_ref[:, part * half : (part + 1) * half], near).astype(BF)
        for inner in range(2):
            group, lane = part * 2 + inner, inner * 128
            tables = [jnp.zeros((64, PAD), F32) for _ in range(GROUP)]
            for side in range(2):
                rows = slice(side * PAD, (side + 1) * PAD)
                query = stack_heads(qkv_ref[part, rows, lane : lane + 128], mask)
                key = qkv_ref[part, rows, half + lane : half + lane + 128]
                value = qkv_ref[part, rows, 2 * half + lane : 2 * half + lane + 128]
                grad_out = stack_heads(grad_attended[rows, lane : lane + 128], mask)
                probs_low = probs_ref[side, group]
                probs = probs_low.astype(F32)
                grad_probs = mm_nt(grad_out, value)
                weighted = jnp.sum(probs * grad_probs, -1, keepdims=True)
                grad_scores = (probs * (grad_probs - weighted)).astype(BF)
                grad_value = mm_tn(probs_low, grad_out)
                grad_query = unstack_heads(mm(grad_scores, key), mask) * SCALE
                grad_key = mm_tn(grad_scores, query) * SCALE
                grad_qkv[part, rows, lane : lane + 128] = grad_query.astype(BF)
                grad_qkv[part, rows, half + lane : half + lane + 128] = grad_key.astype(BF)
                grad_qkv[part, rows, 2 * half + lane : 2 * half + lane + 128] = grad_value.astype(BF)
                picked = mm(grad_scores, picks_ref[...]).astype(BF)
                for head in range(GROUP):
                    tables[head] = tables[head] + mm(picks_t_ref[0:64, :], picked[head * PAD : (head + 1) * PAD])
            for head in range(GROUP):
                table_ref[group * GROUP + head] = tables[head][:56]
        for kind in range(3):
            lanes = slice(kind * half, (kind + 1) * half)
            grads = grad_qkv[part, :, lanes]
            outs[part][kind * half : (kind + 1) * half, :] = mm_tn(normed_ref[:, :half], grads).astype(BF)
            grad_normed = grad_normed + mm_nt(grads, qkv_weights[part][kind])
            if kind != 1:
                line = 3 + kind // 2
                small_outs[part][line : line + 1, :] = jnp.sum(grads.astype(F32), 0, keepdims=True)
    grad_input, grad_gain, grad_shift = norm_back(
        grad_normed, x_ref[...], small_ref[GAIN_ONE : GAIN_ONE + 1]
    )
    total = grad_mid + grad_input
    scratch[...] = total
    if layer % 2 == 1:
        unroll_rows(scratch, grad_ref)
    else:
        flat[0:HALF, :] = scratch[0:HALF, 0:half]
        flat[HALF:IMAGE, :] = scratch[PAD : PAD + HALF, 0:half]
        grad_ref[...] = flat[0:IMAGE, :].astype(BF)
    out_bias = jnp.sum(near.astype(F32), 0, keepdims=True)
    for small in small_outs:
        small[0:1, :] = out_bias
        small[1:2, :] = grad_gain[:, :half]
        small[2:3, :] = grad_shift[:, :half]
        small[5:8, :] = jnp.zeros((3, half), F32)


DOWN_AT, UP_AT, QKV_AT, OUT_AT, TAIL_AT = 0, 1024, 2048, 2816, 3072
BLOCK_ROWS = 3200
RING = 8
PIECE = BLOCK_ROWS // (2 * RING)


def unpack_kernel(count, *refs):
    starts = refs[0]
    pieces = refs[1 : 1 + 2 * count]
    (qkv_ref, qv_ref, out_ref, out_bias_ref, up_ref, up_bias_ref, down_ref, down_bias_ref,
     gain_ref, shift_ref, table_ref, block) = refs[1 + 2 * count :]
    half = D // 2
    for layer in range(LAYERS):
        for number in range(count):
            piece = pieces[layer * count + number]
            size = piece.shape[0]
            at = pl.multiple_of(starts[number], 8)
            block[pl.ds(at, size), :] = piece[...].astype(F32)
        down_ref[layer] = block[DOWN_AT : DOWN_AT + FF // 2, :]
        for piece in range(4):
            up_ref[layer, :, piece * half : (piece + 1) * half] = block[
                UP_AT + piece * half : UP_AT + (piece + 1) * half, :
            ]
        for kind in range(3):
            qkv_ref[layer, kind] = block[QKV_AT + kind * half : QKV_AT + (kind + 1) * half, :]
        out_ref[layer] = block[OUT_AT : OUT_AT + half, :]
        tail = block[TAIL_AT : TAIL_AT + 24, :]
        down_bias_ref[layer : layer + 1, :] = tail[0:1]
        gain_ref[layer, 1:2, :] = tail[1:2]
        shift_ref[layer, 1:2, :] = tail[2:3]
        for piece in range(4):
            up_bias_ref[layer : layer + 1, piece * half : (piece + 1) * half] = tail[3 + piece : 4 + piece]
        out_bias_ref[layer : layer + 1, :] = tail[8:9]
        gain_ref[layer, 0:1, :] = tail[9:10]
        shift_ref[layer, 0:1, :] = tail[10:11]
        qv_ref[layer] = tail[11:13]
        table_ref[layer] = tail[16:24, :TABLE]


ANY = pl.BlockSpec(memory_space=pl.ANY)
VMEM = pl.BlockSpec(memory_space=pltpu.VMEM)
SMEM = pl.BlockSpec(memory_space=pltpu.SMEM)


def call(kernel, outs, scratch, args, micros, specs=None, out_specs=None, limit=40, aliases=None):
    return pl.pallas_call(
        kernel,
        out_shape=[jax.ShapeDtypeStruct(shape, kind) for shape, kind in outs],
        in_specs=specs or [VMEM] * len(args),
        out_specs=out_specs or [VMEM] * len(outs),
        scratch_shapes=scratch,
        input_output_aliases=aliases or {},
        compiler_params=pltpu.CompilerParams(vmem_limit_bytes=limit * 1024 * 1024),
        cost_estimate=pl.CostEstimate(flops=int(micros * 1.15e6), bytes_accessed=0, transcendentals=0),
    )(*args)


def layer_call(kernel, layer, outs, scratch, weights, args, micros, attn, behind=()):
    rooms, weight_copies, load = (
        (ATTN_ROOMS, ATTN_COPIES, attn_weights) if attn else (FFN_ROOMS, FFN_COPIES, ffn_weights)
    )

    def run(*refs):
        refs = list(refs)

        def take(number):
            taken = refs[:number]
            del refs[:number]
            return taken

        weight_refs, arg_refs, _, out_refs = take(len(weights)), take(len(args)), take(len(behind)), take(len(outs))
        weight_rooms, arg_rooms, others, (sems,) = take(len(rooms)), take(len(args)), take(len(scratch)), take(1)
        fetched = [
            whole_fetch(ref, room, sems, weight_copies + at) for at, (ref, room) in enumerate(zip(arg_refs, arg_rooms))
        ]
        loaded = load(layer, weight_refs, weight_rooms, sems, 0)
        if kernel in FORWARD:
            pending = fetched[:2] + loaded[0] + fetched[2:] + loaded[1]
        else:
            pending = fetched[:1] + loaded[1] + fetched[1:] + loaded[0]
        for item in pending:
            item.start()
        kernel(layer, loaded, *fetched, *out_refs, *others)
        for item in pending:
            item.ready()

    spaces = (
        [pltpu.VMEM(shape, kind) for shape, kind in rooms]
        + [pltpu.VMEM(a.shape, a.dtype) for a in args]
        + scratch
        + [pltpu.SemaphoreType.DMA((weight_copies + len(args),))]
    )
    operands = [*weights, *args, *behind]
    return call(run, outs, spaces, operands, micros, [ANY] * len(operands))


def turn_call(layer, forward, blocks, wholes, named, outs):
    half = D // 2
    weights = [*wholes[2:], *blocks, *wholes[:2], *blocks]
    names, args = list(named), list(named.values())
    inner = {"normed_two": ((ROWS, D), BF), "slope": ((ROWS, FF), BF), "hidden": ((ROWS, FF), BF)}
    inner = inner if forward else {}
    spaces = [
        ((ROWS, D), F32), ((200, half), F32), ((ROWS, D), F32), ((2, ROWS, 3 * half), BF), *inner.values(),
    ]

    def run(*refs):
        refs = list(refs)

        def take(number):
            taken = refs[:number]
            del refs[:number]
            return taken

        weight_refs, arg_refs, out_refs = take(14), take(len(args)), take(len(outs))
        ffn_rooms, attn_rooms, arg_rooms = take(4), take(4), take(len(args))
        scratch, flat, grad_mid, grad_qkv = take(4)
        made = dict(zip(inner, take(len(inner))))
        (sems,) = take(1)
        ups, downs = ffn_weights(layer, weight_refs[:7], ffn_rooms, sems, 0)
        qkvs, mixes = attn_weights(layer, weight_refs[7:], attn_rooms, sems, FFN_COPIES)
        got = {
            name: whole_fetch(ref, room, sems, FFN_COPIES + ATTN_COPIES + at)
            for at, (name, ref, room) in enumerate(zip(names, arg_refs, arg_rooms))
        }
        early = ("middle", "small") if forward else ("grad", "slope", "hidden")
        late = [got[name] for name in names if name not in early]
        early = [got[name] for name in early]
        if forward:
            pending = [*early, *ups, *downs, *late, *mixes, *qkvs]
        else:
            pending = [early[0], downs[0], *early[1:], got["normed_two"], ups[0], downs[1], ups[1]]
            pending += [item for item in late if item is not got["normed_two"]] + [*mixes, *qkvs]
        for item in pending:
            item.start()
        got.update(made)
        outputs = list(out_refs)
        if forward:
            ffn_fwd_kernel(
                layer, (ups, downs), got["middle"], got["small"], outputs.pop(0), got["normed_two"], got["slope"],
                got["hidden"], scratch, flat,
            )
        ffn_bwd_kernel(
            layer, (ups, downs), got["grad"], got["slope"], got["hidden"], got["normed_two"], got["small"],
            got["middle"], grad_mid, *outputs[:4],
        )
        attn_bwd_kernel(
            layer, (qkvs, mixes), grad_mid, got["att"], got["qkv"], got["probs"], got["picks"], got["picks_t"],
            got["normed_one"], got["small"], got["x"], *outputs[4:], grad_qkv, scratch, flat,
        )
        for item in pending:
            item.ready()

    scratch = (
        [pltpu.VMEM(shape, kind) for shape, kind in FFN_ROOMS + ATTN_ROOMS]
        + [pltpu.VMEM(a.shape, a.dtype) for a in args]
        + [pltpu.VMEM(shape, kind) for shape, kind in spaces]
        + [pltpu.SemaphoreType.DMA((FFN_COPIES + ATTN_COPIES + len(args),))]
    )
    operands = [*weights, *args]
    return call(run, outs, scratch, operands, 12, [ANY] * len(operands))


FORWARD = (attn_fwd_kernel, ffn_fwd_kernel)


def part_of(kernel, layer):
    def run(*refs):
        return kernel(layer, *refs)

    return run


def ring_perms():
    order = [0, 2, 4, 6, 7, 5, 3, 1]
    onward = [(order[i], order[(i + 1) % RING]) for i in range(RING)]
    return onward, [(b, a) for a, b in onward]


def ring_sum(pieces, place, one, two):
    onward, back = ring_perms()
    for step in range(RING - 1):
        one, two = lax.ppermute(one, "dp", onward), lax.ppermute(two, "dp", back)
        one = one + pick(pieces, (place - 2 - step) % RING)
        two = two + pick(pieces, RING + (place + 2 + step) % RING)
    return ring_gather(one, two)


def pick(values, index):
    return lax.dynamic_index_in_dim(values, index, 0, keepdims=False)


def ring_gather(one, two):
    onward, back = ring_perms()
    pieces = [one, two]
    for _ in range(RING - 1):
        one, two = lax.ppermute(one, "dp", onward), lax.ppermute(two, "dp", back)
        pieces += [one, two]
    return pieces


def piece_starts(place):
    starts = []
    for step in range(RING):
        starts += [((place - step) % RING) * PIECE, (RING + (place + step) % RING) * PIECE]
    return jnp.stack(starts).astype(jnp.int32)


def on_device(
    ring, tokens, cotangent, qkv_weight, qv_bias, out_weight, out_bias, up_weight, up_bias,
    down_weight, down_bias, norm_gain, norm_shift, bias_table, index_map, region_ids,
):
    half, quarter = D // 2, D // 4
    device = lax.axis_index("dp")
    parity = device % 2
    neighbours = [(i, i ^ 1) for i in range(lax.axis_size("dp"))]

    wholes = [qkv_weight.transpose(0, 2, 1, 3), out_weight, up_weight, down_weight]
    parity_ref = parity.astype(jnp.int32).reshape(1)
    sources = [*wholes, tokens, cotangent, norm_gain, norm_shift, out_bias, down_bias]
    pack_outs = [((MISC_ROWS, half), BF), ((3 * D, half), BF), ((3 * D, half), BF)]
    packs = [None, None]
    packs[0], packs[1], whole = call(
        pack_kernel,
        [((MISC_ROWS + 3 * D, half), BF), ((3 * D, half), BF), ((LAYERS * TAIL_AT, half), BF)],
        [pltpu.VMEM(value.shape[1:], value.dtype) for value in wholes] * LAYERS
        + [pltpu.VMEM(shape, kind) for shape, kind in pack_outs]
        + [pltpu.SemaphoreType.DMA((8,)), pltpu.SemaphoreType.DMA((21,))],
        [parity_ref, *sources],
        3,
        [SMEM] + [ANY] * 4 + [VMEM] * 6,
        [ANY] * 3,
        limit=60,
    )
    (misc_row,) = call(
        misc_kernel,
        [((32, half), BF)],
        [],
        [qv_bias, up_bias, bias_table.transpose(0, 2, 1), packs[1]],
        1,
        [VMEM] * 3 + [ANY],
    )
    row_far = swap(misc_row, "row")
    whole_row = swap(whole, "row")
    from_col = [swap(pack, "col") for pack in packs]
    misc, misc_far = packs[0][:MISC_ROWS], from_col[0][:MISC_ROWS]
    from_col[0] = from_col[0][MISC_ROWS:]

    def block(pack, token):
        from_dp = lax.ppermute(pack, "dp", neighbours)
        from_dp = after(from_dp, token)
        return [pack, from_dp, whole_row, swap(pack, "row"), swap(from_dp, "row")]

    picks = np.stack([position_one_hot(layer) for layer in range(LAYERS)])
    picks_t = [jnp.asarray(pick.T, BF) for pick in picks]
    picks_all = jnp.asarray(picks, BF)
    picks = [jnp.asarray(pick, BF) for pick in picks]
    masks = [mask_of(layer, region_ids) for layer in range(LAYERS)]
    wide = ((ROWS, D), F32)
    x, grad, *rest = call(
        prep_kernel,
        [wide, wide, ((16, D), F32), ((16, D), F32), ((HEADS, PAD, PAD), F32), ((HEADS, PAD, PAD), F32)],
        [
            pltpu.VMEM((64, LAYERS * HEADS, PAD), F32), pltpu.VMEM((56, PAD), jnp.int32),
            pltpu.VMEM((208, D), F32),
        ],
        [parity_ref, misc, misc_far, misc_row, row_far, index_map, picks_all],
        4,
        [SMEM] + [VMEM] * 6,
    )
    smalls, bias = rest[:2], rest[2:4]
    blocks = [block(from_col[0], x)]

    image = ((IMAGE, half), BF)
    saved = []
    for layer in range(LAYERS):
        middle, normed_one, qkv, probs, att = layer_call(
            attn_fwd_kernel,
            layer,
            [
                wide, ((ROWS, D), BF), ((2, ROWS, 3 * half), BF),
                ((2, GROUPS, STACK, PAD), BF), ((ROWS, D), BF),
            ],
            [],
            [*wholes[:2], *blocks[layer]],
            [x, smalls[layer], bias[layer], masks[layer]],
            4,
            True,
            [from_col[1]] if layer == 0 else [],
        )
        if layer == LAYERS - 1:
            saved.append((x, middle, normed_one, qkv, probs, att, None, None, None))
            break
        result, normed_two, pre, hidden = layer_call(
            ffn_fwd_kernel,
            layer,
            [wide, ((ROWS, D), BF), ((ROWS, FF), BF), ((ROWS, FF), BF)],
            [pltpu.VMEM((ROWS, D), F32), pltpu.VMEM((200, half), F32)],
            [*wholes[2:], *blocks[layer]],
            [middle, smalls[layer]],
            4,
            False,
        )
        if layer == 0:
            blocks.append(block(from_col[1], result))
        saved.append((x, middle, normed_one, qkv, probs, att, normed_two, pre, hidden))
        x = result

    heads = HEADS // 2
    one_hot = (index_map[:, :, None] == jnp.arange(256, dtype=jnp.int32)).astype(F32).reshape(SPAN * SPAN, 256)
    sums = [None] * LAYERS
    place = jnp.where(parity == 0, device // 2, RING - 1 - device // 2)
    place_ref = place.astype(jnp.int32).reshape(1)
    for layer in reversed(range(LAYERS)):
        x_in, middle, normed_one, qkv, probs, att, normed_two, pre, hidden = saved[layer]
        small_shape = ((8, half), F32)
        named = {
            "middle": middle, "small": smalls[layer], "grad": grad, "slope": pre, "hidden": hidden,
            "normed_two": normed_two, "att": att, "qkv": qkv, "probs": probs, "picks": picks[layer],
            "picks_t": picks_t[layer], "normed_one": normed_one, "x": x_in,
        }
        named = {name: value for name, value in named.items() if value is not None}
        last = layer == LAYERS - 1
        results = turn_call(
            layer,
            last,
            blocks[layer],
            wholes,
            named,
            [image] * last
            + [
                ((FF, half), BF), ((FF, half), BF), small_shape, small_shape,
                wide if layer > 0 else image, ((2 * D, half), BF), ((2 * D, half), BF), small_shape, small_shape,
                ((HEADS, 56, PAD), F32),
            ],
        )
        if last:
            output, *results = results
        ffn_keep, ffn_send, small_keep, small_send, grad, keep, send, att_keep, att_send, counts = results
        ffn_got = swap(ffn_send, "row")
        got = swap(send, "row")
        table = jnp.dot(counts[:, :SPAN, :SPAN].reshape(HEADS, SPAN * SPAN), one_hot, precision=HIGH)
        tail_keep = jnp.concatenate([small_keep, att_keep, table[:heads]], 0)
        tail_send = jnp.concatenate([small_send, att_send, table[heads:]], 0)
        pieces, one, two = call(
            combine_kernel,
            [((2 * RING, PIECE, half), BF), ((PIECE, half), BF), ((PIECE, half), BF)],
            [pltpu.VMEM((BLOCK_ROWS, half), F32)],
            [place_ref, ffn_keep, ffn_got, keep, got, tail_keep, swap(tail_send, "row")],
            2,
            [SMEM] + [VMEM] * 6,
            limit=24,
        )
        if ring:
            sums[layer] = ring_sum(pieces, place, one, two)
        else:
            sums[layer] = [lax.psum(pieces.reshape(BLOCK_ROWS, half), "dp")]
    input_grad = grad

    count = len(sums[0])
    starts = piece_starts(place) if ring else jnp.zeros((1,), jnp.int32)
    qkv, qv, outw, outb, up, upb, down, downb, gain, shift, table = call(
        part_of(unpack_kernel, count),
        [
            ((LAYERS, 3, half, half), F32), ((LAYERS, 2, half), F32), ((LAYERS, half, half), F32),
            ((LAYERS, half), F32), ((LAYERS, half, FF // 2), F32), ((LAYERS, FF // 2), F32),
            ((LAYERS, FF // 2, half), F32), ((LAYERS, half), F32), ((LAYERS, 2, half), F32),
            ((LAYERS, 2, half), F32), ((LAYERS, heads, TABLE), F32),
        ],
        [pltpu.VMEM((BLOCK_ROWS, half), F32)],
        [starts, *sums[0], *sums[1]],
        4,
        [SMEM] + [VMEM] * (2 * count),
    )
    return (
        output, input_grad, qkv.transpose(0, 2, 1, 3), qv, outw, outb, up, upb, down, downb, gain, shift,
        table.transpose(0, 2, 1),
    )


def solution(mesh):
    in_specs = (
        P(("dp", "row"), "col"),
        P(("dp", "row"), "col"),
        P(None, "col", None, "row"),
        P(None, None, "row"),
        P(None, "row", "col"),
        P(None, "col"),
        P(None, "col", "row"),
        P(None, "row"),
        P(None, "row", "col"),
        P(None, "col"),
        P(None, None, "col"),
        P(None, None, "col"),
        P(None, None, "row"),
        P(),
        P(),
    )
    out_specs = (
        P(("dp", "row"), "col"),
        P(("dp", "row"), "col"),
        P(None, "col", None, "row"),
        P(None, None, "row"),
        P(None, "row", "col"),
        P(None, "col"),
        P(None, "col", "row"),
        P(None, "row"),
        P(None, "row", "col"),
        P(None, "col"),
        P(None, None, "col"),
        P(None, None, "col"),
        P(None, None, "row"),
    )
    ring = mesh.shape["dp"] == RING
    return jax.shard_map(
        part_of(on_device, ring), mesh=mesh, in_specs=in_specs, out_specs=out_specs, check_vma=False
    )
```
